32 devices in a mesh: dp: 8 (over z, y), tensor: 4 (over x, core).
Axes of the slice: x: 2, y: 2, z: 4, core: 2. Of those that a mesh axis runs over, the one named last changes fastest.
Arguments:
- hidden_in: bfloat16 [2, 2048, 1536], P(None, ('dp', 'tensor')), may hold values from -6 to 6
- out_grad: bfloat16 [2, 2048, 1536], P(None, ('dp', 'tensor')), may hold values from -6 to 6
- segment_ids: int32 [2, 2048], P(None, 'dp'), may hold values from 0 to 255, as said below
- norm_gains: bfloat16 [4, 1536], P(None, 'dp'), may hold values from 0.5 to 1.5
- w_mixer_in: bfloat16 [1536, 2, 3072], P('dp', None, 'tensor'), may hold values from -0.15625 to 0.15625
- w_xproj: bfloat16 [3072, 128], P(('tensor', 'dp')), may hold values from -0.109375 to 0.109375
- w_dtproj: bfloat16 [96, 3072], P(None, ('tensor', 'dp')), may hold values from -0.625 to 0.625
- mixer_params: bfloat16 [23, 3072], P(None, ('tensor', 'dp')), may hold values from -7 to 3
- w_mixer_out: bfloat16 [3072, 1536], P(('tensor', 'dp')), may hold values from -0.109375 to 0.109375
- w_ffn_a_in: bfloat16 [1536, 2, 4096], P('dp', None, 'tensor'), may hold values from -0.15625 to 0.15625
- w_ffn_a_out: bfloat16 [4096, 1536], P(('tensor', 'dp')), may hold values from -0.09375 to 0.09375
- w_qkv: bfloat16 [1536, 3, 1536], P('dp', None, 'tensor'), may hold values from -0.15625 to 0.15625
- w_attn_out: bfloat16 [1536, 1536], P(('tensor', 'dp')), may hold values from -0.625 to 0.625
- w_ffn_b_in: bfloat16 [1536, 2, 4096], P('dp', None, 'tensor'), may hold values from -0.15625 to 0.15625
- w_ffn_b_out: bfloat16 [4096, 1536], P(('tensor', 'dp')), may hold values from -0.09375 to 0.09375
Outputs:
- block_out: bfloat16 [2, 2048, 1536], P(None, ('dp', 'tensor'))
- input_grad: bfloat16 [2, 2048, 1536], P(None, ('dp', 'tensor'))
- grad_norm_gains: float32 [4, 1536], P(None, 'dp')
- grad_w_mixer_in: float32 [1536, 2, 3072], P('dp', None, 'tensor')
- grad_w_xproj: float32 [3072, 128], P(('tensor', 'dp'))
- grad_w_dtproj: float32 [96, 3072], P(None, ('tensor', 'dp'))
- grad_mixer_params: float32 [23, 3072], P(None, ('tensor', 'dp'))
- grad_w_mixer_out: float32 [3072, 1536], P(('tensor', 'dp'))
- grad_w_ffn_a_in: float32 [1536, 2, 4096], P('dp', None, 'tensor')
- grad_w_ffn_a_out: float32 [4096, 1536], P(('tensor', 'dp'))
- grad_w_qkv: float32 [1536, 3, 1536], P('dp', None, 'tensor')
- grad_w_attn_out: float32 [1536, 1536], P(('tensor', 'dp'))
- grad_w_ffn_b_in: float32 [1536, 2, 4096], P('dp', None, 'tensor')
- grad_w_ffn_b_out: float32 [4096, 1536], P(('tensor', 'dp'))
The draws below stay inside these ranges and needn't reach their ends.
Inputs may be any that keep to these rules, and one draw needn't show every extreme that they name: `segment_ids`: within each packed sequence of 256 rows a token's number is the position where its document starts, so the numbers start at 0, never fall, and a document starts where the number changes; the last position is always a document of its own; in every sequence one document starts before position 64 and runs past position 192.
All inputs are finite; a program needn't handle non-finite values.
Results may differ from the reference program's by a relative error of at most 0.04.
Values may be sent and summed in bfloat16 or wider, within the bound.
No kernel may reach another device: no remote copies, remote signals or barrier semaphores. Data moves between devices by JAX's collectives and lax.ppermute only.
A program may use at most 384 MiB of HBM per device.

```python
import math
import jax
import jax.numpy as jnp
from jax import lax

D = 1536
INNER = 3072
STATE = 16
CONV = 4
RANK = 96
FF = 4096
HEADS = 12
HEAD = 128
MICRO = 2
TOK_MB = 64
SEQ = 256
GROUPS = 8
TOKENS_MB = 2048


def draw_mixer_params(key, part):
    pieces = jax.random.split(key, 5)
    conv_taps = jnp.clip(jax.random.normal(pieces[0], (CONV, INNER), jnp.float32), -4.0, 4.0) * 0.5
    conv_shift = jax.random.uniform(pieces[1], (1, INNER), jnp.float32, -0.5, 0.5)
    step_base = jnp.exp(jax.random.uniform(pieces[2], (1, INNER), jnp.float32, math.log(0.005), math.log(0.2)))
    skip_gain = jax.random.uniform(pieces[3], (1, INNER), jnp.float32, 0.5, 1.5)
    step_shift = jnp.log(jnp.expm1(step_base))
    log_rates = jax.random.uniform(pieces[4], (STATE, INNER), jnp.float32, 0.0, math.log(16.0))
    return jnp.concatenate([conv_taps, conv_shift, step_shift, skip_gain, log_rates], axis=0).astype(jnp.bfloat16)


def draw_segment_ids(key, part):
    key = jax.random.fold_in(key, 11)
    pieces = jax.random.split(key, 3)
    seq_count = MICRO * GROUPS
    opening = jax.random.randint(pieces[0], (seq_count, 1), 0, TOK_MB)
    closing = jax.random.randint(pieces[1], (seq_count, 1), 3 * TOK_MB + 1, SEQ + 1)
    position = jnp.arange(SEQ, dtype=jnp.int32)[None, :]
    random_cut = jax.random.randint(pieces[2], (seq_count, SEQ), 0, 8) == 0
    inside = (position > opening) & (position < closing)
    cut_flags = random_cut & jnp.logical_not(inside) | (position == opening) | (position == closing) | (position == SEQ - 1)
    cut_flags = cut_flags | (position == 0)
    starts = jnp.where(cut_flags, jnp.broadcast_to(position, (seq_count, SEQ)), jnp.zeros((seq_count, SEQ), jnp.int32))
    numbers = lax.cummax(starts, axis=1)
    return numbers.astype(jnp.int32).reshape(MICRO, TOKENS_MB)


def levels(rng, dims, cuts, least, largest):
    level, own = 1.0, jax.random.fold_in(rng, 6)
    for dim, parts in cuts:
        steps = jnp.exp(jax.random.uniform(jax.random.fold_in(own, dim), (parts,), jnp.float32, least / len(cuts), largest / len(cuts)))
        level = level * jnp.repeat(steps, dims[dim] // parts).reshape([-1 if axis == dim else 1 for axis in range(len(dims))])
    return level


def centred(stream_key, dims, deviation, limit, cuts=(), kind=jnp.bfloat16):
    values = jax.random.normal(stream_key, dims, jnp.float32) * deviation
    if len(cuts) > 0:
        values = levels(stream_key, dims, cuts, -0.22, 0.18) * values
    return jnp.clip(values, min=-limit, max=limit).astype(kind)


def setup_inputs(seed: int = 0) -> dict:
    splits = jax.random.split(jax.random.key(seed), 16)
    return {
        "hidden_in": centred(splits[0], (MICRO, TOKENS_MB, D), 1.0, 6.0, ((1, 32),)),
        "out_grad": centred(splits[1], (MICRO, TOKENS_MB, D), 1.0, 6.0, ((1, 32),)),
        "segment_ids": draw_segment_ids(jax.random.fold_in(splits[15], 71), 0),
        "norm_gains": jnp.clip(1.0 + 0.1 * jax.random.normal(splits[3], (4, D), jnp.float32), 0.5, 1.5).astype(jnp.bfloat16),
        "w_mixer_in": centred(splits[4], (D, 2, INNER), D ** -0.5, 0.15625, ((0, 8), (2, 4))),
        "w_xproj": centred(splits[5], (INNER, RANK + 2 * STATE), INNER ** -0.5, 0.109375, ((0, 32),)),
        "w_dtproj": centred(splits[6], (RANK, INNER), RANK ** -0.5, 0.625, ((1, 32),)),
        "mixer_params": draw_mixer_params(jax.random.fold_in(splits[15], 71), 0),
        "w_mixer_out": centred(splits[8], (INNER, D), INNER ** -0.5, 0.109375, ((0, 32),)),
        "w_ffn_a_in": centred(splits[9], (D, 2, FF), D ** -0.5, 0.15625, ((0, 8), (2, 4))),
        "w_ffn_a_out": centred(splits[10], (FF, D), FF ** -0.5, 0.09375, ((0, 32),)),
        "w_qkv": centred(splits[11], (D, 3, HEADS * HEAD), D ** -0.5, 0.15625, ((0, 8), (2, 4))),
        "w_attn_out": centred(splits[12], (HEADS * HEAD, D), (HEADS * HEAD // 16) ** -0.5, 0.625, ((0, 32),)),
        "w_ffn_b_in": centred(splits[13], (D, 2, FF), D ** -0.5, 0.15625, ((0, 8), (2, 4))),
        "w_ffn_b_out": centred(splits[14], (FF, D), FF ** -0.5, 0.09375, ((0, 32),)),
    }


epsilon = 1e-05
floor_score = -1e+30
highest = lax.Precision.HIGHEST

@jax.custom_vjp
def low(v):
    return lax.optimization_barrier(v.astype(jnp.bfloat16)).astype(jnp.float32)

@jax.custom_vjp
def low_back(v):
    return v

def low_keep(v):
    return (low(v), None)

def low_pass(kept, grad):
    return (grad,)

def back_keep(v):
    return (v, None)

def back_low(kept, grad):
    return (low(grad),)
low.defvjp(low_keep, low_pass)
low_back.defvjp(back_keep, back_low)

def matmul(left_side, right_side):
    return jnp.dot(left_side, right_side, precision=highest, preferred_element_type=jnp.float32)

def silu_gate(inputs):
    return inputs * jax.nn.sigmoid(inputs)

def soft_plus(inputs):
    return jnp.maximum(inputs, 0.0) + jnp.log1p(jnp.exp(-jnp.abs(inputs)))

def gate_product(gate_part, up_part):
    return silu_gate(gate_part) * up_part

def rms_piece(row_block, gain):
    return row_block * lax.rsqrt(lax.optimization_barrier(jnp.mean(row_block * row_block, axis=-1, keepdims=True)) + epsilon) * gain[None, :]

def reset_taps(seg_ids, taps_count):
    length = seg_ids.shape[0]
    padded = jnp.concatenate([jnp.full((taps_count - 1,), -1, jnp.int32), seg_ids.astype(jnp.int32)])
    mask_rows = []
    for offset in range(taps_count):
        earlier = padded[taps_count - 1 - offset:taps_count - 1 - offset + length]
        mask_rows.append((earlier == seg_ids).astype(jnp.float32))
    return jnp.stack(mask_rows)

def doc_mask(seg_ids):
    position = lax.iota(jnp.int32, seg_ids.shape[0])
    return (position[None, :] <= position[:, None]) & (seg_ids[None, :] == seg_ids[:, None])

def conv_piece(inputs, conv_weights, conv_bias, tap_masks):
    length = inputs.shape[0]
    taps_count = conv_weights.shape[0]
    padded = jnp.pad(inputs, ((taps_count - 1, 0), (0, 0)))
    running = jnp.broadcast_to(conv_bias[None, :], inputs.shape)
    for offset in range(taps_count):
        shifted = padded[taps_count - 1 - offset:taps_count - 1 - offset + length]
        running = running + conv_weights[offset][None, :] * shifted * tap_masks[offset][:, None]
    return silu_gate(running)

def mix_piece(dt_lin, values, input_coef, output_coef, gate_pre, mixer_rest, keep_mask):
    step_sizes = soft_plus(dt_lin + mixer_rest[0][None, :])
    decay_rate = -jnp.exp(mixer_rest[2:])

    def advance(carried, inputs_t):
        step_t, value_t, input_t, output_t, keep_t = inputs_t
        carried = jnp.exp(step_t[None, :] * decay_rate) * keep_t * carried + (step_t * value_t)[None, :] * input_t[:, None]
        return (carried, lax.optimization_barrier(jnp.sum(output_t[:, None] * carried, axis=0)))
    initial = jnp.zeros(decay_rate.shape, dt_lin.dtype)
    length = dt_lin.shape[0]
    _, scanned = lax.scan(jax.checkpoint(advance), initial, (step_sizes, values, input_coef, output_coef, keep_mask), unroll=min(64, length))
    return (scanned + mixer_rest[1][None, :] * values) * silu_gate(gate_pre)

def rope_piece(head_rows):
    length = head_rows.shape[0]
    half_size = head_rows.shape[2] // 2
    frequency = jnp.exp(lax.iota(jnp.float32, half_size) * (-2.0 * math.log(10000.0) / head_rows.shape[2]))
    angles = lax.iota(jnp.float32, length)[:, None] * frequency[None, :]
    cosine = jnp.cos(angles)[:, None, :]
    sine_part = jnp.sin(angles)[:, None, :]
    first_half = head_rows[..., :half_size]
    second_half = head_rows[..., half_size:]
    return jnp.concatenate([first_half * cosine - second_half * sine_part, second_half * cosine + first_half * sine_part], axis=-1)

def mixer(normed, tap_masks, mixer_in, mixer_x, mixer_dt, mixer_table, mixer_out):
    channels = mixer_in.shape[2]
    projected = low_back(matmul(normed, mixer_in.reshape(mixer_in.shape[0], 2 * channels)))
    values = low(conv_piece(projected[:, :channels], mixer_table[:CONV], mixer_table[CONV], tap_masks))
    extended = low_back(matmul(values, mixer_x))
    dt_low = low(extended[:, :RANK])
    dt_lin = low_back(matmul(dt_low, mixer_dt))
    gated_out = low(mix_piece(dt_lin, values, extended[:, RANK:RANK + STATE], extended[:, RANK + STATE:], projected[:, channels:], mixer_table[CONV + 1:], tap_masks[1]))
    return matmul(gated_out, mixer_out)

def ffn(normed, ffn_in, ffn_out):
    channels = ffn_in.shape[2]
    projected = low_back(matmul(normed, ffn_in.reshape(ffn_in.shape[0], 2 * channels)))
    hidden = low(gate_product(projected[:, :channels], projected[:, channels:]))
    return matmul(hidden, ffn_out)

def attention(normed, allowed, qkv_weight, attn_out):
    length = normed.shape[0]
    columns = qkv_weight.shape[2]
    head_count = columns // HEAD
    projected = low_back(matmul(normed, qkv_weight.reshape(normed.shape[1], 3 * columns)))
    turned = low(rope_piece(projected[:, :2 * columns].reshape(length, 2 * head_count, HEAD)))
    queries = turned[:, :head_count]
    key_heads = turned[:, head_count:]
    value_heads = low(projected[:, 2 * columns:].reshape(length, head_count, HEAD))
    scores = low_back(jnp.einsum('qhd,khd->hqk', queries, key_heads, precision=highest) * HEAD ** (-0.5))
    masked = jnp.where(allowed[None], scores, floor_score)
    row_max = lax.optimization_barrier(jnp.max(masked, axis=-1, keepdims=True))
    expo = jnp.exp(masked - row_max)
    soft_weights = low(expo / lax.optimization_barrier(jnp.sum(expo, axis=-1, keepdims=True)))
    head_mix = low(low_back(jnp.einsum('hqk,khd->qhd', soft_weights, value_heads, precision=highest))).reshape(length, columns)
    return matmul(head_mix, attn_out)

def sublayer(row_block, gain, branch):
    return row_block + low_back(branch(low(rms_piece(row_block, gain))))

def block_pair(seq_rows, seq_ids, params):
    gain_rows, mixer_in, mixer_x, mixer_dt, mixer_table, mixer_out, ffn_a_in, ffn_a_out, qkv_weight, attn_out, ffn_b_in, ffn_b_out = params
    tap_masks = reset_taps(seq_ids, CONV)
    allowed = doc_mask(seq_ids)

    def mixer_branch(normed):
        return mixer(normed, tap_masks, mixer_in, mixer_x, mixer_dt, mixer_table, mixer_out)

    def ffn_a_branch(normed):
        return ffn(normed, ffn_a_in, ffn_a_out)

    def attn_branch(normed):
        return attention(normed, allowed, qkv_weight, attn_out)

    def ffn_b_branch(normed):
        return ffn(normed, ffn_b_in, ffn_b_out)
    residual = sublayer(seq_rows, gain_rows[0], mixer_branch)
    residual = sublayer(residual, gain_rows[1], ffn_a_branch)
    residual = sublayer(residual, gain_rows[2], attn_branch)
    return sublayer(residual, gain_rows[3], ffn_b_branch)

def reference(hidden_in, out_grad, segment_ids, norm_gains, w_mixer_in, w_xproj, w_dtproj, mixer_params, w_mixer_out, w_ffn_a_in, w_ffn_a_out, w_qkv, w_attn_out, w_ffn_b_in, w_ffn_b_out):
    seq_count = MICRO * GROUPS
    inputs = hidden_in.astype(jnp.float32).reshape(seq_count, SEQ, D)
    cotangent = out_grad.astype(jnp.float32).reshape(seq_count, SEQ, D)
    seg_rows = segment_ids.reshape(seq_count, SEQ)
    params = tuple((weight.astype(jnp.float32) for weight in (norm_gains, w_mixer_in, w_xproj, w_dtproj, mixer_params, w_mixer_out, w_ffn_a_in, w_ffn_a_out, w_qkv, w_attn_out, w_ffn_b_in, w_ffn_b_out)))
    paired = jax.checkpoint(block_pair)

    def forward(seq_inputs, weights):

        def visit(carried, per_seq):
            return (carried, paired(per_seq[0], per_seq[1], weights))
        _, outputs = lax.scan(visit, jnp.zeros((), jnp.float32), (seq_inputs, seg_rows))
        return outputs
    outputs, pullback = jax.vjp(forward, inputs, params)
    grad_inputs, grad_params = pullback(cotangent)
    return (outputs.reshape(MICRO, TOKENS_MB, D).astype(jnp.bfloat16), grad_inputs.reshape(MICRO, TOKENS_MB, D).astype(jnp.bfloat16), grad_params[0], grad_params[1], grad_params[2], grad_params[3], grad_params[4], grad_params[5], grad_params[6], grad_params[7], grad_params[8], grad_params[9], grad_params[10], grad_params[11])
```

```python
import math

import jax
import jax.numpy as jnp
from jax import lax
from jax.experimental import pallas as pl
from jax.experimental.pallas import tpu as pltpu
from jax.sharding import PartitionSpec as P

STATE = 16
CONV = 4
RANK = 96
HEAD = 128
MICRO = 2
PIECES = 4
ORDER = (0, 2, 1, 3)

f32 = jnp.float32
bf16 = jnp.bfloat16
epsilon = 1e-05
floor_score = -1e30


def dot(a, b, dims=((1,), (0,)), out=f32):
    return lax.dot_general(a, b, (dims, ((), ())), preferred_element_type=out)


def dot_tn(a, b, out=f32):
    return dot(a, b, ((0,), (0,)), out)


def dot_nt(a, b, out=f32):
    return dot(a, b, ((1,), (1,)), out)


def sigmoid(v):
    return 1.0 / (1.0 + jnp.exp(-v))


def dsilu(v):
    s = jax.nn.sigmoid(v)
    return s * (1.0 + v * (1.0 - s))


def soft_plus(v):
    return jnp.maximum(v, 0.0) + jnp.log1p(jnp.exp(-jnp.abs(v)))


def conv_fwd_kernel(slot, x_ref, mask_ref, par_ref, wx_ref, val_ref, ext_ref, prev):
    @pl.when((pl.program_id(0) == 0) & (pl.program_id(1) == 0))
    def _():
        prev[...] = jnp.zeros_like(prev)

    x = x_ref[0, 0]
    rows = x.shape[0]
    xe = jnp.concatenate([prev[...], x], axis=0)
    mask = mask_ref[0, 0]
    conv = jnp.broadcast_to(par_ref[4:5, :], x.shape)
    for k in range(CONV):
        conv = conv + par_ref[k : k + 1, :] * xe[8 - k : 8 - k + rows] * mask[:, k : k + 1]
    prev[...] = x[rows - 8 :]
    val = (conv * sigmoid(conv)).astype(bf16)
    val_ref[0, 0] = val
    ext_ref[0, 0] = dot(val, wx_ref[...]).astype(bf16)


def conv_bwd_kernel(
    slot, dext_ref, dval_ref, x_ref, xp_ref, mask_ref, par_ref, wx_ref, dx_ref, sum_ref, after
):
    @pl.when((pl.program_id(0) == 0) & (pl.program_id(1) == 0))
    def _():
        after[...] = jnp.zeros_like(after)
        sum_ref[...] = jnp.zeros_like(sum_ref)

    x = x_ref[0, 0]
    rows = x.shape[0]
    xe = jnp.concatenate([xp_ref[0, 0], x], axis=0)
    mask = mask_ref[0, 0]
    conv = jnp.broadcast_to(par_ref[4:5, :], x.shape)
    for k in range(CONV):
        conv = conv + par_ref[k : k + 1, :] * xe[8 - k : 8 - k + rows] * mask[:, k : k + 1]
    sig = sigmoid(conv)
    d_conv = (dval_ref[0, 0] + dot_nt(dext_ref[0, 0], wx_ref[...])) * (
        sig * (1.0 + conv * (1.0 - sig))
    )
    d_x = jnp.zeros_like(x)
    sums = []
    for k in range(CONV):
        held = d_conv * mask[:, k : k + 1]
        sums.append(jnp.sum(held * xe[8 - k : 8 - k + rows], axis=0, keepdims=True))
        if k == 0:
            d_x = d_x + par_ref[0:1, :] * held
        else:
            he = jnp.concatenate([held, after[k - 1]], axis=0)
            d_x = d_x + par_ref[k : k + 1, :] * he[k : k + rows]
            after[k - 1] = held[:8]
    sums.append(jnp.sum(d_conv, axis=0, keepdims=True))
    for k in range(CONV + 1):
        sum_ref[k : k + 1, :] += sums[k]
    dx_ref[0, 0] = d_x.astype(bf16)


def coefficient_rows(ext):
    both = jnp.concatenate([ext, ext], axis=0)
    return both.T[RANK:]


def scan_fwd_kernel(
    slot, ext_ref, wdt_ref, val_ref, z_ref, par_ref, rate_ref, keep_ref,
    gated_ref, scan_ref, h_ref, state, se, sv, sc,
):
    @pl.when((pl.program_id(0) == 0) & (pl.program_id(1) == 0))
    def _():
        state[...] = jnp.zeros_like(state)

    ext_low = ext_ref[0, 0]
    step = soft_plus(dot(ext_low[:, :RANK], wdt_ref[...]) + par_ref[5:6, :])
    val = val_ref[0, 0].astype(f32)
    se[...] = jnp.where(keep_ref[0, 0] > 0.0, step, 1e30)
    sv[...] = step * val
    rate = rate_ref[...]
    coef = coefficient_rows(ext_low.astype(f32))
    shape = rate.shape

    def body(g, h):
        base = pl.multiple_of(8 * g, 8)
        turned = pltpu.roll(coef, (128 - base) % 128, 1)
        se_t = se[pl.ds(base, 8), :]
        sv_t = sv[pl.ds(base, 8), :]
        for j in range(8):
            a = jnp.exp(jnp.broadcast_to(se_t[j : j + 1], shape) * rate)
            h = a * h + jnp.broadcast_to(sv_t[j : j + 1], shape) * turned[:STATE, j : j + 1]
            h_ref[0, base + j] = h.astype(bf16)
            sc[pl.ds(base + j, 1), :] = jnp.sum(
                h * turned[STATE:, j : j + 1], axis=0, keepdims=True
            )
        return h

    state[...] = lax.fori_loop(0, se.shape[0] // 8, body, state[...])
    scanned = sc[...]
    z = z_ref[0, 0]
    scan_ref[0, 0] = scanned
    gated_ref[0, 0] = ((scanned + par_ref[6:7, :] * val) * (z * sigmoid(z))).astype(bf16)


def scan_bwd_kernel(
    slot, ext_ref, wdt_ref, val_ref, z_ref, par_ref, rate_ref, keep_ref, dg_ref, scan_ref,
    h_ref, hp_ref, ddt_ref, dval_ref, dz_ref, dbc_ref, drate_ref, sum_ref,
    carry, se, st, sv, ds, r1, r2, pb, pc,
):
    @pl.when((pl.program_id(0) == 0) & (pl.program_id(1) == 0))
    def _():
        carry[...] = jnp.zeros_like(carry)
        drate_ref[...] = jnp.zeros_like(drate_ref)
        sum_ref[...] = jnp.zeros_like(sum_ref)

    ext_low = ext_ref[0, 0]
    pre = dot(ext_low[:, :RANK], wdt_ref[...]) + par_ref[5:6, :]
    step = soft_plus(pre)
    val = val_ref[0, 0].astype(f32)
    z = z_ref[0, 0]
    sig_z = sigmoid(z)
    d_gated = dg_ref[0, 0].astype(f32)
    skip = par_ref[6:7, :]
    d_scan = d_gated * (z * sig_z)
    dz_ref[0, 0] = (
        d_gated * (scan_ref[0, 0] + skip * val) * (sig_z * (1.0 + z * (1.0 - sig_z)))
    ).astype(bf16)
    se[...] = jnp.where(keep_ref[0, 0] > 0.0, step, 1e30)
    st[...] = step
    sv[...] = step * val
    ds[...] = d_scan
    rate = rate_ref[...]
    shape = rate.shape
    coef = coefficient_rows(ext_low.astype(f32))
    count = se.shape[0] // 8
    lanes = shape[1] // 128

    def fold(v):
        total = v[:, :128]
        for i in range(1, lanes):
            total = total + v[:, 128 * i : 128 * (i + 1)]
        return total

    def body(i, held):
        back, d_rate = held
        base = pl.multiple_of(8 * (count - 1 - i), 8)
        turned = pltpu.roll(coef, (128 - base) % 128, 1)
        se_t = se[pl.ds(base, 8), :]
        st_t = st[pl.ds(base, 8), :]
        sv_t = sv[pl.ds(base, 8), :]
        ds_t = ds[pl.ds(base, 8), :]
        for j in range(7, -1, -1):
            row = base + j
            h_now = h_ref[0, row].astype(f32)
            if j > 0:
                h_before = h_ref[0, row - 1].astype(f32)
            else:
                h_before = jnp.where(
                    base == 0,
                    hp_ref[0, 0].astype(f32),
                    h_ref[0, jnp.maximum(row - 1, 0)].astype(f32),
                )
            a = jnp.exp(jnp.broadcast_to(se_t[j : j + 1], shape) * rate)
            d_row = jnp.broadcast_to(ds_t[j : j + 1], shape)
            lam = d_row * turned[STATE:, j : j + 1] + back
            back = a * lam
            w = back * h_before
            d_rate = d_rate + w * jnp.broadcast_to(st_t[j : j + 1], shape)
            r1[pl.ds(row, 1), :] = jnp.sum(w * rate, axis=0, keepdims=True)
            r2[pl.ds(row, 1), :] = jnp.sum(lam * turned[:STATE, j : j + 1], axis=0, keepdims=True)
            at = pl.ds(pl.multiple_of(row * STATE, STATE), STATE)
            pb[at, :] = fold(lam * jnp.broadcast_to(sv_t[j : j + 1], shape)).astype(bf16)
            pc[at, :] = fold(d_row * h_now).astype(bf16)
        return back, d_rate

    back, d_rate = lax.fori_loop(0, count, body, (carry[...], jnp.zeros(shape, f32)))
    carry[...] = back
    drate_ref[...] += d_rate
    ones = jnp.ones((8, 128), bf16)
    dbc_ref[0, 0, 0] = dot_nt(ones, pb[...])
    dbc_ref[0, 0, 1] = dot_nt(ones, pc[...])
    d_step = r1[...] + val * r2[...]
    d_dt = d_step * sigmoid(pre)
    dval_ref[0, 0] = step * r2[...] + skip * d_scan
    ddt_ref[0, 0] = d_dt.astype(bf16)
    sum_ref[0:1, :] += jnp.sum(d_dt, axis=0, keepdims=True)
    sum_ref[1:2, :] += jnp.sum(d_scan * val, axis=0, keepdims=True)


def turn(v, cos, sin):
    return v * cos + pltpu.roll(v, HEAD // 2, 1) * sin


def attention_parts(seg_c, seg_r, pos_c, pos_r):
    return (seg_c == seg_r) & (pos_r <= pos_c)


def attn_fwd_kernel(qkv_ref, cos_ref, sin_ref, segc, segr, posc, posr, mix_ref, low_ref):
    heads = qkv_ref.shape[3] // (3 * HEAD)
    length = PIECES * qkv_ref.shape[2]
    cos = cos_ref[...].reshape(length, HEAD)
    sin = sin_ref[...].reshape(length, HEAD)
    allowed = attention_parts(segc[...].reshape(length, 1), segr[0], posc[...], posr[...])

    def take(i):
        return qkv_ref[:, 0, :, i * HEAD : (i + 1) * HEAD].reshape(length, HEAD)

    def put(ref, i, v):
        ref[:, 0, :, i * HEAD : (i + 1) * HEAD] = v.reshape(PIECES, -1, HEAD)

    for h in range(heads):
        q = turn(take(h), cos, sin).astype(bf16)
        k = turn(take(heads + h), cos, sin).astype(bf16)
        v = take(2 * heads + h).astype(bf16)
        scores = jnp.where(allowed, dot_nt(q, k) * HEAD ** (-0.5), floor_score)
        e = jnp.exp(scores - jnp.max(scores, axis=1, keepdims=True))
        probs = (e / jnp.sum(e, axis=1, keepdims=True)).astype(bf16)
        put(mix_ref, h, dot(probs, v).astype(bf16))
        put(low_ref, h, q)
        put(low_ref, heads + h, k)
        put(low_ref, 2 * heads + h, v)


def attn_bwd_kernel(low_ref, dmix_ref, cos_ref, sin_ref, segc, segr, posc, posr, dqkv_ref):
    heads = low_ref.shape[3] // (3 * HEAD)
    length = PIECES * low_ref.shape[2]
    cos = cos_ref[...].reshape(length, HEAD)
    sin = -sin_ref[...].reshape(length, HEAD)
    allowed = attention_parts(segc[...].reshape(length, 1), segr[0], posc[...], posr[...])
    scale = HEAD ** (-0.5)

    def take(ref, i):
        return ref[:, 0, :, i * HEAD : (i + 1) * HEAD].reshape(length, HEAD)

    def put(i, v):
        dqkv_ref[:, 0, :, i * HEAD : (i + 1) * HEAD] = v.astype(bf16).reshape(PIECES, -1, HEAD)

    for h in range(heads):
        q, k, v = take(low_ref, h), take(low_ref, heads + h), take(low_ref, 2 * heads + h)
        d_mix = take(dmix_ref, h)
        scores = jnp.where(allowed, dot_nt(q, k) * scale, floor_score)
        e = jnp.exp(scores - jnp.max(scores, axis=1, keepdims=True))
        probs = e / jnp.sum(e, axis=1, keepdims=True)
        d_probs = dot_nt(d_mix, v)
        d_scores = (
            probs * (d_probs - jnp.sum(probs * d_probs, axis=1, keepdims=True))
        ).astype(bf16)
        put(h, turn(dot(d_scores, k) * scale, cos, sin))
        put(heads + h, turn(dot_tn(d_scores, q) * scale, cos, sin))
        put(2 * heads + h, dot_tn(probs.astype(bf16), d_mix))


BIG = 48 * 1024 * 1024


def params(dims):
    return pltpu.CompilerParams(
        dimension_semantics=("arbitrary",) * dims, vmem_limit_bytes=BIG
    )


def rel(rows, cols, col=0):
    return pl.BlockSpec((1, 1, rows, cols), lambda m, j, s: (s[j], m, 0, col))


def rel_back(rows, cols, col=0):
    return pl.BlockSpec((1, 1, rows, cols), lambda m, j, s: (s[PIECES - 1 - j], m, 0, col))


def ordered(rows, cols):
    return pl.BlockSpec((1, 1, rows, cols), lambda m, j, s: (m, j, 0, 0))


def ordered_back(rows, cols):
    return pl.BlockSpec((1, 1, rows, cols), lambda m, j, s: (m, PIECES - 1 - j, 0, 0))


def fixed(*shape):
    return pl.BlockSpec(shape, lambda m, j, s: (0,) * len(shape))


def conv_forward(slots, pre, masks, par, wx):
    rows, width = pre.shape[2], pre.shape[3] // 2
    grid = pltpu.PrefetchScalarGridSpec(
        num_scalar_prefetch=1,
        grid=(MICRO, PIECES),
        in_specs=[rel(rows, width), ordered(rows, CONV), fixed(8, width), fixed(*wx.shape)],
        out_specs=[rel(rows, width), rel(rows, wx.shape[1])],
        scratch_shapes=[pltpu.VMEM((8, width), f32)],
    )
    return pl.pallas_call(
        conv_fwd_kernel,
        grid_spec=grid,
        out_shape=[
            jax.ShapeDtypeStruct((PIECES, MICRO, rows, width), bf16),
            jax.ShapeDtypeStruct((PIECES, MICRO, rows, wx.shape[1]), bf16),
        ],
        compiler_params=params(2),
        name="conv_forward",
    )(slots, pre, masks, par, wx)


def conv_backward(slots, d_ext, d_val, pre, masks, par, wx):
    rows, width = pre.shape[2], pre.shape[3] // 2
    last = rows // 8 - 1
    grid = pltpu.PrefetchScalarGridSpec(
        num_scalar_prefetch=1,
        grid=(MICRO, PIECES),
        in_specs=[
            rel_back(rows, wx.shape[1]),
            rel_back(rows, width),
            rel_back(rows, width),
            pl.BlockSpec(
                (1, 1, 8, width),
                lambda m, j, s: (s[jnp.maximum(PIECES - 2 - j, 0)], m, last, 0),
            ),
            ordered_back(rows, CONV),
            fixed(8, width),
            fixed(*wx.shape),
        ],
        out_specs=[rel_back(rows, width), fixed(8, width)],
        scratch_shapes=[pltpu.VMEM((CONV - 1, 8, width), f32)],
    )
    return pl.pallas_call(
        conv_bwd_kernel,
        grid_spec=grid,
        out_shape=[
            jax.ShapeDtypeStruct((PIECES, MICRO, rows, width), bf16),
            jax.ShapeDtypeStruct((8, width), f32),
        ],
        compiler_params=params(2),
        name="conv_backward",
    )(slots, d_ext, d_val, pre, pre, masks, par, wx)


def scan_forward(slots, ext, wdt, val, pre, par, rate, keep):
    rows, width = val.shape[2], val.shape[3]
    grid = pltpu.PrefetchScalarGridSpec(
        num_scalar_prefetch=1,
        grid=(MICRO, PIECES),
        in_specs=[
            rel(rows, ext.shape[3]), fixed(*wdt.shape), rel(rows, width), rel(rows, width, 1),
            fixed(8, width), fixed(STATE, width), ordered(rows, 1),
        ],
        out_specs=[
            rel(rows, width), rel(rows, width),
            pl.BlockSpec((1, rows, STATE, width), lambda m, j, s: (m * PIECES + j, 0, 0, 0)),
        ],
        scratch_shapes=[pltpu.VMEM((STATE, width), f32)] + [pltpu.VMEM((rows, width), f32)] * 3,
    )
    return pl.pallas_call(
        scan_fwd_kernel,
        grid_spec=grid,
        out_shape=[
            jax.ShapeDtypeStruct((PIECES, MICRO, rows, width), bf16),
            jax.ShapeDtypeStruct((PIECES, MICRO, rows, width), f32),
            jax.ShapeDtypeStruct((MICRO * PIECES, rows, STATE, width), bf16),
        ],
        compiler_params=params(2),
        name="scan_forward",
    )(slots, ext, wdt, val, pre, par, rate, keep)


def scan_backward(slots, ext, wdt, val, pre, par, rate, keep, d_gated, scanned, states):
    rows, width = val.shape[2], val.shape[3]
    grid = pltpu.PrefetchScalarGridSpec(
        num_scalar_prefetch=1,
        grid=(MICRO, PIECES),
        in_specs=[
            rel_back(rows, ext.shape[3]), fixed(*wdt.shape), rel_back(rows, width),
            rel_back(rows, width, 1), fixed(8, width), fixed(STATE, width), ordered_back(rows, 1),
            rel_back(rows, width), rel_back(rows, width),
            pl.BlockSpec(
                (1, rows, STATE, width),
                lambda m, j, s: (m * PIECES + PIECES - 1 - j, 0, 0, 0),
            ),
            pl.BlockSpec(
                (1, 1, STATE, width),
                lambda m, j, s: (
                    jnp.maximum(m * PIECES + PIECES - 2 - j, 0), rows - 1, 0, 0,
                ),
            ),
        ],
        out_specs=[
            rel_back(rows, width), rel_back(rows, width), rel_back(rows, width),
            pl.BlockSpec(
                (1, 1, 2, 8, rows * STATE),
                lambda m, j, s: (s[PIECES - 1 - j], m, 0, 0, 0),
            ),
            fixed(STATE, width), fixed(8, width),
        ],
        scratch_shapes=[pltpu.VMEM((STATE, width), f32)]
        + [pltpu.VMEM((rows, width), f32)] * 6
        + [pltpu.VMEM((rows * STATE, 128), bf16)] * 2,
    )
    return pl.pallas_call(
        scan_bwd_kernel,
        grid_spec=grid,
        out_shape=[
            jax.ShapeDtypeStruct((PIECES, MICRO, rows, width), bf16),
            jax.ShapeDtypeStruct((PIECES, MICRO, rows, width), f32),
            jax.ShapeDtypeStruct((PIECES, MICRO, rows, width), bf16),
            jax.ShapeDtypeStruct((PIECES, MICRO, 2, 8, rows * STATE), f32),
            jax.ShapeDtypeStruct((STATE, width), f32),
            jax.ShapeDtypeStruct((8, width), f32),
        ],
        compiler_params=params(2),
        name="scan_backward",
    )(slots, ext, wdt, val, pre, par, rate, keep, d_gated, scanned, states, states)


def attention_specs(rows, length):
    return [
        pl.BlockSpec((PIECES, rows, HEAD), lambda m: (0, 0, 0)),
        pl.BlockSpec((PIECES, rows, HEAD), lambda m: (0, 0, 0)),
        pl.BlockSpec((PIECES, 1, rows, 1), lambda m: (0, m, 0, 0)),
        pl.BlockSpec((1, 1, length), lambda m: (m, 0, 0)),
        pl.BlockSpec((length, 1), lambda m: (0, 0)),
        pl.BlockSpec((1, length), lambda m: (0, 0)),
    ]


def attention_forward(qkv, tables):
    rows, width = qkv.shape[2], qkv.shape[3]

    def whole(cols):
        return pl.BlockSpec((PIECES, 1, rows, cols), lambda m: (0, m, 0, 0))

    return pl.pallas_call(
        attn_fwd_kernel,
        grid=(MICRO,),
        in_specs=[whole(width)] + attention_specs(rows, PIECES * rows),
        out_specs=[whole(width // 3), whole(width)],
        out_shape=[
            jax.ShapeDtypeStruct((PIECES, MICRO, rows, width // 3), bf16),
            jax.ShapeDtypeStruct((PIECES, MICRO, rows, width), bf16),
        ],
        compiler_params=params(1),
        name="attention_forward",
    )(qkv, *tables)


def attention_backward(low, d_mix, tables):
    rows, width = low.shape[2], low.shape[3]

    def whole(cols):
        return pl.BlockSpec((PIECES, 1, rows, cols), lambda m: (0, m, 0, 0))

    return pl.pallas_call(
        attn_bwd_kernel,
        grid=(MICRO,),
        in_specs=[whole(width), whole(width // 3)] + attention_specs(rows, PIECES * rows),
        out_specs=whole(width),
        out_shape=jax.ShapeDtypeStruct((PIECES, MICRO, rows, width), bf16),
        compiler_params=params(1),
        name="attention_backward",
    )(low, d_mix, *tables)


class Links:
    def __init__(self, mesh):
        self.dp = mesh.shape["dp"]
        self.nz = self.dp // 2
        self.y = lax.axis_index("dp") % 2
        self.z = lax.axis_index("dp") // 2
        self.t = lax.axis_index("tensor")
        self.groups = [[2 * z + y for z in range(self.nz)] for y in range(2)]

    def swap_y(self, v):
        return lax.ppermute(v, "dp", [(i, i ^ 1) for i in range(self.dp)])

    def shift_z(self, v, k):
        n = self.nz
        return lax.ppermute(
            v, "dp", [(2 * z + y, 2 * ((z + k) % n) + y) for z in range(n) for y in range(2)]
        )

    def swap_core(self, v):
        return lax.ppermute(v, "tensor", [(i, i ^ 1) for i in range(PIECES)])

    def swap_x(self, v):
        return lax.ppermute(v, "tensor", [(i, i ^ 2) for i in range(PIECES)])

    def gather_z(self, v):
        return lax.all_gather(v, "dp", axis=0, tiled=True, axis_index_groups=self.groups)

    def scatter_z(self, v):
        return lax.psum_scatter(
            v, "dp", scatter_dimension=0, tiled=True, axis_index_groups=self.groups
        )

    def gather_small(self, v):
        both = self.by_y(v[None], self.swap_y(v)[None])
        if self.nz > 4:
            return jnp.swapaxes(self.gather_z(both[None]), 0, 1)
        came = [both] + [self.shift_z(both, k) for k in range(1, self.nz)]
        ring = jnp.stack([came[k] for k in range(self.nz - 1, -1, -1)] + [
            came[k] for k in range(self.nz - 1, 0, -1)
        ])
        window = lax.dynamic_slice_in_dim(ring, self.nz - 1 - self.z, self.nz, 0)
        return jnp.swapaxes(window, 0, 1)

    def scatter_small(self, v):
        low = v.astype(bf16)
        own = lax.dynamic_index_in_dim(v, self.y, 0, False)
        other = self.swap_y(lax.dynamic_index_in_dim(low, 1 - self.y, 0, False))
        part = own + other.astype(f32)
        if self.nz > 4:
            return self.scatter_z(part.astype(bf16)).reshape(-1).astype(f32)
        total = lax.dynamic_index_in_dim(part, self.z, 0, False)
        part_low = part.astype(bf16)
        for k in range(1, self.nz):
            piece = lax.dynamic_index_in_dim(part_low, (self.z + k) % self.nz, 0, False)
            total = total + self.shift_z(piece, k).astype(f32)
        return total

    def by_y(self, own, other, axis=0):
        return jnp.where(
            self.y == 0,
            jnp.concatenate([own, other], axis),
            jnp.concatenate([other, own], axis),
        )

    def own_first(self, v):
        half = v.shape[1] // 2
        return jnp.where(
            self.y == 0, v, jnp.concatenate([v[:, half:], v[:, :half]], axis=1)
        )

    def gather_rows(self, v):
        x = self.swap_x(v)
        core = self.swap_core(v)
        return jnp.concatenate([v, x, core, self.swap_core(x)], axis=0)

    def scatter_rows(self, part):
        quarter = part.shape[0] // PIECES
        came = self.swap_core(part[2 * quarter :].astype(bf16)).astype(f32)
        x = self.swap_x((part[quarter : 2 * quarter] + came[quarter:]).astype(bf16))
        return part[:quarter] + came[:quarter] + x.astype(f32)

    def sum_rows(self, v):
        low = v.astype(bf16)
        q = low.shape[0] // PIECES
        turned = jnp.concatenate([low[2 * q :], low[: 2 * q]], axis=0)
        low = (low.astype(f32) + self.swap_core(turned).astype(f32)).astype(bf16)
        turned = jnp.concatenate([low[q : 2 * q], low[:q], low[3 * q :], low[2 * q : 3 * q]], axis=0)
        return (low.astype(f32) + self.swap_x(turned).astype(f32)).astype(bf16)

    def gather_weight(self, shard):
        own = self.gather_z(shard)
        return own, self.swap_y(own)

    def scatter_weight(self, own, other):
        came = self.swap_y(other)
        return self.scatter_z((own + came.astype(f32)).astype(bf16)).astype(f32)


def regroup(v, nz, axis):
    shape = v.shape
    u = shape[axis] // (2 * nz)
    v = v.reshape(shape[:axis] + (nz, 2, u) + shape[axis + 1 :])
    return jnp.swapaxes(v, axis, axis + 1).reshape(shape)


def ungroup(v, nz, axis):
    shape = v.shape
    u = shape[axis] // (2 * nz)
    v = v.reshape(shape[:axis] + (2, nz, u) + shape[axis + 1 :])
    return jnp.swapaxes(v, axis, axis + 1).reshape(shape)


def norm_forward(x, gain):
    r = lax.rsqrt(jnp.mean(x * x, axis=1, keepdims=True) + epsilon)
    return (x * r * gain).astype(bf16), r


def norm_backward(x, r, gain, d_n):
    u = x * r
    g = d_n * gain
    d_x = r * (g - u * jnp.mean(g * u, axis=1, keepdims=True))
    return d_x, jnp.sum(d_n * u, axis=0)


def times(x, own, other):
    half = x.shape[1] // 2
    return dot(x[:, :half], own) + dot(x[:, half:], other)


def back_times(d, own, other):
    return jnp.concatenate([dot_nt(d, own), dot_nt(d, other)], axis=1)


def ffn_forward(links, n, w_in, w_out):
    pair = times(n, *w_in)
    units = pair.shape[1] // 2
    gate, up = pair[:, :units], pair[:, units:]
    hid = (gate * jax.nn.sigmoid(gate) * up).astype(bf16)
    return dot(hid, w_out), (n, gate.astype(bf16), up.astype(bf16), hid)


def split_y(links, v):
    half = v.shape[1] // 2
    own = lax.dynamic_slice_in_dim(v, links.y * half, half, 1)
    other = lax.dynamic_slice_in_dim(v, (1 - links.y) * half, half, 1)
    return own, other


def ffn_backward(links, dy, kept, w_in, w_out):
    n, gate, up, hid = kept
    hid_own, hid_other = split_y(links, hid)
    grad_out = links.scatter_weight(dot_tn(hid_own, dy), dot_tn(hid_other, dy, bf16))
    d_hid = dot_nt(dy, w_out)
    gate, up = gate.astype(f32), up.astype(f32)
    sig = jax.nn.sigmoid(gate)
    d_pair = jnp.concatenate(
        [d_hid * up * (sig * (1.0 + gate * (1.0 - sig))), d_hid * (gate * sig)], axis=1
    ).astype(bf16)
    half = n.shape[1] // 2
    grad_in = links.scatter_weight(
        dot_tn(n[:, :half], d_pair), dot_tn(n[:, half:], d_pair, bf16)
    )
    return back_times(d_pair, *w_in), grad_in, grad_out


def per_device(
    mesh,
    hidden_in, out_grad, segment_ids, norm_gains, w_mixer_in, w_xproj, w_dtproj, mixer_params,
    w_mixer_out, w_ffn_a_in, w_ffn_a_out, w_qkv, w_attn_out, w_ffn_b_in, w_ffn_b_out,
):
    links = Links(mesh)
    nz, dp, t = links.nz, links.dp, links.t
    micro, rows, features = hidden_in.shape
    local = micro * rows
    length = PIECES * rows

    small = [norm_gains, w_xproj, w_dtproj, mixer_params]
    gathered = links.gather_small(jnp.concatenate([v.reshape(-1) for v in small]))
    offset = 0
    parts = []
    for v in small:
        parts.append(gathered[:, :, offset : offset + v.size].reshape((2, nz) + v.shape))
        offset += v.size
    gains = jnp.moveaxis(parts[0], 2, 0).reshape(norm_gains.shape[0], features).astype(f32)
    wx = parts[1].reshape(-1, w_xproj.shape[1])
    wdt = jnp.moveaxis(parts[2], 2, 0).reshape(w_dtproj.shape[0], -1)
    table = jnp.moveaxis(parts[3], 2, 0).reshape(mixer_params.shape[0], -1).astype(f32)
    width = table.shape[1]
    par = jnp.concatenate([table[: CONV + 3], jnp.zeros((1, width), f32)], axis=0)
    rate = -jnp.exp(table[CONV + 3 :])

    def in_weight(w, group):
        cols = w.shape[2]
        if group:
            w = regroup(w, nz, 2)
        return links.gather_weight(w.reshape(w.shape[0], w.shape[1] * cols))

    def out_weight(w):
        own, other = links.gather_weight(regroup(w, nz, 1))
        return links.by_y(own, other)

    mixer_in = in_weight(w_mixer_in, True)
    mixer_out = out_weight(w_mixer_out)
    ffn_a_in = in_weight(w_ffn_a_in, True)
    ffn_a_out = out_weight(w_ffn_a_out)
    qkv_in = in_weight(w_qkv, False)
    attn_out = ungroup(out_weight(w_attn_out), nz, 0)
    attn_out = attn_out.reshape(-1, features)
    ffn_b_in = in_weight(w_ffn_b_in, True)
    ffn_b_out = out_weight(w_ffn_b_out)

    seg = segment_ids.reshape(micro, length)
    masks = []
    for k in range(CONV):
        earlier = jnp.pad(seg, ((0, 0), (k, 0)), constant_values=-1)[:, :length]
        masks.append((earlier == seg).astype(f32))
    masks = jnp.stack(masks, axis=-1).reshape(micro, PIECES, rows, CONV)
    keep = masks[..., 1:2]
    slots = jnp.stack([sum(i * (ORDER[i] == (j ^ t)) for i in range(PIECES)) for j in range(PIECES)])
    slots = slots.astype(jnp.int32)
    seg_pieces = seg.reshape(micro, PIECES, rows)
    seg_rel = jnp.stack(
        [lax.dynamic_index_in_dim(seg_pieces, t ^ k, 1, False) for k in ORDER]
    )
    position = jnp.concatenate([(t ^ k) * rows + lax.iota(jnp.int32, rows) for k in ORDER])
    half = HEAD // 2
    frequency = jnp.exp(lax.iota(f32, half) * (-2.0 * math.log(10000.0) / HEAD))
    angles = position.astype(f32)[:, None] * frequency[None, :]
    cos, sin = jnp.cos(angles), jnp.sin(angles)
    tables = (
        jnp.concatenate([cos, cos], axis=1).reshape(PIECES, rows, HEAD),
        jnp.concatenate([-sin, sin], axis=1).reshape(PIECES, rows, HEAD),
        seg_rel[..., None],
        jnp.swapaxes(seg_rel, 0, 1).reshape(micro, 1, length),
        position[:, None],
        position[None, :],
    )

    def pieces(v):
        return v.reshape(PIECES, micro, rows, v.shape[-1])

    def flat(v):
        return v.reshape(PIECES * local, v.shape[-1])

    def enter(x, i):
        n, r = norm_forward(x, gains[i : i + 1])
        return links.gather_rows(links.own_first(n)), r

    x0 = regroup(hidden_in.reshape(local, features), nz, 1).astype(f32)
    n1, r1 = enter(x0, 0)
    pre = pieces(times(n1, *mixer_in))
    values, ext_part = conv_forward(slots, pre, masks, par, wx)
    ext = pieces(links.sum_rows(flat(ext_part)))
    gated, scanned, states = scan_forward(slots, ext, wdt, values, pre, par, rate, keep)
    x1 = x0 + links.scatter_rows(dot(flat(gated), mixer_out))

    n2, r2 = enter(x1, 1)
    y_a, kept_a = ffn_forward(links, n2, ffn_a_in, ffn_a_out)
    x2 = x1 + links.scatter_rows(y_a)

    n3, r3 = enter(x2, 2)
    mix, low = attention_forward(pieces(times(n3, *qkv_in)), tables)
    x3 = x2 + links.scatter_rows(dot(flat(mix), attn_out))

    n4, r4 = enter(x3, 3)
    y_b, kept_b = ffn_forward(links, n4, ffn_b_in, ffn_b_out)
    x4 = x3 + links.scatter_rows(y_b)
    block_out = ungroup(x4, nz, 1).astype(bf16).reshape(hidden_in.shape)

    def leave(g, x, r, i, d_normed):
        d_n = links.own_first(links.scatter_rows(d_normed))
        d_x, d_gain = norm_backward(x, r, gains[i : i + 1], d_n)
        return g + d_x, d_gain

    g4_low = regroup(out_grad.reshape(local, features), nz, 1)
    g4 = g4_low.astype(f32)
    d_n4, grad_b_in, grad_b_out = ffn_backward(
        links, links.gather_rows(g4_low), kept_b, ffn_b_in, ffn_b_out
    )
    g3, gain_d = leave(g4, x3, r4, 3, d_n4)

    dy3 = links.gather_rows(g3.astype(bf16))
    mix_rows = regroup(flat(mix), nz, 1)
    mix_own, mix_other = split_y(links, mix_rows)
    grad_attn_out = links.scatter_weight(dot_tn(mix_own, dy3), dot_tn(mix_other, dy3, bf16))
    d_mix = dot_nt(dy3, attn_out).astype(bf16)
    d_qkv = flat(attention_backward(low, pieces(d_mix), tables))
    fh = features // 2
    grad_qkv = links.scatter_weight(
        dot_tn(n3[:, :fh], d_qkv), dot_tn(n3[:, fh:], d_qkv, bf16)
    )
    g2, gain_c = leave(g3, x2, r3, 2, back_times(d_qkv, *qkv_in))

    dy2 = links.gather_rows(g2.astype(bf16))
    d_n2, grad_a_in, grad_a_out = ffn_backward(links, dy2, kept_a, ffn_a_in, ffn_a_out)
    g1, gain_b = leave(g2, x1, r2, 1, d_n2)

    dy1 = links.gather_rows(g1.astype(bf16))
    gated = flat(gated)
    gated_own, gated_other = split_y(links, gated)
    grad_mixer_out = links.scatter_weight(
        dot_tn(gated_own, dy1), dot_tn(gated_other, dy1, bf16)
    )
    d_gated = pieces(dot_nt(dy1, mixer_out))
    d_dt, d_val, d_z, d_bc, d_rate, sums = scan_backward(
        slots, ext, wdt, values, pre, par, rate, keep, d_gated, scanned, states
    )
    d_dt = flat(d_dt)
    d_bc = d_bc[:, :, :, 0, :].reshape(PIECES, micro, 2, rows, STATE)
    d_bc = jnp.swapaxes(d_bc, 2, 3).reshape(PIECES * local, 2 * STATE)
    d_ext = links.sum_rows(jnp.concatenate([dot_nt(d_dt, wdt), d_bc], axis=1))
    grad_dt = dot_tn(flat(ext)[:, :RANK], d_dt)
    grad_x = dot_tn(flat(values), d_ext)
    d_x, conv_sums = conv_backward(slots, pieces(d_ext), d_val, pre, masks, par, wx)
    d_pre = jnp.concatenate([flat(d_x), flat(d_z)], axis=1)
    grad_mixer_in = links.scatter_weight(
        dot_tn(n1[:, :fh], d_pre), dot_tn(n1[:, fh:], d_pre, bf16)
    )
    g0, gain_a = leave(g1, x0, r1, 0, back_times(d_pre, *mixer_in))
    input_grad = ungroup(g0, nz, 1).astype(bf16).reshape(hidden_in.shape)

    grad_table = jnp.concatenate([conv_sums[: CONV + 1], sums[:2], d_rate * rate], axis=0)
    grad_gains = jnp.stack([gain_a, gain_b, gain_c, gain_d])

    def by_owner(v, axis):
        u = v.shape[axis] // dp
        v = v.reshape(v.shape[:axis] + (2, nz, u) + v.shape[axis + 1 :])
        return jnp.moveaxis(v, (axis, axis + 1), (0, 1)).reshape(2, nz, -1)

    packed = jnp.concatenate(
        [by_owner(grad_gains, 1), by_owner(grad_x, 0), by_owner(grad_dt, 1), by_owner(grad_table, 1)],
        axis=2,
    )
    summed = links.scatter_small(packed)
    offset = 0
    outs = []
    for v in small:
        outs.append(summed[offset : offset + v.size].reshape(v.shape))
        offset += v.size
    gain_total = outs[0]
    gain_total = gain_total + links.swap_core(gain_total)
    gain_total = gain_total + links.swap_x(gain_total)

    def in_grad(v, like, group):
        v = v.reshape(like.shape)
        return ungroup(v, nz, 2) if group else v

    def out_grad_of(v):
        return ungroup(v, nz, 1)

    return (
        block_out,
        input_grad,
        gain_total,
        in_grad(grad_mixer_in, w_mixer_in, True),
        outs[1],
        outs[2],
        outs[3],
        out_grad_of(grad_mixer_out),
        in_grad(grad_a_in, w_ffn_a_in, True),
        out_grad_of(grad_a_out),
        in_grad(grad_qkv, w_qkv, False),
        out_grad_of(grad_attn_out),
        in_grad(grad_b_in, w_ffn_b_in, True),
        out_grad_of(grad_b_out),
    )


def solution(mesh):
    def body(*args):
        return per_device(mesh, *args)

    rows = P(None, ("dp", "tensor"), None)
    weight_in = P("dp", None, "tensor")
    weight_out = P(("tensor", "dp"), None)
    columns = P(None, ("tensor", "dp"))
    gains = P(None, "dp")
    weights = (
        gains, weight_in, weight_out, columns, columns, weight_out, weight_in, weight_out,
        weight_in, weight_out, weight_in, weight_out,
    )
    return jax.shard_map(
        body,
        mesh=mesh,
        in_specs=(rows, rows, P(None, "dp")) + weights,
        out_specs=(rows, rows) + weights,
        check_vma=False,
    )
```

```python
import math

import jax
import jax.numpy as jnp
from jax import lax
from jax.experimental import pallas as pl
from jax.experimental.pallas import tpu as pltpu
from jax.sharding import PartitionSpec as P

STATE = 16
CONV = 4
RANK = 96
HEAD = 128
MICRO = 2
PIECES = 4
ORDER = (0, 2, 1, 3)

f32 = jnp.float32
bf16 = jnp.bfloat16
epsilon = 1e-05
floor_score = -1e30


def dot(a, b, dims=((1,), (0,)), out=f32):
    return lax.dot_general(a, b, (dims, ((), ())), preferred_element_type=out)


def dot_tn(a, b, out=f32):
    return dot(a, b, ((0,), (0,)), out)


def dot_nt(a, b, out=f32):
    return dot(a, b, ((1,), (1,)), out)


def sigmoid(v):
    return 1.0 / (1.0 + jnp.exp(-v))


def dsilu(v):
    s = jax.nn.sigmoid(v)
    return s * (1.0 + v * (1.0 - s))


def soft_plus(v):
    return jnp.maximum(v, 0.0) + jnp.log1p(jnp.exp(-jnp.abs(v)))


def conv_fwd_kernel(slot, x_ref, mask_ref, par_ref, wx_ref, val_ref, ext_ref, prev):
    @pl.when((pl.program_id(0) == 0) & (pl.program_id(1) == 0))
    def _():
        prev[...] = jnp.zeros_like(prev)

    x = x_ref[0, 0]
    rows = x.shape[0]
    xe = jnp.concatenate([prev[...], x], axis=0)
    mask = mask_ref[0, 0]
    conv = jnp.broadcast_to(par_ref[4:5, :], x.shape)
    for k in range(CONV):
        conv = conv + par_ref[k : k + 1, :] * xe[8 - k : 8 - k + rows] * mask[:, k : k + 1]
    prev[...] = x[rows - 8 :]
    val = (conv * sigmoid(conv)).astype(bf16)
    val_ref[0, 0] = val
    ext_ref[0, 0] = dot(val, wx_ref[...]).astype(bf16)


def conv_bwd_kernel(
    slot, dext_ref, dval_ref, x_ref, xp_ref, mask_ref, par_ref, wx_ref, dx_ref, sum_ref, after
):
    @pl.when((pl.program_id(0) == 0) & (pl.program_id(1) == 0))
    def _():
        after[...] = jnp.zeros_like(after)
        sum_ref[...] = jnp.zeros_like(sum_ref)

    x = x_ref[0, 0]
    rows = x.shape[0]
    xe = jnp.concatenate([xp_ref[0, 0], x], axis=0)
    mask = mask_ref[0, 0]
    conv = jnp.broadcast_to(par_ref[4:5, :], x.shape)
    for k in range(CONV):
        conv = conv + par_ref[k : k + 1, :] * xe[8 - k : 8 - k + rows] * mask[:, k : k + 1]
    sig = sigmoid(conv)
    d_conv = (dval_ref[0, 0] + dot_nt(dext_ref[0, 0], wx_ref[...])) * (
        sig * (1.0 + conv * (1.0 - sig))
    )
    d_x = jnp.zeros_like(x)
    sums = []
    for k in range(CONV):
        held = d_conv * mask[:, k : k + 1]
        sums.append(jnp.sum(held * xe[8 - k : 8 - k + rows], axis=0, keepdims=True))
        if k == 0:
            d_x = d_x + par_ref[0:1, :] * held
        else:
            he = jnp.concatenate([held, after[k - 1]], axis=0)
            d_x = d_x + par_ref[k : k + 1, :] * he[k : k + rows]
            after[k - 1] = held[:8]
    sums.append(jnp.sum(d_conv, axis=0, keepdims=True))
    for k in range(CONV + 1):
        sum_ref[k : k + 1, :] += sums[k]
    dx_ref[0, 0] = d_x.astype(bf16)


def coefficient_rows(ext):
    both = jnp.concatenate([ext, ext], axis=0)
    return both.T[RANK:]


def scan_fwd_kernel(
    slot, ext_ref, wdt_ref, val_ref, z_ref, par_ref, rate_ref, keep_ref,
    gated_ref, scan_ref, h_ref, state, se, sv, sc,
):
    @pl.when((pl.program_id(0) == 0) & (pl.program_id(1) == 0))
    def _():
        state[...] = jnp.zeros_like(state)

    ext_low = ext_ref[0, 0]
    step = soft_plus(dot(ext_low[:, :RANK], wdt_ref[...]) + par_ref[5:6, :])
    val = val_ref[0, 0].astype(f32)
    se[...] = jnp.where(keep_ref[0, 0] > 0.0, step, 1e30)
    sv[...] = step * val
    rate = rate_ref[...]
    coef = coefficient_rows(ext_low.astype(f32))
    shape = rate.shape

    def body(g, h):
        base = pl.multiple_of(8 * g, 8)
        turned = pltpu.roll(coef, (128 - base) % 128, 1)
        se_t = se[pl.ds(base, 8), :]
        sv_t = sv[pl.ds(base, 8), :]
        for j in range(8):
            a = jnp.exp(jnp.broadcast_to(se_t[j : j + 1], shape) * rate)
            h = a * h + jnp.broadcast_to(sv_t[j : j + 1], shape) * turned[:STATE, j : j + 1]
            h_ref[0, base + j] = h.astype(bf16)
            sc[pl.ds(base + j, 1), :] = jnp.sum(
                h * turned[STATE:, j : j + 1], axis=0, keepdims=True
            )
        return h

    state[...] = lax.fori_loop(0, se.shape[0] // 8, body, state[...])
    scanned = sc[...]
    z = z_ref[0, 0]
    scan_ref[0, 0] = scanned
    gated_ref[0, 0] = ((scanned + par_ref[6:7, :] * val) * (z * sigmoid(z))).astype(bf16)


def scan_bwd_kernel(
    slot, ext_ref, wdt_ref, val_ref, z_ref, par_ref, rate_ref, keep_ref, dg_ref, scan_ref,
    h_ref, hp_ref, ddt_ref, dval_ref, dz_ref, dbc_ref, drate_ref, sum_ref,
    carry, se, st, sv, ds, r1, r2, pb, pc,
):
    @pl.when((pl.program_id(0) == 0) & (pl.program_id(1) == 0))
    def _():
        carry[...] = jnp.zeros_like(carry)
        drate_ref[...] = jnp.zeros_like(drate_ref)
        sum_ref[...] = jnp.zeros_like(sum_ref)

    ext_low = ext_ref[0, 0]
    pre = dot(ext_low[:, :RANK], wdt_ref[...]) + par_ref[5:6, :]
    step = soft_plus(pre)
    val = val_ref[0, 0].astype(f32)
    z = z_ref[0, 0]
    sig_z = sigmoid(z)
    d_gated = dg_ref[0, 0].astype(f32)
    skip = par_ref[6:7, :]
    d_scan = d_gated * (z * sig_z)
    dz_ref[0, 0] = (
        d_gated * (scan_ref[0, 0] + skip * val) * (sig_z * (1.0 + z * (1.0 - sig_z)))
    ).astype(bf16)
    se[...] = jnp.where(keep_ref[0, 0] > 0.0, step, 1e30)
    st[...] = step
    sv[...] = step * val
    ds[...] = d_scan
    rate = rate_ref[...]
    shape = rate.shape
    coef = coefficient_rows(ext_low.astype(f32))
    count = se.shape[0] // 8
    lanes = shape[1] // 128

    def fold(v):
        total = v[:, :128]
        for i in range(1, lanes):
            total = total + v[:, 128 * i : 128 * (i + 1)]
        return total

    def body(i, held):
        back, d_rate = held
        base = pl.multiple_of(8 * (count - 1 - i), 8)
        turned = pltpu.roll(coef, (128 - base) % 128, 1)
        se_t = se[pl.ds(base, 8), :]
        st_t = st[pl.ds(base, 8), :]
        sv_t = sv[pl.ds(base, 8), :]
        ds_t = ds[pl.ds(base, 8), :]
        for j in range(7, -1, -1):
            row = base + j
            h_now = h_ref[0, row].astype(f32)
            if j > 0:
                h_before = h_ref[0, row - 1].astype(f32)
            else:
                h_before = jnp.where(
                    base == 0,
                    hp_ref[0, 0].astype(f32),
                    h_ref[0, jnp.maximum(row - 1, 0)].astype(f32),
                )
            a = jnp.exp(jnp.broadcast_to(se_t[j : j + 1], shape) * rate)
            d_row = jnp.broadcast_to(ds_t[j : j + 1], shape)
            lam = d_row * turned[STATE:, j : j + 1] + back
            back = a * lam
            w = back * h_before
            d_rate = d_rate + w * jnp.broadcast_to(st_t[j : j + 1], shape)
            r1[pl.ds(row, 1), :] = jnp.sum(w * rate, axis=0, keepdims=True)
            r2[pl.ds(row, 1), :] = jnp.sum(lam * turned[:STATE, j : j + 1], axis=0, keepdims=True)
            at = pl.ds(pl.multiple_of(row * STATE, STATE), STATE)
            pb[at, :] = fold(lam * jnp.broadcast_to(sv_t[j : j + 1], shape)).astype(bf16)
            pc[at, :] = fold(d_row * h_now).astype(bf16)
        return back, d_rate

    back, d_rate = lax.fori_loop(0, count, body, (carry[...], jnp.zeros(shape, f32)))
    carry[...] = back
    drate_ref[...] += d_rate
    ones = jnp.ones((8, 128), bf16)
    dbc_ref[0, 0, 0] = dot_nt(ones, pb[...])
    dbc_ref[0, 0, 1] = dot_nt(ones, pc[...])
    d_step = r1[...] + val * r2[...]
    d_dt = d_step * sigmoid(pre)
    dval_ref[0, 0] = step * r2[...] + skip * d_scan
    ddt_ref[0, 0] = d_dt.astype(bf16)
    sum_ref[0:1, :] += jnp.sum(d_dt, axis=0, keepdims=True)
    sum_ref[1:2, :] += jnp.sum(d_scan * val, axis=0, keepdims=True)


def turn(v, cos, sin):
    return v * cos + pltpu.roll(v, HEAD // 2, 1) * sin


def attention_parts(seg_c, seg_r, pos_c, pos_r):
    return (seg_c == seg_r) & (pos_r <= pos_c)


def attn_fwd_kernel(qkv_ref, cos_ref, sin_ref, segc, segr, posc, posr, mix_ref, low_ref):
    heads = qkv_ref.shape[3] // (3 * HEAD)
    length = PIECES * qkv_ref.shape[2]
    cos = cos_ref[...].reshape(length, HEAD)
    sin = sin_ref[...].reshape(length, HEAD)
    allowed = attention_parts(segc[...].reshape(length, 1), segr[0], posc[...], posr[...])

    def take(i):
        return qkv_ref[:, 0, :, i * HEAD : (i + 1) * HEAD].reshape(length, HEAD)

    def put(ref, i, v):
        ref[:, 0, :, i * HEAD : (i + 1) * HEAD] = v.reshape(PIECES, -1, HEAD)

    for h in range(heads):
        q = turn(take(h), cos, sin).astype(bf16)
        k = turn(take(heads + h), cos, sin).astype(bf16)
        v = take(2 * heads + h).astype(bf16)
        scores = jnp.where(allowed, dot_nt(q, k) * HEAD ** (-0.5), floor_score)
        e = jnp.exp(scores - jnp.max(scores, axis=1, keepdims=True))
        probs = (e / jnp.sum(e, axis=1, keepdims=True)).astype(bf16)
        put(mix_ref, h, dot(probs, v).astype(bf16))
        put(low_ref, h, q)
        put(low_ref, heads + h, k)
        put(low_ref, 2 * heads + h, v)


def attn_bwd_kernel(low_ref, dmix_ref, cos_ref, sin_ref, segc, segr, posc, posr, dqkv_ref):
    heads = low_ref.shape[3] // (3 * HEAD)
    length = PIECES * low_ref.shape[2]
    cos = cos_ref[...].reshape(length, HEAD)
    sin = -sin_ref[...].reshape(length, HEAD)
    allowed = attention_parts(segc[...].reshape(length, 1), segr[0], posc[...], posr[...])
    scale = HEAD ** (-0.5)

    def take(ref, i):
        return ref[:, 0, :, i * HEAD : (i + 1) * HEAD].reshape(length, HEAD)

    def put(i, v):
        dqkv_ref[:, 0, :, i * HEAD : (i + 1) * HEAD] = v.astype(bf16).reshape(PIECES, -1, HEAD)

    for h in range(heads):
        q, k, v = take(low_ref, h), take(low_ref, heads + h), take(low_ref, 2 * heads + h)
        d_mix = take(dmix_ref, h)
        scores = jnp.where(allowed, dot_nt(q, k) * scale, floor_score)
        e = jnp.exp(scores - jnp.max(scores, axis=1, keepdims=True))
        probs = e / jnp.sum(e, axis=1, keepdims=True)
        d_probs = dot_nt(d_mix, v)
        d_scores = (
            probs * (d_probs - jnp.sum(probs * d_probs, axis=1, keepdims=True))
        ).astype(bf16)
        put(h, turn(dot(d_scores, k) * scale, cos, sin))
        put(heads + h, turn(dot_tn(d_scores, q) * scale, cos, sin))
        put(2 * heads + h, dot_tn(probs.astype(bf16), d_mix))


BIG = 48 * 1024 * 1024


def params(dims):
    return pltpu.CompilerParams(
        dimension_semantics=("arbitrary",) * dims, vmem_limit_bytes=BIG
    )


def rel(rows, cols, col=0):
    return pl.BlockSpec((1, 1, rows, cols), lambda m, j, s: (s[j], m, 0, col))


def rel_back(rows, cols, col=0):
    return pl.BlockSpec((1, 1, rows, cols), lambda m, j, s: (s[PIECES - 1 - j], m, 0, col))


def ordered(rows, cols):
    return pl.BlockSpec((1, 1, rows, cols), lambda m, j, s: (m, j, 0, 0))


def ordered_back(rows, cols):
    return pl.BlockSpec((1, 1, rows, cols), lambda m, j, s: (m, PIECES - 1 - j, 0, 0))


def fixed(*shape):
    return pl.BlockSpec(shape, lambda m, j, s: (0,) * len(shape))


def conv_forward(slots, pre, masks, par, wx):
    rows, width = pre.shape[2], pre.shape[3] // 2
    grid = pltpu.PrefetchScalarGridSpec(
        num_scalar_prefetch=1,
        grid=(MICRO, PIECES),
        in_specs=[rel(rows, width), ordered(rows, CONV), fixed(8, width), fixed(*wx.shape)],
        out_specs=[rel(rows, width), rel(rows, wx.shape[1])],
        scratch_shapes=[pltpu.VMEM((8, width), f32)],
    )
    return pl.pallas_call(
        conv_fwd_kernel,
        grid_spec=grid,
        out_shape=[
            jax.ShapeDtypeStruct((PIECES, MICRO, rows, width), bf16),
            jax.ShapeDtypeStruct((PIECES, MICRO, rows, wx.shape[1]), bf16),
        ],
        compiler_params=params(2),
        name="conv_forward",
    )(slots, pre, masks, par, wx)


def conv_backward(slots, d_ext, d_val, pre, masks, par, wx):
    rows, width = pre.shape[2], pre.shape[3] // 2
    last = rows // 8 - 1
    grid = pltpu.PrefetchScalarGridSpec(
        num_scalar_prefetch=1,
        grid=(MICRO, PIECES),
        in_specs=[
            rel_back(rows, wx.shape[1]),
            rel_back(rows, width),
            rel_back(rows, width),
            pl.BlockSpec(
                (1, 1, 8, width),
                lambda m, j, s: (s[jnp.maximum(PIECES - 2 - j, 0)], m, last, 0),
            ),
            ordered_back(rows, CONV),
            fixed(8, width),
            fixed(*wx.shape),
        ],
        out_specs=[rel_back(rows, width), fixed(8, width)],
        scratch_shapes=[pltpu.VMEM((CONV - 1, 8, width), f32)],
    )
    return pl.pallas_call(
        conv_bwd_kernel,
        grid_spec=grid,
        out_shape=[
            jax.ShapeDtypeStruct((PIECES, MICRO, rows, width), bf16),
            jax.ShapeDtypeStruct((8, width), f32),
        ],
        compiler_params=params(2),
        name="conv_backward",
    )(slots, d_ext, d_val, pre, pre, masks, par, wx)


def scan_forward(slots, ext, wdt, val, pre, par, rate, keep):
    rows, width = val.shape[2], val.shape[3]
    grid = pltpu.PrefetchScalarGridSpec(
        num_scalar_prefetch=1,
        grid=(MICRO, PIECES),
        in_specs=[
            rel(rows, ext.shape[3]), fixed(*wdt.shape), rel(rows, width), rel(rows, width, 1),
            fixed(8, width), fixed(STATE, width), ordered(rows, 1),
        ],
        out_specs=[
            rel(rows, width), rel(rows, width),
            pl.BlockSpec((1, rows, STATE, width), lambda m, j, s: (m * PIECES + j, 0, 0, 0)),
        ],
        scratch_shapes=[pltpu.VMEM((STATE, width), f32)] + [pltpu.VMEM((rows, width), f32)] * 3,
    )
    return pl.pallas_call(
        scan_fwd_kernel,
        grid_spec=grid,
        out_shape=[
            jax.ShapeDtypeStruct((PIECES, MICRO, rows, width), bf16),
            jax.ShapeDtypeStruct((PIECES, MICRO, rows, width), f32),
            jax.ShapeDtypeStruct((MICRO * PIECES, rows, STATE, width), bf16),
        ],
        compiler_params=params(2),
        name="scan_forward",
    )(slots, ext, wdt, val, pre, par, rate, keep)


def scan_backward(slots, ext, wdt, val, pre, par, rate, keep, d_gated, scanned, states):
    rows, width = val.shape[2], val.shape[3]
    grid = pltpu.PrefetchScalarGridSpec(
        num_scalar_prefetch=1,
        grid=(MICRO, PIECES),
        in_specs=[
            rel_back(rows, ext.shape[3]), fixed(*wdt.shape), rel_back(rows, width),
            rel_back(rows, width, 1), fixed(8, width), fixed(STATE, width), ordered_back(rows, 1),
            rel_back(rows, width), rel_back(rows, width),
            pl.BlockSpec(
                (1, rows, STATE, width),
                lambda m, j, s: (m * PIECES + PIECES - 1 - j, 0, 0, 0),
            ),
            pl.BlockSpec(
                (1, 1, STATE, width),
                lambda m, j, s: (
                    jnp.maximum(m * PIECES + PIECES - 2 - j, 0), rows - 1, 0, 0,
                ),
            ),
        ],
        out_specs=[
            rel_back(rows, width), rel_back(rows, width), rel_back(rows, width),
            pl.BlockSpec(
                (1, 1, 2, 8, rows * STATE),
                lambda m, j, s: (s[PIECES - 1 - j], m, 0, 0, 0),
            ),
            fixed(STATE, width), fixed(8, width),
        ],
        scratch_shapes=[pltpu.VMEM((STATE, width), f32)]
        + [pltpu.VMEM((rows, width), f32)] * 6
        + [pltpu.VMEM((rows * STATE, 128), bf16)] * 2,
    )
    return pl.pallas_call(
        scan_bwd_kernel,
        grid_spec=grid,
        out_shape=[
            jax.ShapeDtypeStruct((PIECES, MICRO, rows, width), bf16),
            jax.ShapeDtypeStruct((PIECES, MICRO, rows, width), f32),
            jax.ShapeDtypeStruct((PIECES, MICRO, rows, width), bf16),
            jax.ShapeDtypeStruct((PIECES, MICRO, 2, 8, rows * STATE), f32),
            jax.ShapeDtypeStruct((STATE, width), f32),
            jax.ShapeDtypeStruct((8, width), f32),
        ],
        compiler_params=params(2),
        name="scan_backward",
    )(slots, ext, wdt, val, pre, par, rate, keep, d_gated, scanned, states, states)


def attention_specs(rows, length):
    return [
        pl.BlockSpec((PIECES, rows, HEAD), lambda m: (0, 0, 0)),
        pl.BlockSpec((PIECES, rows, HEAD), lambda m: (0, 0, 0)),
        pl.BlockSpec((PIECES, 1, rows, 1), lambda m: (0, m, 0, 0)),
        pl.BlockSpec((1, 1, length), lambda m: (m, 0, 0)),
        pl.BlockSpec((length, 1), lambda m: (0, 0)),
        pl.BlockSpec((1, length), lambda m: (0, 0)),
    ]


def attention_forward(qkv, tables):
    rows, width = qkv.shape[2], qkv.shape[3]

    def whole(cols):
        return pl.BlockSpec((PIECES, 1, rows, cols), lambda m: (0, m, 0, 0))

    return pl.pallas_call(
        attn_fwd_kernel,
        grid=(MICRO,),
        in_specs=[whole(width)] + attention_specs(rows, PIECES * rows),
        out_specs=[whole(width // 3), whole(width)],
        out_shape=[
            jax.ShapeDtypeStruct((PIECES, MICRO, rows, width // 3), bf16),
            jax.ShapeDtypeStruct((PIECES, MICRO, rows, width), bf16),
        ],
        compiler_params=params(1),
        name="attention_forward",
    )(qkv, *tables)


def attention_backward(low, d_mix, tables):
    rows, width = low.shape[2], low.shape[3]

    def whole(cols):
        return pl.BlockSpec((PIECES, 1, rows, cols), lambda m: (0, m, 0, 0))

    return pl.pallas_call(
        attn_bwd_kernel,
        grid=(MICRO,),
        in_specs=[whole(width), whole(width // 3)] + attention_specs(rows, PIECES * rows),
        out_specs=whole(width),
        out_shape=jax.ShapeDtypeStruct((PIECES, MICRO, rows, width), bf16),
        compiler_params=params(1),
        name="attention_backward",
    )(low, d_mix, *tables)


class Links:
    def __init__(self, mesh):
        self.dp = mesh.shape["dp"]
        self.nz = self.dp // 2
        self.y = lax.axis_index("dp") % 2
        self.z = lax.axis_index("dp") // 2
        self.t = lax.axis_index("tensor")
        self.groups = [[2 * z + y for z in range(self.nz)] for y in range(2)]

    def swap_y(self, v):
        return lax.ppermute(v, "dp", [(i, i ^ 1) for i in range(self.dp)])

    def shift_z(self, v, k):
        n = self.nz
        return lax.ppermute(
            v, "dp", [(2 * z + y, 2 * ((z + k) % n) + y) for z in range(n) for y in range(2)]
        )

    def swap_core(self, v):
        return lax.ppermute(v, "tensor", [(i, i ^ 1) for i in range(PIECES)])

    def swap_x(self, v):
        return lax.ppermute(v, "tensor", [(i, i ^ 2) for i in range(PIECES)])

    def gather_z(self, v):
        return lax.all_gather(v, "dp", axis=0, tiled=True, axis_index_groups=self.groups)

    def scatter_z(self, v):
        return lax.psum_scatter(
            v, "dp", scatter_dimension=0, tiled=True, axis_index_groups=self.groups
        )

    def gather_small(self, v):
        if self.dp > 8:
            both = self.by_y(v[None], self.swap_y(v)[None])
            return jnp.swapaxes(self.gather_z(both[None]), 0, 1)
        n = self.dp
        came = [v] + [
            lax.ppermute(v, "dp", [(i, (i + k) % n) for i in range(n)]) for k in range(1, n)
        ]
        ring = jnp.stack(came[:0:-1] + came[:1] + came[:0:-1])
        window = lax.dynamic_slice_in_dim(ring, n - 1 - lax.axis_index("dp"), n, 0)
        return jnp.swapaxes(window.reshape(self.nz, 2, -1), 0, 1)

    def scatter_small(self, v):
        low = v.astype(bf16)
        own = lax.dynamic_index_in_dim(v, self.y, 0, False)
        other = self.swap_y(lax.dynamic_index_in_dim(low, 1 - self.y, 0, False))
        part = own + other.astype(f32)
        if self.nz > 4:
            return self.scatter_z(part.astype(bf16)).reshape(-1).astype(f32)
        total = lax.dynamic_index_in_dim(part, self.z, 0, False)
        part_low = part.astype(bf16)
        for k in range(1, self.nz):
            piece = lax.dynamic_index_in_dim(part_low, (self.z + k) % self.nz, 0, False)
            total = total + self.shift_z(piece, k).astype(f32)
        return total

    def by_y(self, own, other, axis=0):
        return jnp.where(
            self.y == 0,
            jnp.concatenate([own, other], axis),
            jnp.concatenate([other, own], axis),
        )

    def own_first(self, v):
        half = v.shape[1] // 2
        return jnp.where(
            self.y == 0, v, jnp.concatenate([v[:, half:], v[:, :half]], axis=1)
        )

    def gather_rows(self, v):
        x = self.swap_x(v)
        core = self.swap_core(v)
        return jnp.concatenate([v, x, core, self.swap_core(x)], axis=0)

    def scatter_rows(self, part, *order):
        quarter = part.shape[0] // PIECES
        came = self.swap_core(part[2 * quarter :].astype(bf16)).astype(f32)
        x = (part[quarter : 2 * quarter] + came[quarter:]).astype(bf16)
        x = self.swap_x(after(x, *order))
        return part[:quarter] + came[:quarter] + x.astype(f32)

    def sum_rows(self, v):
        low = v.astype(bf16)
        q = low.shape[0] // PIECES
        turned = jnp.concatenate([low[2 * q :], low[: 2 * q]], axis=0)
        low = (low.astype(f32) + self.swap_core(turned).astype(f32)).astype(bf16)
        turned = jnp.concatenate([low[q : 2 * q], low[:q], low[3 * q :], low[2 * q : 3 * q]], axis=0)
        return (low.astype(f32) + self.swap_x(turned).astype(f32)).astype(bf16)

    def gather_z_direct(self, shard):
        if self.nz > 4:
            return self.gather_z(shard)
        came = [shard] + [self.shift_z(shard, k) for k in range(1, self.nz)]
        ring = jnp.concatenate(came[:0:-1] + came[:1] + came[:0:-1], axis=0)
        rows = shard.shape[0]
        return lax.dynamic_slice_in_dim(
            ring, (self.nz - 1 - self.z) * rows, self.nz * rows, 0
        )

    def scatter_z_direct(self, v):
        if self.nz > 4:
            return self.scatter_z(v.astype(bf16)).astype(f32)
        rows = v.shape[0] // self.nz
        total = lax.dynamic_slice_in_dim(v, self.z * rows, rows, 0).astype(f32)
        for k in range(1, self.nz):
            piece = lax.dynamic_slice_in_dim(v, ((self.z + k) % self.nz) * rows, rows, 0)
            total = total + self.shift_z(piece, k).astype(f32)
        return total


class Sent:
    def __init__(self, links, left_own, left_other, right, *order):
        self.links, self.left, self.right = links, left_own, right
        self.product = dot_tn(left_other, right, bf16)
        self.came = links.swap_y(after(self.product, *order))

    def finish(self, *order, direct=False):
        came = after(self.came, *order)
        self.total = (dot_tn(self.left, self.right) + came.astype(f32)).astype(bf16)
        if direct:
            self.out = self.links.scatter_z_direct(self.total)
        else:
            self.out = self.links.scatter_z(self.total).astype(f32)
        return self.total


def after(v, *order):
    if not order:
        return v
    return lax.optimization_barrier((v,) + order)[0]


def regroup(v, nz, axis):
    shape = v.shape
    u = shape[axis] // (2 * nz)
    v = v.reshape(shape[:axis] + (nz, 2, u) + shape[axis + 1 :])
    return jnp.swapaxes(v, axis, axis + 1).reshape(shape)


def ungroup(v, nz, axis):
    shape = v.shape
    u = shape[axis] // (2 * nz)
    v = v.reshape(shape[:axis] + (2, nz, u) + shape[axis + 1 :])
    return jnp.swapaxes(v, axis, axis + 1).reshape(shape)


def norm_forward(x, gain):
    r = lax.rsqrt(jnp.mean(x * x, axis=1, keepdims=True) + epsilon)
    return (x * r * gain).astype(bf16), r


def norm_backward(x, r, gain, d_n):
    u = x * r
    g = d_n * gain
    d_x = r * (g - u * jnp.mean(g * u, axis=1, keepdims=True))
    return d_x, jnp.sum(d_n * u, axis=0)


def times(x, own, other):
    half = x.shape[1] // 2
    return dot(x[:, :half], own) + dot(x[:, half:], other)


def back_times(d, own, other):
    return jnp.concatenate([dot_nt(d, own), dot_nt(d, other)], axis=1)


def ffn_forward(links, n, w_in, w_out, *order):
    pair = times(n, *w_in)
    units = pair.shape[1] // 2
    gate, up = pair[:, :units], pair[:, units:]
    hid = (gate * jax.nn.sigmoid(gate) * up).astype(bf16)
    return dot(after(hid, *order), w_out), (n, gate.astype(bf16), up.astype(bf16), hid)


def split_y(links, v):
    half = v.shape[1] // 2
    own = lax.dynamic_slice_in_dim(v, links.y * half, half, 1)
    other = lax.dynamic_slice_in_dim(v, (1 - links.y) * half, half, 1)
    return own, other


def ffn_backward(links, dy, kept, w_in, w_out, *order):
    n, gate, up, hid = kept
    hid_own, hid_other = split_y(links, hid)
    sent_out = Sent(links, hid_own, hid_other, dy, *order)
    d_hid = dot_nt(after(dy, sent_out.product), w_out)
    gate, up = gate.astype(f32), up.astype(f32)
    sig = jax.nn.sigmoid(gate)
    d_pair = jnp.concatenate(
        [d_hid * up * (sig * (1.0 + gate * (1.0 - sig))), d_hid * (gate * sig)], axis=1
    ).astype(bf16)
    half = n.shape[1] // 2
    sent_in = Sent(links, n[:, :half], n[:, half:], d_pair, sent_out.came)
    d_normed = back_times(after(d_pair, sent_in.product), *w_in)
    return d_normed, sent_in, sent_out


def per_device(
    mesh,
    hidden_in, out_grad, segment_ids, norm_gains, w_mixer_in, w_xproj, w_dtproj, mixer_params,
    w_mixer_out, w_ffn_a_in, w_ffn_a_out, w_qkv, w_attn_out, w_ffn_b_in, w_ffn_b_out,
):
    links = Links(mesh)
    nz, dp, t = links.nz, links.dp, links.t
    micro, rows, features = hidden_in.shape
    local = micro * rows
    length = PIECES * rows

    small = [norm_gains, w_xproj, w_dtproj, mixer_params]
    gathered = links.gather_small(jnp.concatenate([v.reshape(-1) for v in small]))
    offset = 0
    parts = []
    for v in small:
        parts.append(gathered[:, :, offset : offset + v.size].reshape((2, nz) + v.shape))
        offset += v.size
    gains = jnp.moveaxis(parts[0], 2, 0).reshape(norm_gains.shape[0], features).astype(f32)
    wx = parts[1].reshape(-1, w_xproj.shape[1])
    wdt = jnp.moveaxis(parts[2], 2, 0).reshape(w_dtproj.shape[0], -1)
    table = jnp.moveaxis(parts[3], 2, 0).reshape(mixer_params.shape[0], -1).astype(f32)
    width = table.shape[1]
    par = jnp.concatenate([table[: CONV + 3], jnp.zeros((1, width), f32)], axis=0)
    rate = -jnp.exp(table[CONV + 3 :])

    def in_shard(w, group):
        if group:
            w = regroup(w, nz, 2)
        return w.reshape(w.shape[0], -1)

    shards = [
        in_shard(w_mixer_in, True),
        jnp.concatenate([regroup(w_mixer_out, nz, 1), regroup(w_attn_out, nz, 1)], axis=0),
        in_shard(w_ffn_a_in, True),
        regroup(w_ffn_a_out, nz, 1),
        in_shard(w_qkv, False),
        in_shard(w_ffn_b_in, True),
        regroup(w_ffn_b_out, nz, 1),
    ]
    shards = lax.optimization_barrier(shards)
    own = [links.gather_z(v) for v in shards]
    other = []
    for v in own:
        other.append(links.swap_y(after(v, *other[-1:])))
    mixer_in, outs, ffn_a_in, ffn_a_out, qkv_in, ffn_b_in, ffn_b_out = zip(own, other)

    def rows_of(v, lo, hi):
        return v.reshape(nz, -1, features)[:, lo:hi].reshape(-1, features)

    cut, end = w_mixer_out.shape[0], w_mixer_out.shape[0] + w_attn_out.shape[0]
    mixer_out = links.by_y(*[rows_of(v, 0, cut) for v in outs])
    attn_out = ungroup(links.by_y(*[rows_of(v, cut, end) for v in outs]), nz, 0)
    ffn_a_out = links.by_y(*ffn_a_out)
    ffn_b_out = links.by_y(*ffn_b_out)

    seg = segment_ids.reshape(micro, length)
    masks = []
    for k in range(CONV):
        earlier = jnp.pad(seg, ((0, 0), (k, 0)), constant_values=-1)[:, :length]
        masks.append((earlier == seg).astype(f32))
    masks = jnp.stack(masks, axis=-1).reshape(micro, PIECES, rows, CONV)
    keep = masks[..., 1:2]
    slots = jnp.stack([sum(i * (ORDER[i] == (j ^ t)) for i in range(PIECES)) for j in range(PIECES)])
    slots = slots.astype(jnp.int32)
    seg_pieces = seg.reshape(micro, PIECES, rows)
    seg_rel = jnp.stack(
        [lax.dynamic_index_in_dim(seg_pieces, t ^ k, 1, False) for k in ORDER]
    )
    position = jnp.concatenate([(t ^ k) * rows + lax.iota(jnp.int32, rows) for k in ORDER])
    half = HEAD // 2
    frequency = jnp.exp(lax.iota(f32, half) * (-2.0 * math.log(10000.0) / HEAD))
    angles = position.astype(f32)[:, None] * frequency[None, :]
    cos, sin = jnp.cos(angles), jnp.sin(angles)
    tables = (
        jnp.concatenate([cos, cos], axis=1).reshape(PIECES, rows, HEAD),
        jnp.concatenate([-sin, sin], axis=1).reshape(PIECES, rows, HEAD),
        seg_rel[..., None],
        jnp.swapaxes(seg_rel, 0, 1).reshape(micro, 1, length),
        position[:, None],
        position[None, :],
    )

    def pieces(v):
        return v.reshape(PIECES, micro, rows, v.shape[-1])

    def flat(v):
        return v.reshape(PIECES * local, v.shape[-1])

    def enter(x, i):
        n, r = norm_forward(x, gains[i : i + 1])
        return links.gather_rows(links.own_first(n)), r

    x0 = regroup(after(hidden_in, *shards).reshape(local, features), nz, 1).astype(f32)
    n1, r1 = enter(x0, 0)
    pre = pieces(times(n1, *mixer_in))
    values, ext_part = conv_forward(slots, pre, masks, par, wx)
    ext = pieces(links.sum_rows(flat(ext_part)))
    gated, scanned, states = scan_forward(slots, ext, wdt, values, pre, par, rate, keep)
    x1 = x0 + links.scatter_rows(dot(flat(gated), mixer_out))

    n2, r2 = enter(x1, 1)
    y_a, kept_a = ffn_forward(links, n2, ffn_a_in, ffn_a_out)
    x2 = x1 + links.scatter_rows(y_a)

    n3, r3 = enter(x2, 2)
    mix, low = attention_forward(pieces(times(n3, *qkv_in)), tables)
    x3 = x2 + links.scatter_rows(dot(after(flat(mix), own[5]), attn_out))

    n4, r4 = enter(x3, 3)
    y_b, kept_b = ffn_forward(links, n4, ffn_b_in, ffn_b_out)
    x4 = x3 + links.scatter_rows(y_b)
    block_out = ungroup(x4, nz, 1).astype(bf16).reshape(hidden_in.shape)

    def leave(g, x, r, i, d_normed, *order):
        d_n = links.own_first(links.scatter_rows(d_normed, *order))
        d_x, d_gain = norm_backward(x, r, gains[i : i + 1], d_n)
        return g + d_x, d_gain

    g4_low = regroup(out_grad.reshape(local, features), nz, 1)
    g4 = g4_low.astype(f32)
    fh = features // 2
    dy4 = links.gather_rows(g4_low)
    d_n4, b_in, b_out = ffn_backward(links, dy4, kept_b, ffn_b_in, ffn_b_out)
    g3, gain_d = leave(g4, x3, r4, 3, d_n4, b_out.finish(d_n4))

    dy3 = links.gather_rows(g3.astype(bf16))
    mix_own, mix_other = split_y(links, regroup(flat(mix), nz, 1))
    a_out = Sent(links, mix_own, mix_other, dy3, b_in.came)
    d_mix = dot_nt(after(dy3, a_out.product), attn_out).astype(bf16)
    d_qkv = flat(attention_backward(low, pieces(d_mix), tables))
    q_in = Sent(links, n3[:, :fh], n3[:, fh:], d_qkv, a_out.came)
    d_qkv = after(d_qkv, q_in.product, b_in.finish(b_out.out, q_in.product))
    d_n3 = back_times(d_qkv, *qkv_in)
    g2, gain_c = leave(g3, x2, r3, 2, d_n3, a_out.finish(d_n3))

    dy2 = links.gather_rows(g2.astype(bf16))
    d_n2, f_in, f_out = ffn_backward(
        links, after(dy2, q_in.finish(dy2)), kept_a, ffn_a_in, ffn_a_out, q_in.came
    )
    d_n2 = after(d_n2, f_out.finish(b_in.out, d_n2))
    g1, gain_b = leave(g2, x1, r2, 1, d_n2)

    dy1 = links.gather_rows(g1.astype(bf16))
    gated = flat(gated)
    m_out = Sent(links, *split_y(links, gated), dy1, f_in.came)
    d_gated = pieces(dot_nt(after(dy1, m_out.product), mixer_out))
    d_dt, d_val, d_z, d_bc, d_rate, sums = scan_backward(
        slots, ext, wdt, values, pre, par, rate, keep, d_gated, scanned, states
    )
    d_dt, d_z = flat(d_dt), flat(d_z)
    m_z = Sent(links, n1[:, :fh], n1[:, fh:], d_z, m_out.came)
    d_dt = after(d_dt, m_z.product, f_in.finish(m_z.product, a_out.out, q_in.out, f_out.out))
    d_bc = d_bc[:, :, :, 0, :].reshape(PIECES, micro, 2, rows, STATE)
    d_bc = jnp.swapaxes(d_bc, 2, 3).reshape(PIECES * local, 2 * STATE)
    d_ext = links.sum_rows(jnp.concatenate([dot_nt(d_dt, wdt), d_bc], axis=1))
    grad_dt = dot_tn(flat(ext)[:, :RANK], d_dt)
    grad_x = dot_tn(flat(values), d_ext)
    d_x, conv_sums = conv_backward(
        slots, pieces(after(d_ext, m_out.finish(d_ext, direct=True))), d_val, pre, masks, par, wx
    )
    d_x = flat(d_x)
    m_x = Sent(links, n1[:, :fh], n1[:, fh:], d_x, m_z.came)
    d_x = after(d_x, m_x.product)
    d_n1 = back_times(d_x, *[w[:, :width] for w in mixer_in])
    d_n1 = d_n1 + back_times(d_z, *[w[:, width:] for w in mixer_in])
    d_n1 = after(d_n1, m_z.finish(d_n1, f_in.out))
    g0, gain_a = leave(g1, x0, r1, 0, d_n1)
    input_grad = ungroup(g0, nz, 1).astype(bf16).reshape(hidden_in.shape)
    m_x.finish(direct=True)

    grad_table = jnp.concatenate([conv_sums[: CONV + 1], sums[:2], d_rate * rate], axis=0)
    grad_gains = jnp.stack([gain_a, gain_b, gain_c, gain_d])

    def by_owner(v, axis):
        u = v.shape[axis] // dp
        v = v.reshape(v.shape[:axis] + (2, nz, u) + v.shape[axis + 1 :])
        return jnp.moveaxis(v, (axis, axis + 1), (0, 1)).reshape(2, nz, -1)

    packed = jnp.concatenate(
        [by_owner(grad_gains, 1), by_owner(grad_x, 0), by_owner(grad_dt, 1), by_owner(grad_table, 1)],
        axis=2,
    )
    summed = links.scatter_small(packed)
    offset = 0
    grads = []
    for v in small:
        grads.append(summed[offset : offset + v.size].reshape(v.shape))
        offset += v.size
    gain_total = grads[0]
    gain_total = gain_total + links.swap_core(gain_total)
    gain_total = gain_total + links.swap_x(gain_total)

    def in_grad(v, like, group):
        v = v.reshape(like.shape)
        return ungroup(v, nz, 2) if group else v

    def out_grad_of(v):
        return ungroup(v.out, nz, 1)

    return (
        block_out,
        input_grad,
        gain_total,
        jnp.stack([ungroup(m_x.out, nz, 1), ungroup(m_z.out, nz, 1)], axis=1),
        grads[1],
        grads[2],
        grads[3],
        out_grad_of(m_out),
        in_grad(f_in.out, w_ffn_a_in, True),
        out_grad_of(f_out),
        in_grad(q_in.out, w_qkv, False),
        out_grad_of(a_out),
        in_grad(b_in.out, w_ffn_b_in, True),
        out_grad_of(b_out),
    )


def solution(mesh):
    def body(*args):
        return per_device(mesh, *args)

    rows = P(None, ("dp", "tensor"), None)
    weight_in = P("dp", None, "tensor")
    weight_out = P(("tensor", "dp"), None)
    columns = P(None, ("tensor", "dp"))
    gains = P(None, "dp")
    weights = (
        gains, weight_in, weight_out, columns, columns, weight_out, weight_in, weight_out,
        weight_in, weight_out, weight_in, weight_out,
    )
    return jax.shard_map(
        body,
        mesh=mesh,
        in_specs=(rows, rows, P(None, "dp")) + weights,
        out_specs=(rows, rows) + weights,
        check_vma=False,
    )
```

```python
import math

import jax
import jax.numpy as jnp
from jax import lax
from jax.experimental import pallas as pl
from jax.experimental.pallas import tpu as pltpu
from jax.sharding import PartitionSpec as P

STATE = 16
CONV = 4
RANK = 96
HEAD = 128
MICRO = 2
PIECES = 4
ORDER = (0, 2, 1, 3)

f32 = jnp.float32
bf16 = jnp.bfloat16
epsilon = 1e-05
floor_score = -1e30


def dot(a, b, dims=((1,), (0,)), out=f32):
    return lax.dot_general(a, b, (dims, ((), ())), preferred_element_type=out)


def dot_tn(a, b, out=f32):
    return dot(a, b, ((0,), (0,)), out)


def dot_nt(a, b, out=f32):
    return dot(a, b, ((1,), (1,)), out)


def sigmoid(v):
    return 1.0 / (1.0 + jnp.exp(-v))


def dsilu(v):
    s = jax.nn.sigmoid(v)
    return s * (1.0 + v * (1.0 - s))


def soft_plus(v):
    return jnp.maximum(v, 0.0) + jnp.log1p(jnp.exp(-jnp.abs(v)))


def conv_fwd_kernel(slot, x_ref, mask_ref, par_ref, wx_ref, val_ref, ext_ref, prev):
    @pl.when((pl.program_id(0) == 0) & (pl.program_id(1) == 0))
    def _():
        prev[...] = jnp.zeros_like(prev)

    x = x_ref[0, 0]
    rows = x.shape[0]
    xe = jnp.concatenate([prev[...], x], axis=0)
    mask = mask_ref[0, 0]
    conv = jnp.broadcast_to(par_ref[4:5, :], x.shape)
    for k in range(CONV):
        conv = conv + par_ref[k : k + 1, :] * xe[8 - k : 8 - k + rows] * mask[:, k : k + 1]
    prev[...] = x[rows - 8 :]
    val = (conv * sigmoid(conv)).astype(bf16)
    val_ref[0, 0] = val
    ext_ref[0, 0] = dot(val, wx_ref[...]).astype(bf16)


def conv_bwd_kernel(
    slot, dext_ref, dval_ref, x_ref, xp_ref, mask_ref, par_ref, wx_ref, dx_ref, sum_ref, after
):
    @pl.when((pl.program_id(0) == 0) & (pl.program_id(1) == 0))
    def _():
        after[...] = jnp.zeros_like(after)
        sum_ref[...] = jnp.zeros_like(sum_ref)

    x = x_ref[0, 0]
    rows = x.shape[0]
    xe = jnp.concatenate([xp_ref[0, 0], x], axis=0)
    mask = mask_ref[0, 0]
    conv = jnp.broadcast_to(par_ref[4:5, :], x.shape)
    for k in range(CONV):
        conv = conv + par_ref[k : k + 1, :] * xe[8 - k : 8 - k + rows] * mask[:, k : k + 1]
    sig = sigmoid(conv)
    d_conv = (dval_ref[0, 0] + dot_nt(dext_ref[0, 0], wx_ref[...])) * (
        sig * (1.0 + conv * (1.0 - sig))
    )
    d_x = jnp.zeros_like(x)
    sums = []
    for k in range(CONV):
        held = d_conv * mask[:, k : k + 1]
        sums.append(jnp.sum(held * xe[8 - k : 8 - k + rows], axis=0, keepdims=True))
        if k == 0:
            d_x = d_x + par_ref[0:1, :] * held
        else:
            he = jnp.concatenate([held, after[k - 1]], axis=0)
            d_x = d_x + par_ref[k : k + 1, :] * he[k : k + rows]
            after[k - 1] = held[:8]
    sums.append(jnp.sum(d_conv, axis=0, keepdims=True))
    for k in range(CONV + 1):
        sum_ref[k : k + 1, :] += sums[k]
    dx_ref[0, 0] = d_x.astype(bf16)


def coefficient_rows(ext):
    both = jnp.concatenate([ext, ext], axis=0)
    return both.T[RANK:]


def scan_fwd_kernel(
    slot, ext_ref, wdt_ref, val_ref, z_ref, par_ref, rate_ref, keep_ref,
    gated_ref, scan_ref, h_ref, state, se, sv, sc,
):
    @pl.when((pl.program_id(0) == 0) & (pl.program_id(1) == 0))
    def _():
        state[...] = jnp.zeros_like(state)

    ext_low = ext_ref[0, 0]
    step = soft_plus(dot(ext_low[:, :RANK], wdt_ref[...]) + par_ref[5:6, :])
    val = val_ref[0, 0].astype(f32)
    se[...] = jnp.where(keep_ref[0, 0] > 0.0, step, 1e30)
    sv[...] = step * val
    rate = rate_ref[...]
    coef = coefficient_rows(ext_low.astype(f32))
    shape = rate.shape

    def body(g, h):
        base = pl.multiple_of(8 * g, 8)
        turned = pltpu.roll(coef, (128 - base) % 128, 1)
        se_t = se[pl.ds(base, 8), :]
        sv_t = sv[pl.ds(base, 8), :]
        for j in range(8):
            a = jnp.exp(jnp.broadcast_to(se_t[j : j + 1], shape) * rate)
            h = a * h + jnp.broadcast_to(sv_t[j : j + 1], shape) * turned[:STATE, j : j + 1]
            h_ref[0, base + j] = h.astype(bf16)
            sc[pl.ds(base + j, 1), :] = jnp.sum(
                h * turned[STATE:, j : j + 1], axis=0, keepdims=True
            )
        return h

    state[...] = lax.fori_loop(0, se.shape[0] // 8, body, state[...])
    scanned = sc[...]
    z = z_ref[0, 0]
    scan_ref[0, 0] = scanned
    gated_ref[0, 0] = ((scanned + par_ref[6:7, :] * val) * (z * sigmoid(z))).astype(bf16)


def scan_bwd_kernel(
    slot, ext_ref, wdt_ref, val_ref, z_ref, par_ref, rate_ref, keep_ref, dg_ref, scan_ref,
    h_ref, hp_ref, ddt_ref, dval_ref, dz_ref, dbc_ref, drate_ref, sum_ref,
    carry, se, st, sv, ds, r1, r2, pb, pc,
):
    @pl.when((pl.program_id(0) == 0) & (pl.program_id(1) == 0))
    def _():
        carry[...] = jnp.zeros_like(carry)
        drate_ref[...] = jnp.zeros_like(drate_ref)
        sum_ref[...] = jnp.zeros_like(sum_ref)

    ext_low = ext_ref[0, 0]
    pre = dot(ext_low[:, :RANK], wdt_ref[...]) + par_ref[5:6, :]
    step = soft_plus(pre)
    val = val_ref[0, 0].astype(f32)
    z = z_ref[0, 0]
    sig_z = sigmoid(z)
    d_gated = dg_ref[0, 0].astype(f32)
    skip = par_ref[6:7, :]
    d_scan = d_gated * (z * sig_z)
    dz_ref[0, 0] = (
        d_gated * (scan_ref[0, 0] + skip * val) * (sig_z * (1.0 + z * (1.0 - sig_z)))
    ).astype(bf16)
    se[...] = jnp.where(keep_ref[0, 0] > 0.0, step, 1e30)
    st[...] = step
    sv[...] = step * val
    ds[...] = d_scan
    rate = rate_ref[...]
    shape = rate.shape
    coef = coefficient_rows(ext_low.astype(f32))
    count = se.shape[0] // 8
    lanes = shape[1] // 128

    def fold(v):
        total = v[:, :128]
        for i in range(1, lanes):
            total = total + v[:, 128 * i : 128 * (i + 1)]
        return total

    def body(i, held):
        back, d_rate = held
        base = pl.multiple_of(8 * (count - 1 - i), 8)
        turned = pltpu.roll(coef, (128 - base) % 128, 1)
        se_t = se[pl.ds(base, 8), :]
        st_t = st[pl.ds(base, 8), :]
        sv_t = sv[pl.ds(base, 8), :]
        ds_t = ds[pl.ds(base, 8), :]
        for j in range(7, -1, -1):
            row = base + j
            h_now = h_ref[0, row].astype(f32)
            if j > 0:
                h_before = h_ref[0, row - 1].astype(f32)
            else:
                h_before = jnp.where(
                    base == 0,
                    hp_ref[0, 0].astype(f32),
                    h_ref[0, jnp.maximum(row - 1, 0)].astype(f32),
                )
            a = jnp.exp(jnp.broadcast_to(se_t[j : j + 1], shape) * rate)
            d_row = jnp.broadcast_to(ds_t[j : j + 1], shape)
            lam = d_row * turned[STATE:, j : j + 1] + back
            back = a * lam
            w = back * h_before
            d_rate = d_rate + w * jnp.broadcast_to(st_t[j : j + 1], shape)
            r1[pl.ds(row, 1), :] = jnp.sum(w * rate, axis=0, keepdims=True)
            r2[pl.ds(row, 1), :] = jnp.sum(lam * turned[:STATE, j : j + 1], axis=0, keepdims=True)
            at = pl.ds(pl.multiple_of(row * STATE, STATE), STATE)
            pb[at, :] = fold(lam * jnp.broadcast_to(sv_t[j : j + 1], shape)).astype(bf16)
            pc[at, :] = fold(d_row * h_now).astype(bf16)
        return back, d_rate

    back, d_rate = lax.fori_loop(0, count, body, (carry[...], jnp.zeros(shape, f32)))
    carry[...] = back
    drate_ref[...] += d_rate
    ones = jnp.ones((8, 128), bf16)
    dbc_ref[0, 0, 0] = dot_nt(ones, pb[...])
    dbc_ref[0, 0, 1] = dot_nt(ones, pc[...])
    d_step = r1[...] + val * r2[...]
    d_dt = d_step * sigmoid(pre)
    dval_ref[0, 0] = step * r2[...] + skip * d_scan
    ddt_ref[0, 0] = d_dt.astype(bf16)
    sum_ref[0:1, :] += jnp.sum(d_dt, axis=0, keepdims=True)
    sum_ref[1:2, :] += jnp.sum(d_scan * val, axis=0, keepdims=True)


def turn(v, cos, sin):
    return v * cos + pltpu.roll(v, HEAD // 2, 1) * sin


def attention_parts(seg_c, seg_r, pos_c, pos_r):
    return (seg_c == seg_r) & (pos_r <= pos_c)


def attn_fwd_kernel(qkv_ref, cos_ref, sin_ref, segc, segr, posc, posr, mix_ref, low_ref):
    heads = qkv_ref.shape[3] // (3 * HEAD)
    length = PIECES * qkv_ref.shape[2]
    cos = cos_ref[...].reshape(length, HEAD)
    sin = sin_ref[...].reshape(length, HEAD)
    allowed = attention_parts(segc[...].reshape(length, 1), segr[0], posc[...], posr[...])

    def take(i):
        return qkv_ref[:, 0, :, i * HEAD : (i + 1) * HEAD].reshape(length, HEAD)

    def put(ref, i, v):
        ref[:, 0, :, i * HEAD : (i + 1) * HEAD] = v.reshape(PIECES, -1, HEAD)

    for h in range(heads):
        q = turn(take(h), cos, sin).astype(bf16)
        k = turn(take(heads + h), cos, sin).astype(bf16)
        v = take(2 * heads + h).astype(bf16)
        scores = jnp.where(allowed, dot_nt(q, k) * HEAD ** (-0.5), floor_score)
        e = jnp.exp(scores - jnp.max(scores, axis=1, keepdims=True))
        probs = (e / jnp.sum(e, axis=1, keepdims=True)).astype(bf16)
        put(mix_ref, h, dot(probs, v).astype(bf16))
        put(low_ref, h, q)
        put(low_ref, heads + h, k)
        put(low_ref, 2 * heads + h, v)


def attn_bwd_kernel(low_ref, dmix_ref, cos_ref, sin_ref, segc, segr, posc, posr, dqkv_ref):
    heads = low_ref.shape[3] // (3 * HEAD)
    length = PIECES * low_ref.shape[2]
    cos = cos_ref[...].reshape(length, HEAD)
    sin = -sin_ref[...].reshape(length, HEAD)
    allowed = attention_parts(segc[...].reshape(length, 1), segr[0], posc[...], posr[...])
    scale = HEAD ** (-0.5)

    def take(ref, i):
        return ref[:, 0, :, i * HEAD : (i + 1) * HEAD].reshape(length, HEAD)

    def put(i, v):
        dqkv_ref[:, 0, :, i * HEAD : (i + 1) * HEAD] = v.astype(bf16).reshape(PIECES, -1, HEAD)

    for h in range(heads):
        q, k, v = take(low_ref, h), take(low_ref, heads + h), take(low_ref, 2 * heads + h)
        d_mix = take(dmix_ref, h)
        scores = jnp.where(allowed, dot_nt(q, k) * scale, floor_score)
        e = jnp.exp(scores - jnp.max(scores, axis=1, keepdims=True))
        probs = e / jnp.sum(e, axis=1, keepdims=True)
        d_probs = dot_nt(d_mix, v)
        d_scores = (
            probs * (d_probs - jnp.sum(probs * d_probs, axis=1, keepdims=True))
        ).astype(bf16)
        put(h, turn(dot(d_scores, k) * scale, cos, sin))
        put(heads + h, turn(dot_tn(d_scores, q) * scale, cos, sin))
        put(2 * heads + h, dot_tn(probs.astype(bf16), d_mix))


BIG = 48 * 1024 * 1024
BRIEF = pl.CostEstimate(flops=1, bytes_accessed=1, transcendentals=0)


def params(dims):
    return pltpu.CompilerParams(
        dimension_semantics=("arbitrary",) * dims, vmem_limit_bytes=BIG
    )


def rel(rows, cols, col=0):
    return pl.BlockSpec((1, 1, rows, cols), lambda m, j, s: (s[j], m, 0, col))


def rel_back(rows, cols, col=0):
    return pl.BlockSpec((1, 1, rows, cols), lambda m, j, s: (s[PIECES - 1 - j], m, 0, col))


def ordered(rows, cols):
    return pl.BlockSpec((1, 1, rows, cols), lambda m, j, s: (m, j, 0, 0))


def ordered_back(rows, cols):
    return pl.BlockSpec((1, 1, rows, cols), lambda m, j, s: (m, PIECES - 1 - j, 0, 0))


def fixed(*shape):
    return pl.BlockSpec(shape, lambda m, j, s: (0,) * len(shape))


def conv_forward(slots, pre, masks, par, wx):
    rows, width = pre.shape[2], pre.shape[3] // 2
    grid = pltpu.PrefetchScalarGridSpec(
        num_scalar_prefetch=1,
        grid=(MICRO, PIECES),
        in_specs=[rel(rows, width), ordered(rows, CONV), fixed(8, width), fixed(*wx.shape)],
        out_specs=[rel(rows, width), rel(rows, wx.shape[1])],
        scratch_shapes=[pltpu.VMEM((8, width), f32)],
    )
    return pl.pallas_call(
        conv_fwd_kernel,
        grid_spec=grid,
        out_shape=[
            jax.ShapeDtypeStruct((PIECES, MICRO, rows, width), bf16),
            jax.ShapeDtypeStruct((PIECES, MICRO, rows, wx.shape[1]), bf16),
        ],
        compiler_params=params(2),
        cost_estimate=BRIEF,
        name="conv_forward",
    )(slots, pre, masks, par, wx)


def conv_backward(slots, d_ext, d_val, pre, masks, par, wx):
    rows, width = pre.shape[2], pre.shape[3] // 2
    last = rows // 8 - 1
    grid = pltpu.PrefetchScalarGridSpec(
        num_scalar_prefetch=1,
        grid=(MICRO, PIECES),
        in_specs=[
            rel_back(rows, wx.shape[1]),
            rel_back(rows, width),
            rel_back(rows, width),
            pl.BlockSpec(
                (1, 1, 8, width),
                lambda m, j, s: (s[jnp.maximum(PIECES - 2 - j, 0)], m, last, 0),
            ),
            ordered_back(rows, CONV),
            fixed(8, width),
            fixed(*wx.shape),
        ],
        out_specs=[rel_back(rows, width), fixed(8, width)],
        scratch_shapes=[pltpu.VMEM((CONV - 1, 8, width), f32)],
    )
    return pl.pallas_call(
        conv_bwd_kernel,
        grid_spec=grid,
        out_shape=[
            jax.ShapeDtypeStruct((PIECES, MICRO, rows, width), bf16),
            jax.ShapeDtypeStruct((8, width), f32),
        ],
        compiler_params=params(2),
        cost_estimate=BRIEF,
        name="conv_backward",
    )(slots, d_ext, d_val, pre, pre, masks, par, wx)


def scan_forward(slots, ext, wdt, val, pre, par, rate, keep):
    rows, width = val.shape[2], val.shape[3]
    grid = pltpu.PrefetchScalarGridSpec(
        num_scalar_prefetch=1,
        grid=(MICRO, PIECES),
        in_specs=[
            rel(rows, ext.shape[3]), fixed(*wdt.shape), rel(rows, width), rel(rows, width, 1),
            fixed(8, width), fixed(STATE, width), ordered(rows, 1),
        ],
        out_specs=[
            rel(rows, width), rel(rows, width),
            pl.BlockSpec((1, rows, STATE, width), lambda m, j, s: (m * PIECES + j, 0, 0, 0)),
        ],
        scratch_shapes=[pltpu.VMEM((STATE, width), f32)] + [pltpu.VMEM((rows, width), f32)] * 3,
    )
    return pl.pallas_call(
        scan_fwd_kernel,
        grid_spec=grid,
        out_shape=[
            jax.ShapeDtypeStruct((PIECES, MICRO, rows, width), bf16),
            jax.ShapeDtypeStruct((PIECES, MICRO, rows, width), f32),
            jax.ShapeDtypeStruct((MICRO * PIECES, rows, STATE, width), bf16),
        ],
        compiler_params=params(2),
        cost_estimate=BRIEF,
        name="scan_forward",
    )(slots, ext, wdt, val, pre, par, rate, keep)


def scan_backward(slots, ext, wdt, val, pre, par, rate, keep, d_gated, scanned, states):
    rows, width = val.shape[2], val.shape[3]
    grid = pltpu.PrefetchScalarGridSpec(
        num_scalar_prefetch=1,
        grid=(MICRO, PIECES),
        in_specs=[
            rel_back(rows, ext.shape[3]), fixed(*wdt.shape), rel_back(rows, width),
            rel_back(rows, width, 1), fixed(8, width), fixed(STATE, width), ordered_back(rows, 1),
            rel_back(rows, width), rel_back(rows, width),
            pl.BlockSpec(
                (1, rows, STATE, width),
                lambda m, j, s: (m * PIECES + PIECES - 1 - j, 0, 0, 0),
            ),
            pl.BlockSpec(
                (1, 1, STATE, width),
                lambda m, j, s: (
                    jnp.maximum(m * PIECES + PIECES - 2 - j, 0), rows - 1, 0, 0,
                ),
            ),
        ],
        out_specs=[
            rel_back(rows, width), rel_back(rows, width), rel_back(rows, width),
            pl.BlockSpec(
                (1, 1, 2, 8, rows * STATE),
                lambda m, j, s: (s[PIECES - 1 - j], m, 0, 0, 0),
            ),
            fixed(STATE, width), fixed(8, width),
        ],
        scratch_shapes=[pltpu.VMEM((STATE, width), f32)]
        + [pltpu.VMEM((rows, width), f32)] * 6
        + [pltpu.VMEM((rows * STATE, 128), bf16)] * 2,
    )
    return pl.pallas_call(
        scan_bwd_kernel,
        grid_spec=grid,
        out_shape=[
            jax.ShapeDtypeStruct((PIECES, MICRO, rows, width), bf16),
            jax.ShapeDtypeStruct((PIECES, MICRO, rows, width), f32),
            jax.ShapeDtypeStruct((PIECES, MICRO, rows, width), bf16),
            jax.ShapeDtypeStruct((PIECES, MICRO, 2, 8, rows * STATE), f32),
            jax.ShapeDtypeStruct((STATE, width), f32),
            jax.ShapeDtypeStruct((8, width), f32),
        ],
        compiler_params=params(2),
        cost_estimate=BRIEF,
        name="scan_backward",
    )(slots, ext, wdt, val, pre, par, rate, keep, d_gated, scanned, states, states)


def attention_specs(rows, length):
    return [
        pl.BlockSpec((PIECES, rows, HEAD), lambda m: (0, 0, 0)),
        pl.BlockSpec((PIECES, rows, HEAD), lambda m: (0, 0, 0)),
        pl.BlockSpec((PIECES, 1, rows, 1), lambda m: (0, m, 0, 0)),
        pl.BlockSpec((1, 1, length), lambda m: (m, 0, 0)),
        pl.BlockSpec((length, 1), lambda m: (0, 0)),
        pl.BlockSpec((1, length), lambda m: (0, 0)),
    ]


def attention_forward(qkv, tables):
    rows, width = qkv.shape[2], qkv.shape[3]

    def whole(cols):
        return pl.BlockSpec((PIECES, 1, rows, cols), lambda m: (0, m, 0, 0))

    return pl.pallas_call(
        attn_fwd_kernel,
        grid=(MICRO,),
        in_specs=[whole(width)] + attention_specs(rows, PIECES * rows),
        out_specs=[whole(width // 3), whole(width)],
        out_shape=[
            jax.ShapeDtypeStruct((PIECES, MICRO, rows, width // 3), bf16),
            jax.ShapeDtypeStruct((PIECES, MICRO, rows, width), bf16),
        ],
        compiler_params=params(1),
        cost_estimate=BRIEF,
        name="attention_forward",
    )(qkv, *tables)


def attention_backward(low, d_mix, tables):
    rows, width = low.shape[2], low.shape[3]

    def whole(cols):
        return pl.BlockSpec((PIECES, 1, rows, cols), lambda m: (0, m, 0, 0))

    return pl.pallas_call(
        attn_bwd_kernel,
        grid=(MICRO,),
        in_specs=[whole(width), whole(width // 3)] + attention_specs(rows, PIECES * rows),
        out_specs=whole(width),
        out_shape=jax.ShapeDtypeStruct((PIECES, MICRO, rows, width), bf16),
        compiler_params=params(1),
        cost_estimate=BRIEF,
        name="attention_backward",
    )(low, d_mix, *tables)


def tile_of(n):
    return 256 if n % 256 == 0 else n


def tn_kernel(count, added, *refs):
    left, rights, adds, out = refs[0], refs[1 : 1 + count], refs[1 + count : -1], refs[-1]
    col = 0
    for i in range(count):
        width = rights[i].shape[1]
        part = dot_tn(left[...], rights[i][...])
        if added:
            part = part + adds[0][:, col : col + width].astype(f32)
        out[:, col : col + width] = part.astype(bf16)
        col += width


def product_tn(left, rights, adds=()):
    rows, m = left.shape
    tile = tile_of(m)
    width = sum(v.shape[1] for v in rights)
    whole = [pl.BlockSpec(v.shape, lambda i: (0, 0)) for v in rights]
    return pl.pallas_call(
        lambda *refs: tn_kernel(len(rights), bool(adds), *refs),
        grid=(m // tile,),
        in_specs=[pl.BlockSpec((rows, tile), lambda i: (0, i))]
        + whole
        + [pl.BlockSpec((tile, v.shape[1]), lambda i: (i, 0)) for v in adds],
        out_specs=pl.BlockSpec((tile, width), lambda i: (i, 0)),
        out_shape=jax.ShapeDtypeStruct((m, width), bf16),
        compiler_params=params(1),
        cost_estimate=BRIEF,
        name="product_tn",
    )(left, *rights, *adds)


def nt_kernel(count, steps, *refs):
    ds, ws, out = refs[:count], refs[count:-1], refs[-1]

    def part(w):
        total, col = None, 0
        for d in ds:
            width = d.shape[1]
            term = dot_nt(d[...], w[:, col : col + width])
            total = term if total is None else total + term
            col += width
        out[...] = total.astype(bf16)

    if len(ws) == 1:
        part(ws[0])
    else:
        pl.when(pl.program_id(0) < steps)(lambda: part(ws[0]))
        pl.when(pl.program_id(0) >= steps)(lambda: part(ws[1]))


def product_nt(ds, ws):
    rows = ds[0].shape[0]
    m, width = ws[0].shape
    tile = tile_of(m)
    steps = m // tile
    maps = [lambda i: (jnp.minimum(i, steps - 1), 0), lambda i: (jnp.maximum(i - steps, 0), 0)]
    return pl.pallas_call(
        lambda *refs: nt_kernel(len(ds), steps, *refs),
        grid=(steps * len(ws),),
        in_specs=[pl.BlockSpec(v.shape, lambda i: (0, 0)) for v in ds]
        + [pl.BlockSpec((tile, width), maps[j]) for j in range(len(ws))],
        out_specs=pl.BlockSpec((rows, tile), lambda i: (0, i)),
        out_shape=jax.ShapeDtypeStruct((rows, m * len(ws)), bf16),
        compiler_params=params(1),
        cost_estimate=BRIEF,
        name="product_nt",
    )(*ds, *ws)


def gate_bwd_kernel(dy, w, gate, up, d_gate, d_up):
    d_hid = dot_nt(dy[...], w[...])
    g = gate[...].astype(f32)
    sig = sigmoid(g)
    d_gate[...] = (d_hid * up[...].astype(f32) * (sig * (1.0 + g * (1.0 - sig)))).astype(bf16)
    d_up[...] = (d_hid * (g * sig)).astype(bf16)


def gate_backward(dy, w, gate, up):
    rows, units = gate.shape
    tile = tile_of(units)
    column = pl.BlockSpec((rows, tile), lambda i: (0, i))
    return pl.pallas_call(
        gate_bwd_kernel,
        grid=(units // tile,),
        in_specs=[
            pl.BlockSpec(dy.shape, lambda i: (0, 0)),
            pl.BlockSpec((tile, w.shape[1]), lambda i: (i, 0)),
            column,
            column,
        ],
        out_specs=[column, column],
        out_shape=[jax.ShapeDtypeStruct((rows, units), bf16)] * 2,
        compiler_params=params(1),
        cost_estimate=BRIEF,
        name="gate_backward",
    )(dy, w, gate, up)


def spread_kernel(nz, count, *refs):
    terms, out = refs[:-1], refs[-1]
    total = sum(v[...].astype(f32) for v in terms)
    cols = total.shape[1] // count
    u = cols // (2 * nz)
    for i in range(count):
        blocks = []
        for z in range(nz):
            for y in range(2):
                at = i * cols + (y * nz + z) * u
                blocks.append(total[:, at : at + u])
        if count == 1:
            out[...] = jnp.concatenate(blocks, axis=1)
        else:
            for j, block in enumerate(blocks):
                out[:, i, j * u : (j + 1) * u] = block


def spread(terms, nz, shape):
    rows, cols = terms[0].shape
    count = shape[1] if len(shape) == 3 else 1
    tile = rows // 2 if rows % 32 == 0 else rows
    block = (tile, cols) if count == 1 else (tile, count, cols // count)
    return pl.pallas_call(
        lambda *refs: spread_kernel(nz, count, *refs),
        grid=(rows // tile,),
        in_specs=[pl.BlockSpec((tile, cols), lambda i: (i, 0))] * len(terms),
        out_specs=pl.BlockSpec(block, lambda i: (i,) + (0,) * (len(block) - 1)),
        out_shape=jax.ShapeDtypeStruct(shape, f32),
        compiler_params=params(1),
        cost_estimate=BRIEF,
        name="spread",
    )(*terms)


class Links:
    def __init__(self, mesh):
        self.dp = mesh.shape["dp"]
        self.nz = self.dp // 2
        self.y = lax.axis_index("dp") % 2
        self.z = lax.axis_index("dp") // 2
        self.t = lax.axis_index("tensor")
        self.groups = [[2 * z + y for z in range(self.nz)] for y in range(2)]

    def swap_y(self, v):
        return lax.ppermute(v, "dp", [(i, i ^ 1) for i in range(self.dp)])

    def shift_z(self, v, k):
        n = self.nz
        return lax.ppermute(
            v, "dp", [(2 * z + y, 2 * ((z + k) % n) + y) for z in range(n) for y in range(2)]
        )

    def swap_core(self, v):
        return lax.ppermute(v, "tensor", [(i, i ^ 1) for i in range(PIECES)])

    def swap_x(self, v):
        return lax.ppermute(v, "tensor", [(i, i ^ 2) for i in range(PIECES)])

    def gather_z(self, v):
        return lax.all_gather(v, "dp", axis=0, tiled=True, axis_index_groups=self.groups)

    def scatter_z(self, v):
        return lax.psum_scatter(
            v, "dp", scatter_dimension=0, tiled=True, axis_index_groups=self.groups
        )

    def gather_small(self, v):
        if self.dp > 8:
            both = self.by_y(v[None], self.swap_y(v)[None])
            return jnp.swapaxes(self.gather_z(both[None]), 0, 1)
        n = self.dp
        came = [v] + [
            lax.ppermute(v, "dp", [(i, (i + k) % n) for i in range(n)]) for k in range(1, n)
        ]
        ring = jnp.stack(came[:0:-1] + came[:1] + came[:0:-1])
        window = lax.dynamic_slice_in_dim(ring, n - 1 - lax.axis_index("dp"), n, 0)
        return jnp.swapaxes(window.reshape(self.nz, 2, -1), 0, 1)

    def scatter_small(self, v, order=()):
        low = v.astype(bf16)
        own = lax.dynamic_index_in_dim(v, self.y, 0, False)
        other = self.swap_y(lax.dynamic_index_in_dim(low, 1 - self.y, 0, False))
        part = after(own + other.astype(f32), *order)
        if self.nz > 4:
            return self.scatter_z(part.astype(bf16))[0].astype(f32)
        total = lax.dynamic_index_in_dim(part, self.z, 0, False)
        part_low = part.astype(bf16)
        for k in range(1, self.nz):
            piece = lax.dynamic_index_in_dim(part_low, (self.z + k) % self.nz, 0, False)
            total = total + self.shift_z(piece, k).astype(f32)
        return total

    def by_y(self, own, other, axis=0):
        return jnp.where(
            self.y == 0,
            jnp.concatenate([own, other], axis),
            jnp.concatenate([other, own], axis),
        )

    def own_first(self, v):
        half = v.shape[1] // 2
        return jnp.where(
            self.y == 0, v, jnp.concatenate([v[:, half:], v[:, :half]], axis=1)
        )

    def gather_rows(self, v):
        x = self.swap_x(v)
        core = self.swap_core(v)
        return jnp.concatenate([v, x, core, self.swap_core(x)], axis=0)

    def scatter_rows(self, part, *order):
        quarter = part.shape[0] // PIECES
        came = self.swap_core(part[2 * quarter :].astype(bf16)).astype(f32)
        x = (part[quarter : 2 * quarter].astype(f32) + came[quarter:]).astype(bf16)
        x = self.swap_x(after(x, *order))
        return part[:quarter].astype(f32) + came[:quarter] + x.astype(f32)

    def sum_rows(self, v):
        low = v.astype(bf16)
        q = low.shape[0] // PIECES
        turned = jnp.concatenate([low[2 * q :], low[: 2 * q]], axis=0)
        low = (low.astype(f32) + self.swap_core(turned).astype(f32)).astype(bf16)
        turned = jnp.concatenate([low[q : 2 * q], low[:q], low[3 * q :], low[2 * q : 3 * q]], axis=0)
        return (low.astype(f32) + self.swap_x(turned).astype(f32)).astype(bf16)

    def gather_z_direct(self, shard):
        if self.nz > 4:
            return self.gather_z(shard)
        came = [shard] + [self.shift_z(shard, k) for k in range(1, self.nz)]
        ring = jnp.concatenate(came[:0:-1] + came[:1] + came[:0:-1], axis=0)
        rows = shard.shape[0]
        return lax.dynamic_slice_in_dim(
            ring, (self.nz - 1 - self.z) * rows, self.nz * rows, 0
        )

    def scatter_z_direct(self, v):
        if self.nz > 4:
            return [self.scatter_z(v)]
        rows = v.shape[0] // self.nz
        terms = [lax.dynamic_slice_in_dim(v, self.z * rows, rows, 0)]
        for k in range(1, self.nz):
            piece = lax.dynamic_slice_in_dim(v, ((self.z + k) % self.nz) * rows, rows, 0)
            terms.append(self.shift_z(piece, k))
        return terms


class Sent:
    def __init__(self, links, left_own, left_other, rights, *order):
        self.links, self.left, self.rights = links, left_own, rights
        self.product = product_tn(left_other, rights)
        self.came = links.swap_y(after(self.product, *order))

    def finish(self, *order, direct=False):
        self.total = product_tn(self.left, self.rights, [after(self.came, *order)])
        if direct:
            self.terms = self.links.scatter_z_direct(self.total)
        else:
            self.terms = [self.links.scatter_z(self.total)]
        return self.total

    def land(self, *order):
        return [after(v, *order) for v in self.terms]


def after(v, *order):
    if not order:
        return v
    return lax.optimization_barrier((v,) + order)[0]


def regroup(v, nz, axis):
    shape = v.shape
    u = shape[axis] // (2 * nz)
    v = v.reshape(shape[:axis] + (nz, 2, u) + shape[axis + 1 :])
    return jnp.swapaxes(v, axis, axis + 1).reshape(shape)


def ungroup(v, nz, axis):
    shape = v.shape
    u = shape[axis] // (2 * nz)
    v = v.reshape(shape[:axis] + (2, nz, u) + shape[axis + 1 :])
    return jnp.swapaxes(v, axis, axis + 1).reshape(shape)


def norm_forward(x, gain):
    r = lax.rsqrt(jnp.mean(x * x, axis=1, keepdims=True) + epsilon)
    return (x * r * gain).astype(bf16), r


def norm_backward(x, r, gain, d_n):
    u = x * r
    g = d_n * gain
    d_x = r * (g - u * jnp.mean(g * u, axis=1, keepdims=True))
    return d_x, jnp.sum(d_n * u, axis=0)


def times(x, own, other, *order):
    half = x.shape[1] // 2
    return after(dot(x[:, :half], own), *order) + dot(x[:, half:], other)


def back_times(d, own, other):
    return jnp.concatenate([dot_nt(d, own), dot_nt(d, other)], axis=1)


def ffn_forward(n, w_in, *order):
    pair = times(n, *w_in, *order)
    units = pair.shape[1] // 2
    gate, up = pair[:, :units], pair[:, units:]
    hid = (gate * jax.nn.sigmoid(gate) * up).astype(bf16)
    return hid, (n, gate.astype(bf16), up.astype(bf16), hid)


def split_y(links, v):
    half = v.shape[1] // 2
    own = lax.dynamic_slice_in_dim(v, links.y * half, half, 1)
    other = lax.dynamic_slice_in_dim(v, (1 - links.y) * half, half, 1)
    return own, other


def ffn_backward(links, dy, kept, w_out, *order, finish=None):
    n, gate, up, hid = kept
    hid_own, hid_other = split_y(links, hid)
    sent_out = Sent(links, hid_own, hid_other, [dy], *order)
    dy = after(dy, sent_out.product)
    if finish is not None:
        dy = after(dy, finish.finish(sent_out.product))
    d_pair = gate_backward(dy, w_out, gate, up)
    half = n.shape[1] // 2
    sent_in = Sent(links, n[:, :half], n[:, half:], d_pair, sent_out.came)
    return sent_in, sent_out, [after(d_pair[0], sent_in.product), d_pair[1]]


def per_device(
    mesh,
    hidden_in, out_grad, segment_ids, norm_gains, w_mixer_in, w_xproj, w_dtproj, mixer_params,
    w_mixer_out, w_ffn_a_in, w_ffn_a_out, w_qkv, w_attn_out, w_ffn_b_in, w_ffn_b_out,
):
    links = Links(mesh)
    nz, dp, t = links.nz, links.dp, links.t
    micro, rows, features = hidden_in.shape
    local = micro * rows
    length = PIECES * rows

    small = [norm_gains, w_xproj, w_dtproj, mixer_params]
    gathered = links.gather_small(jnp.concatenate([v.reshape(-1) for v in small]))
    offset = 0
    parts = []
    for v in small:
        parts.append(gathered[:, :, offset : offset + v.size].reshape((2, nz) + v.shape))
        offset += v.size
    gains = jnp.moveaxis(parts[0], 2, 0).reshape(norm_gains.shape[0], features).astype(f32)
    wx = parts[1].reshape(-1, w_xproj.shape[1])
    wdt = jnp.moveaxis(parts[2], 2, 0).reshape(w_dtproj.shape[0], -1)
    table = jnp.moveaxis(parts[3], 2, 0).reshape(mixer_params.shape[0], -1).astype(f32)
    width = table.shape[1]
    par = jnp.concatenate([table[: CONV + 3], jnp.zeros((1, width), f32)], axis=0)
    rate = -jnp.exp(table[CONV + 3 :])

    def in_shard(w, group):
        if group:
            w = regroup(w, nz, 2)
        return w.reshape(w.shape[0], -1)

    shards = [
        in_shard(w_mixer_in, True),
        jnp.concatenate([regroup(w_mixer_out, nz, 1), regroup(w_attn_out, nz, 1)], axis=0),
        in_shard(w_ffn_a_in, True),
        regroup(w_ffn_a_out, nz, 1),
        in_shard(w_qkv, False),
        in_shard(w_ffn_b_in, True),
        regroup(w_ffn_b_out, nz, 1),
    ]
    shards[1:] = lax.optimization_barrier(shards[1:])
    own = [links.gather_z(v) for v in shards]
    other = []
    for v in own:
        other.append(links.swap_y(after(v, *other[-1:])))
    mixer_in, outs, ffn_a_in, ffn_a_out, qkv_in, ffn_b_in, ffn_b_out = zip(own, other)

    def rows_of(v, lo, hi):
        return v.reshape(nz, -1, features)[:, lo:hi].reshape(-1, features)

    cut, end = w_mixer_out.shape[0], w_mixer_out.shape[0] + w_attn_out.shape[0]
    mixer_out = links.by_y(*[rows_of(v, 0, cut) for v in outs])
    attn_out = ungroup(links.by_y(*[rows_of(v, cut, end) for v in outs]), nz, 0)
    ffn_a_out = links.by_y(*ffn_a_out)
    ffn_b_out = links.by_y(*ffn_b_out)

    seg = segment_ids.reshape(micro, length)
    masks = []
    for k in range(CONV):
        earlier = jnp.pad(seg, ((0, 0), (k, 0)), constant_values=-1)[:, :length]
        masks.append((earlier == seg).astype(f32))
    masks = jnp.stack(masks, axis=-1).reshape(micro, PIECES, rows, CONV)
    keep = masks[..., 1:2]
    slots = jnp.stack([sum(i * (ORDER[i] == (j ^ t)) for i in range(PIECES)) for j in range(PIECES)])
    slots = slots.astype(jnp.int32)
    seg_pieces = seg.reshape(micro, PIECES, rows)
    seg_rel = jnp.stack(
        [lax.dynamic_index_in_dim(seg_pieces, t ^ k, 1, False) for k in ORDER]
    )
    position = jnp.concatenate([(t ^ k) * rows + lax.iota(jnp.int32, rows) for k in ORDER])
    half = HEAD // 2
    frequency = jnp.exp(lax.iota(f32, half) * (-2.0 * math.log(10000.0) / HEAD))
    angles = position.astype(f32)[:, None] * frequency[None, :]
    cos, sin = jnp.cos(angles), jnp.sin(angles)
    tables = (
        jnp.concatenate([cos, cos], axis=1).reshape(PIECES, rows, HEAD),
        jnp.concatenate([-sin, sin], axis=1).reshape(PIECES, rows, HEAD),
        seg_rel[..., None],
        jnp.swapaxes(seg_rel, 0, 1).reshape(micro, 1, length),
        position[:, None],
        position[None, :],
    )

    def pieces(v):
        return v.reshape(PIECES, micro, rows, v.shape[-1])

    def flat(v):
        return v.reshape(PIECES * local, v.shape[-1])

    def enter(x, i):
        n, r = norm_forward(x, gains[i : i + 1])
        return links.gather_rows(links.own_first(n)), r

    x0 = regroup(after(hidden_in, *shards[1:]).reshape(local, features), nz, 1).astype(f32)
    n1, r1 = enter(x0, 0)
    pre = pieces(times(n1, *mixer_in))
    values, ext_part = conv_forward(slots, pre, masks, par, wx)
    ext = pieces(links.sum_rows(flat(ext_part)))
    gated, scanned, states = scan_forward(slots, ext, wdt, values, pre, par, rate, keep)
    x1 = x0 + links.scatter_rows(dot(flat(gated), mixer_out))

    n2, r2 = enter(x1, 1)
    g4_low = regroup(out_grad.reshape(local, features), nz, 1)
    dy4 = links.gather_rows(g4_low)
    hid_a, kept_a = ffn_forward(after(n2, dy4), ffn_a_in, own[4])
    x2 = x1 + links.scatter_rows(dot(hid_a, ffn_a_out), other[4])

    n3, r3 = enter(x2, 2)
    mix, low = attention_forward(pieces(times(n3, *qkv_in)), tables)
    mix = after(flat(mix), other[5])
    mix_own, mix_other = split_y(links, regroup(mix, nz, 1))
    x3 = x2 + links.scatter_rows(dot(mix, attn_out), own[6])

    n4, r4 = enter(x3, 3)
    n4 = after(n4, mix_own, mix_other, other[6])
    hid_b, kept_b = ffn_forward(n4, ffn_b_in)

    def leave(g, x, r, i, d_normed, *order, late=()):
        d_n = links.own_first(after(links.scatter_rows(d_normed, *order), *late))
        d_x, d_gain = norm_backward(x, r, gains[i : i + 1], d_n)
        return g + d_x, d_gain

    g4 = g4_low.astype(f32)
    fh = features // 2
    b_in, b_out, d_pair = ffn_backward(links, dy4, kept_b, ffn_b_out)
    x4 = x3 + links.scatter_rows(dot(after(hid_b, b_in.product), ffn_b_out))
    block_out = ungroup(x4, nz, 1).astype(bf16).reshape(hidden_in.shape)
    d_n4 = product_nt(d_pair, ffn_b_in)
    g3, gain_d = leave(g4, x3, r4, 3, d_n4, b_out.came)

    dy3 = links.gather_rows(g3.astype(bf16))
    dy3 = after(dy3, b_out.finish(g3))
    a_out = Sent(links, mix_own, mix_other, [dy3], b_in.came)
    d_mix = product_nt([after(dy3, a_out.product)], [attn_out])
    d_qkv = flat(attention_backward(low, pieces(d_mix), tables))
    q_in = Sent(links, n3[:, :fh], n3[:, fh:], [d_qkv], a_out.came)
    done = b_in.finish(b_out.terms[0], q_in.product, block_out)
    d_n3 = product_nt([after(d_qkv, done, a_out.came)], qkv_in)
    g2, gain_c = leave(g3, x2, r3, 2, d_n3, a_out.finish(d_n3))

    dy2 = links.gather_rows(g2.astype(bf16))
    dy2 = after(dy2, q_in.came)
    f_in, f_out, d_pair = ffn_backward(
        links, dy2, kept_a, ffn_a_out, q_in.came, finish=q_in
    )
    d_n2 = product_nt(d_pair, ffn_a_in)
    g1, gain_b = leave(g2, x1, r2, 1, d_n2, f_out.came)

    dy1 = links.gather_rows(g1.astype(bf16))
    dy1 = after(dy1, f_out.finish(b_in.terms[0], g1))
    gated = flat(gated)
    m_out = Sent(links, *split_y(links, gated), [dy1], f_in.came)
    d_gated = pieces(product_nt([after(dy1, m_out.product)], [mixer_out]))
    d_dt, d_val, d_z, d_bc, d_rate, sums = scan_backward(
        slots, ext, wdt, values, pre, par, rate, keep, d_gated, scanned, states
    )
    d_dt, d_z = flat(d_dt), flat(d_z)
    m_z = Sent(links, n1[:, :fh], n1[:, fh:], [d_z], m_out.came)
    d_dt = after(d_dt, f_in.finish(m_z.product, a_out.terms[0], q_in.terms[0], f_out.terms[0]))
    d_bc = d_bc[:, :, :, 0, :].reshape(PIECES, micro, 2, rows, STATE)
    d_bc = jnp.swapaxes(d_bc, 2, 3).reshape(PIECES * local, 2 * STATE)
    d_ext = links.sum_rows(jnp.concatenate([dot_nt(d_dt, wdt), d_bc], axis=1))
    d_x, conv_sums = conv_backward(slots, pieces(d_ext), d_val, pre, masks, par, wx)
    d_x = flat(d_x)
    m_x = Sent(links, n1[:, :fh], n1[:, fh:], [d_x], m_z.came)
    d_x = after(d_x, m_x.product, m_out.finish(m_x.product))

    grad_dt = dot_tn(d_dt, flat(ext)[:, :RANK])
    grad_x = dot_tn(flat(values), d_ext)
    grad_table = jnp.concatenate([conv_sums[: CONV + 1], sums[:2], d_rate * rate], axis=0)
    packed = jnp.concatenate([grad_x, grad_dt, grad_table.T], axis=1)
    summed = links.scatter_small(after(packed, m_x.product).reshape(2, nz, -1, packed.shape[1]))
    states = w_xproj.shape[1]
    grads = [
        summed[:, :states],
        summed[:, states : states + RANK].T,
        summed[:, states + RANK :].T,
    ]

    d_n1 = product_nt([d_x, d_z], mixer_in)
    done = m_z.finish(d_n1, *f_in.terms, direct=True)
    last = m_x.finish(done, direct=True)
    g0, gain_a = leave(g1, x0, r1, 0, d_n1, done, summed, late=(last, *m_z.terms))
    input_grad = ungroup(g0, nz, 1).astype(bf16).reshape(hidden_in.shape)

    def grad_of(sent, like):
        return spread(sent.land(done), nz, like.shape)

    outs = [
        grad_of(f_in, w_ffn_a_in),
        grad_of(f_out, w_ffn_a_out),
        q_in.land(done)[0].astype(f32).reshape(w_qkv.shape),
        grad_of(a_out, w_attn_out),
        grad_of(b_in, w_ffn_b_in),
        grad_of(b_out, w_ffn_b_out),
    ]
    grad_gains = jnp.stack([gain_a, gain_b, gain_c, gain_d])
    grad_gains = jnp.moveaxis(grad_gains.reshape(4, 2, nz, -1), 0, 2)
    gain_total = links.scatter_small(after(grad_gains, *outs, *m_x.terms))
    gain_total = gain_total + links.swap_core(gain_total)
    gain_total = gain_total + links.swap_x(gain_total)
    grad_out = spread(m_out.land(last), nz, w_mixer_out.shape)
    grad_z = ungroup(sum(v.astype(f32) for v in m_z.land(last)), nz, 1)
    grad_x_in = ungroup(sum(v.astype(f32) for v in m_x.land()), nz, 1)
    grad_in = jnp.stack([grad_x_in, grad_z], axis=1)
    return (block_out, input_grad, gain_total, grad_in, *grads, grad_out, *outs)


def solution(mesh):
    def body(*args):
        return per_device(mesh, *args)

    rows = P(None, ("dp", "tensor"), None)
    weight_in = P("dp", None, "tensor")
    weight_out = P(("tensor", "dp"), None)
    columns = P(None, ("tensor", "dp"))
    gains = P(None, "dp")
    weights = (
        gains, weight_in, weight_out, columns, columns, weight_out, weight_in, weight_out,
        weight_in, weight_out, weight_in, weight_out,
    )
    return jax.shard_map(
        body,
        mesh=mesh,
        in_specs=(rows, rows, P(None, "dp")) + weights,
        out_specs=(rows, rows) + weights,
        check_vma=False,
    )
```

```python
import math

import jax
import jax.numpy as jnp
from jax import lax
from jax.experimental import pallas as pl
from jax.experimental.pallas import tpu as pltpu
from jax.sharding import PartitionSpec as P

STATE = 16
CONV = 4
RANK = 96
HEAD = 128
MICRO = 2
PIECES = 4
ORDER = (0, 2, 1, 3)

f32 = jnp.float32
bf16 = jnp.bfloat16
epsilon = 1e-05
floor_score = -1e30


def dot(a, b, dims=((1,), (0,)), out=f32):
    return lax.dot_general(a, b, (dims, ((), ())), preferred_element_type=out)


def dot_tn(a, b, out=f32):
    return dot(a, b, ((0,), (0,)), out)


def dot_nt(a, b, out=f32):
    return dot(a, b, ((1,), (1,)), out)


def sigmoid(v):
    return 1.0 / (1.0 + jnp.exp(-v))


def dsilu(v):
    s = jax.nn.sigmoid(v)
    return s * (1.0 + v * (1.0 - s))


def soft_plus(v):
    return jnp.maximum(v, 0.0) + jnp.log1p(jnp.exp(-jnp.abs(v)))


def conv_fwd_kernel(slot, x_ref, mask_ref, par_ref, wx_ref, val_ref, ext_ref, prev):
    @pl.when((pl.program_id(0) == 0) & (pl.program_id(1) == 0))
    def _():
        prev[...] = jnp.zeros_like(prev)

    x = x_ref[0, 0]
    rows = x.shape[0]
    xe = jnp.concatenate([prev[...], x], axis=0)
    mask = mask_ref[0, 0]
    conv = jnp.broadcast_to(par_ref[4:5, :], x.shape)
    for k in range(CONV):
        conv = conv + par_ref[k : k + 1, :] * xe[8 - k : 8 - k + rows] * mask[:, k : k + 1]
    prev[...] = x[rows - 8 :]
    val = (conv * sigmoid(conv)).astype(bf16)
    val_ref[0, 0] = val
    ext_ref[0, 0] = dot(val, wx_ref[...]).astype(bf16)


def conv_bwd_kernel(
    slot, dext_ref, dval_ref, x_ref, xp_ref, mask_ref, par_ref, wx_ref, dx_ref, sum_ref, after
):
    @pl.when((pl.program_id(0) == 0) & (pl.program_id(1) == 0))
    def _():
        after[...] = jnp.zeros_like(after)
        sum_ref[...] = jnp.zeros_like(sum_ref)

    x = x_ref[0, 0]
    rows = x.shape[0]
    xe = jnp.concatenate([xp_ref[0, 0], x], axis=0)
    mask = mask_ref[0, 0]
    conv = jnp.broadcast_to(par_ref[4:5, :], x.shape)
    for k in range(CONV):
        conv = conv + par_ref[k : k + 1, :] * xe[8 - k : 8 - k + rows] * mask[:, k : k + 1]
    sig = sigmoid(conv)
    d_conv = (dval_ref[0, 0] + dot_nt(dext_ref[0, 0], wx_ref[...])) * (
        sig * (1.0 + conv * (1.0 - sig))
    )
    d_x = jnp.zeros_like(x)
    sums = []
    for k in range(CONV):
        held = d_conv * mask[:, k : k + 1]
        sums.append(jnp.sum(held * xe[8 - k : 8 - k + rows], axis=0, keepdims=True))
        if k == 0:
            d_x = d_x + par_ref[0:1, :] * held
        else:
            he = jnp.concatenate([held, after[k - 1]], axis=0)
            d_x = d_x + par_ref[k : k + 1, :] * he[k : k + rows]
            after[k - 1] = held[:8]
    sums.append(jnp.sum(d_conv, axis=0, keepdims=True))
    for k in range(CONV + 1):
        sum_ref[k : k + 1, :] += sums[k]
    dx_ref[0, 0] = d_x.astype(bf16)


def coefficient_rows(ext):
    both = jnp.concatenate([ext, ext], axis=0)
    return both.T[RANK:]


def scan_fwd_kernel(
    slot, ext_ref, wdt_ref, val_ref, z_ref, par_ref, rate_ref, keep_ref,
    gated_ref, scan_ref, h_ref, state, se, sv, sc,
):
    @pl.when((pl.program_id(0) == 0) & (pl.program_id(1) == 0))
    def _():
        state[...] = jnp.zeros_like(state)

    ext_low = ext_ref[0, 0]
    step = soft_plus(dot(ext_low[:, :RANK], wdt_ref[...]) + par_ref[5:6, :])
    val = val_ref[0, 0].astype(f32)
    se[...] = jnp.where(keep_ref[0, 0] > 0.0, step, 1e30)
    sv[...] = step * val
    rate = rate_ref[...]
    coef = coefficient_rows(ext_low.astype(f32))
    shape = rate.shape

    def body(g, h):
        base = pl.multiple_of(8 * g, 8)
        turned = pltpu.roll(coef, (128 - base) % 128, 1)
        se_t = se[pl.ds(base, 8), :]
        sv_t = sv[pl.ds(base, 8), :]
        for j in range(8):
            a = jnp.exp(jnp.broadcast_to(se_t[j : j + 1], shape) * rate)
            h = a * h + jnp.broadcast_to(sv_t[j : j + 1], shape) * turned[:STATE, j : j + 1]
            h_ref[0, base + j] = h.astype(bf16)
            sc[pl.ds(base + j, 1), :] = jnp.sum(
                h * turned[STATE:, j : j + 1], axis=0, keepdims=True
            )
        return h

    state[...] = lax.fori_loop(0, se.shape[0] // 8, body, state[...])
    scanned = sc[...]
    z = z_ref[0, 0]
    scan_ref[0, 0] = scanned
    gated_ref[0, 0] = ((scanned + par_ref[6:7, :] * val) * (z * sigmoid(z))).astype(bf16)


def scan_bwd_kernel(
    slot, ext_ref, wdt_ref, val_ref, z_ref, par_ref, rate_ref, keep_ref, dg_ref, scan_ref,
    h_ref, hp_ref, ddt_ref, dval_ref, dz_ref, dbc_ref, drate_ref, sum_ref,
    carry, se, st, sv, ds, r1, r2, pb, pc,
):
    @pl.when((pl.program_id(0) == 0) & (pl.program_id(1) == 0))
    def _():
        carry[...] = jnp.zeros_like(carry)
        drate_ref[...] = jnp.zeros_like(drate_ref)
        sum_ref[...] = jnp.zeros_like(sum_ref)

    ext_low = ext_ref[0, 0]
    pre = dot(ext_low[:, :RANK], wdt_ref[...]) + par_ref[5:6, :]
    step = soft_plus(pre)
    val = val_ref[0, 0].astype(f32)
    z = z_ref[0, 0]
    sig_z = sigmoid(z)
    d_gated = dg_ref[0, 0].astype(f32)
    skip = par_ref[6:7, :]
    d_scan = d_gated * (z * sig_z)
    dz_ref[0, 0] = (
        d_gated * (scan_ref[0, 0] + skip * val) * (sig_z * (1.0 + z * (1.0 - sig_z)))
    ).astype(bf16)
    se[...] = jnp.where(keep_ref[0, 0] > 0.0, step, 1e30)
    st[...] = step
    sv[...] = step * val
    ds[...] = d_scan
    rate = rate_ref[...]
    shape = rate.shape
    coef = coefficient_rows(ext_low.astype(f32))
    count = se.shape[0] // 8
    lanes = shape[1] // 128

    def fold(v):
        total = v[:, :128]
        for i in range(1, lanes):
            total = total + v[:, 128 * i : 128 * (i + 1)]
        return total

    def body(i, held):
        back, d_rate = held
        base = pl.multiple_of(8 * (count - 1 - i), 8)
        turned = pltpu.roll(coef, (128 - base) % 128, 1)
        se_t = se[pl.ds(base, 8), :]
        st_t = st[pl.ds(base, 8), :]
        sv_t = sv[pl.ds(base, 8), :]
        ds_t = ds[pl.ds(base, 8), :]
        for j in range(7, -1, -1):
            row = base + j
            h_now = h_ref[0, row].astype(f32)
            if j > 0:
                h_before = h_ref[0, row - 1].astype(f32)
            else:
                h_before = jnp.where(
                    base == 0,
                    hp_ref[0, 0].astype(f32),
                    h_ref[0, jnp.maximum(row - 1, 0)].astype(f32),
                )
            a = jnp.exp(jnp.broadcast_to(se_t[j : j + 1], shape) * rate)
            d_row = jnp.broadcast_to(ds_t[j : j + 1], shape)
            lam = d_row * turned[STATE:, j : j + 1] + back
            back = a * lam
            w = back * h_before
            d_rate = d_rate + w * jnp.broadcast_to(st_t[j : j + 1], shape)
            r1[pl.ds(row, 1), :] = jnp.sum(w * rate, axis=0, keepdims=True)
            r2[pl.ds(row, 1), :] = jnp.sum(lam * turned[:STATE, j : j + 1], axis=0, keepdims=True)
            at = pl.ds(pl.multiple_of(row * STATE, STATE), STATE)
            pb[at, :] = fold(lam * jnp.broadcast_to(sv_t[j : j + 1], shape)).astype(bf16)
            pc[at, :] = fold(d_row * h_now).astype(bf16)
        return back, d_rate

    back, d_rate = lax.fori_loop(0, count, body, (carry[...], jnp.zeros(shape, f32)))
    carry[...] = back
    drate_ref[...] += d_rate
    ones = jnp.ones((8, 128), bf16)
    dbc_ref[0, 0, 0] = dot_nt(ones, pb[...])
    dbc_ref[0, 0, 1] = dot_nt(ones, pc[...])
    d_step = r1[...] + val * r2[...]
    d_dt = d_step * sigmoid(pre)
    dval_ref[0, 0] = step * r2[...] + skip * d_scan
    ddt_ref[0, 0] = d_dt.astype(bf16)
    sum_ref[0:1, :] += jnp.sum(d_dt, axis=0, keepdims=True)
    sum_ref[1:2, :] += jnp.sum(d_scan * val, axis=0, keepdims=True)


def turn(v, cos, sin):
    return v * cos + pltpu.roll(v, HEAD // 2, 1) * sin


def attention_parts(seg_c, seg_r, pos_c, pos_r):
    return (seg_c == seg_r) & (pos_r <= pos_c)


def attn_fwd_kernel(qkv_ref, cos_ref, sin_ref, segc, segr, posc, posr, mix_ref, low_ref):
    heads = qkv_ref.shape[3] // (3 * HEAD)
    length = PIECES * qkv_ref.shape[2]
    cos = cos_ref[...].reshape(length, HEAD)
    sin = sin_ref[...].reshape(length, HEAD)
    allowed = attention_parts(segc[...].reshape(length, 1), segr[0], posc[...], posr[...])

    def take(i):
        return qkv_ref[:, 0, :, i * HEAD : (i + 1) * HEAD].reshape(length, HEAD)

    def put(ref, i, v):
        ref[:, 0, :, i * HEAD : (i + 1) * HEAD] = v.reshape(PIECES, -1, HEAD)

    for h in range(heads):
        q = turn(take(h), cos, sin).astype(bf16)
        k = turn(take(heads + h), cos, sin).astype(bf16)
        v = take(2 * heads + h).astype(bf16)
        scores = jnp.where(allowed, dot_nt(q, k) * HEAD ** (-0.5), floor_score)
        e = jnp.exp(scores - jnp.max(scores, axis=1, keepdims=True))
        probs = (e / jnp.sum(e, axis=1, keepdims=True)).astype(bf16)
        put(mix_ref, h, dot(probs, v).astype(bf16))
        put(low_ref, h, q)
        put(low_ref, heads + h, k)
        put(low_ref, 2 * heads + h, v)


def attn_bwd_kernel(low_ref, dmix_ref, cos_ref, sin_ref, segc, segr, posc, posr, dqkv_ref):
    heads = low_ref.shape[3] // (3 * HEAD)
    length = PIECES * low_ref.shape[2]
    cos = cos_ref[...].reshape(length, HEAD)
    sin = -sin_ref[...].reshape(length, HEAD)
    allowed = attention_parts(segc[...].reshape(length, 1), segr[0], posc[...], posr[...])
    scale = HEAD ** (-0.5)

    def take(ref, i):
        return ref[:, 0, :, i * HEAD : (i + 1) * HEAD].reshape(length, HEAD)

    def put(i, v):
        dqkv_ref[:, 0, :, i * HEAD : (i + 1) * HEAD] = v.astype(bf16).reshape(PIECES, -1, HEAD)

    for h in range(heads):
        q, k, v = take(low_ref, h), take(low_ref, heads + h), take(low_ref, 2 * heads + h)
        d_mix = take(dmix_ref, h)
        scores = jnp.where(allowed, dot_nt(q, k) * scale, floor_score)
        e = jnp.exp(scores - jnp.max(scores, axis=1, keepdims=True))
        probs = e / jnp.sum(e, axis=1, keepdims=True)
        d_probs = dot_nt(d_mix, v)
        d_scores = (
            probs * (d_probs - jnp.sum(probs * d_probs, axis=1, keepdims=True))
        ).astype(bf16)
        put(h, turn(dot(d_scores, k) * scale, cos, sin))
        put(heads + h, turn(dot_tn(d_scores, q) * scale, cos, sin))
        put(2 * heads + h, dot_tn(probs.astype(bf16), d_mix))


BIG = 48 * 1024 * 1024
BRIEF = pl.CostEstimate(flops=1, bytes_accessed=1, transcendentals=0)


def params(dims):
    return pltpu.CompilerParams(
        dimension_semantics=("arbitrary",) * dims, vmem_limit_bytes=BIG
    )


def rel(rows, cols, col=0):
    return pl.BlockSpec((1, 1, rows, cols), lambda m, j, s: (s[j], m, 0, col))


def rel_back(rows, cols, col=0):
    return pl.BlockSpec((1, 1, rows, cols), lambda m, j, s: (s[PIECES - 1 - j], m, 0, col))


def ordered(rows, cols):
    return pl.BlockSpec((1, 1, rows, cols), lambda m, j, s: (m, j, 0, 0))


def ordered_back(rows, cols):
    return pl.BlockSpec((1, 1, rows, cols), lambda m, j, s: (m, PIECES - 1 - j, 0, 0))


def fixed(*shape):
    return pl.BlockSpec(shape, lambda m, j, s: (0,) * len(shape))


def conv_forward(slots, pre, masks, par, wx):
    rows, width = pre.shape[2], pre.shape[3] // 2
    grid = pltpu.PrefetchScalarGridSpec(
        num_scalar_prefetch=1,
        grid=(MICRO, PIECES),
        in_specs=[rel(rows, width), ordered(rows, CONV), fixed(8, width), fixed(*wx.shape)],
        out_specs=[rel(rows, width), rel(rows, wx.shape[1])],
        scratch_shapes=[pltpu.VMEM((8, width), f32)],
    )
    return pl.pallas_call(
        conv_fwd_kernel,
        grid_spec=grid,
        out_shape=[
            jax.ShapeDtypeStruct((PIECES, MICRO, rows, width), bf16),
            jax.ShapeDtypeStruct((PIECES, MICRO, rows, wx.shape[1]), bf16),
        ],
        compiler_params=params(2),
        cost_estimate=BRIEF,
        name="conv_forward",
    )(slots, pre, masks, par, wx)


def conv_backward(slots, d_ext, d_val, pre, masks, par, wx):
    rows, width = pre.shape[2], pre.shape[3] // 2
    last = rows // 8 - 1
    grid = pltpu.PrefetchScalarGridSpec(
        num_scalar_prefetch=1,
        grid=(MICRO, PIECES),
        in_specs=[
            rel_back(rows, wx.shape[1]),
            rel_back(rows, width),
            rel_back(rows, width),
            pl.BlockSpec(
                (1, 1, 8, width),
                lambda m, j, s: (s[jnp.maximum(PIECES - 2 - j, 0)], m, last, 0),
            ),
            ordered_back(rows, CONV),
            fixed(8, width),
            fixed(*wx.shape),
        ],
        out_specs=[rel_back(rows, width), fixed(8, width)],
        scratch_shapes=[pltpu.VMEM((CONV - 1, 8, width), f32)],
    )
    return pl.pallas_call(
        conv_bwd_kernel,
        grid_spec=grid,
        out_shape=[
            jax.ShapeDtypeStruct((PIECES, MICRO, rows, width), bf16),
            jax.ShapeDtypeStruct((8, width), f32),
        ],
        compiler_params=params(2),
        cost_estimate=BRIEF,
        name="conv_backward",
    )(slots, d_ext, d_val, pre, pre, masks, par, wx)


def scan_forward(slots, ext, wdt, val, pre, par, rate, keep):
    rows, width = val.shape[2], val.shape[3]
    grid = pltpu.PrefetchScalarGridSpec(
        num_scalar_prefetch=1,
        grid=(MICRO, PIECES),
        in_specs=[
            rel(rows, ext.shape[3]), fixed(*wdt.shape), rel(rows, width), rel(rows, width, 1),
            fixed(8, width), fixed(STATE, width), ordered(rows, 1),
        ],
        out_specs=[
            rel(rows, width), rel(rows, width),
            pl.BlockSpec((1, rows, STATE, width), lambda m, j, s: (m * PIECES + j, 0, 0, 0)),
        ],
        scratch_shapes=[pltpu.VMEM((STATE, width), f32)] + [pltpu.VMEM((rows, width), f32)] * 3,
    )
    return pl.pallas_call(
        scan_fwd_kernel,
        grid_spec=grid,
        out_shape=[
            jax.ShapeDtypeStruct((PIECES, MICRO, rows, width), bf16),
            jax.ShapeDtypeStruct((PIECES, MICRO, rows, width), f32),
            jax.ShapeDtypeStruct((MICRO * PIECES, rows, STATE, width), bf16),
        ],
        compiler_params=params(2),
        cost_estimate=BRIEF,
        name="scan_forward",
    )(slots, ext, wdt, val, pre, par, rate, keep)


def scan_backward(slots, ext, wdt, val, pre, par, rate, keep, d_gated, scanned, states):
    rows, width = val.shape[2], val.shape[3]
    grid = pltpu.PrefetchScalarGridSpec(
        num_scalar_prefetch=1,
        grid=(MICRO, PIECES),
        in_specs=[
            rel_back(rows, ext.shape[3]), fixed(*wdt.shape), rel_back(rows, width),
            rel_back(rows, width, 1), fixed(8, width), fixed(STATE, width), ordered_back(rows, 1),
            rel_back(rows, width), rel_back(rows, width),
            pl.BlockSpec(
                (1, rows, STATE, width),
                lambda m, j, s: (m * PIECES + PIECES - 1 - j, 0, 0, 0),
            ),
            pl.BlockSpec(
                (1, 1, STATE, width),
                lambda m, j, s: (
                    jnp.maximum(m * PIECES + PIECES - 2 - j, 0), rows - 1, 0, 0,
                ),
            ),
        ],
        out_specs=[
            rel_back(rows, width), rel_back(rows, width), rel_back(rows, width),
            pl.BlockSpec(
                (1, 1, 2, 8, rows * STATE),
                lambda m, j, s: (s[PIECES - 1 - j], m, 0, 0, 0),
            ),
            fixed(STATE, width), fixed(8, width),
        ],
        scratch_shapes=[pltpu.VMEM((STATE, width), f32)]
        + [pltpu.VMEM((rows, width), f32)] * 6
        + [pltpu.VMEM((rows * STATE, 128), bf16)] * 2,
    )
    return pl.pallas_call(
        scan_bwd_kernel,
        grid_spec=grid,
        out_shape=[
            jax.ShapeDtypeStruct((PIECES, MICRO, rows, width), bf16),
            jax.ShapeDtypeStruct((PIECES, MICRO, rows, width), f32),
            jax.ShapeDtypeStruct((PIECES, MICRO, rows, width), bf16),
            jax.ShapeDtypeStruct((PIECES, MICRO, 2, 8, rows * STATE), f32),
            jax.ShapeDtypeStruct((STATE, width), f32),
            jax.ShapeDtypeStruct((8, width), f32),
        ],
        compiler_params=params(2),
        cost_estimate=BRIEF,
        name="scan_backward",
    )(slots, ext, wdt, val, pre, par, rate, keep, d_gated, scanned, states, states)


def attention_specs(rows, length):
    return [
        pl.BlockSpec((PIECES, rows, HEAD), lambda m: (0, 0, 0)),
        pl.BlockSpec((PIECES, rows, HEAD), lambda m: (0, 0, 0)),
        pl.BlockSpec((PIECES, 1, rows, 1), lambda m: (0, m, 0, 0)),
        pl.BlockSpec((1, 1, length), lambda m: (m, 0, 0)),
        pl.BlockSpec((length, 1), lambda m: (0, 0)),
        pl.BlockSpec((1, length), lambda m: (0, 0)),
    ]


def attention_forward(qkv, tables):
    rows, width = qkv.shape[2], qkv.shape[3]

    def whole(cols):
        return pl.BlockSpec((PIECES, 1, rows, cols), lambda m: (0, m, 0, 0))

    return pl.pallas_call(
        attn_fwd_kernel,
        grid=(MICRO,),
        in_specs=[whole(width)] + attention_specs(rows, PIECES * rows),
        out_specs=[whole(width // 3), whole(width)],
        out_shape=[
            jax.ShapeDtypeStruct((PIECES, MICRO, rows, width // 3), bf16),
            jax.ShapeDtypeStruct((PIECES, MICRO, rows, width), bf16),
        ],
        compiler_params=params(1),
        cost_estimate=BRIEF,
        name="attention_forward",
    )(qkv, *tables)


def attention_backward(low, d_mix, tables):
    rows, width = low.shape[2], low.shape[3]

    def whole(cols):
        return pl.BlockSpec((PIECES, 1, rows, cols), lambda m: (0, m, 0, 0))

    return pl.pallas_call(
        attn_bwd_kernel,
        grid=(MICRO,),
        in_specs=[whole(width), whole(width // 3)] + attention_specs(rows, PIECES * rows),
        out_specs=whole(width),
        out_shape=jax.ShapeDtypeStruct((PIECES, MICRO, rows, width), bf16),
        compiler_params=params(1),
        cost_estimate=BRIEF,
        name="attention_backward",
    )(low, d_mix, *tables)


def tile_of(n):
    return 256 if n % 256 == 0 else n


def tn_kernel(count, added, *refs):
    left, rights, adds, out = refs[0], refs[1 : 1 + count], refs[1 + count : -1], refs[-1]
    col = 0
    for i in range(count):
        width = rights[i].shape[1]
        part = dot_tn(left[...], rights[i][...])
        if added:
            part = part + adds[0][:, col : col + width].astype(f32)
        out[:, col : col + width] = part.astype(bf16)
        col += width


def product_tn(left, rights, adds=()):
    rows, m = left.shape
    tile = tile_of(m)
    width = sum(v.shape[1] for v in rights)
    whole = [pl.BlockSpec(v.shape, lambda i: (0, 0)) for v in rights]
    return pl.pallas_call(
        lambda *refs: tn_kernel(len(rights), bool(adds), *refs),
        grid=(m // tile,),
        in_specs=[pl.BlockSpec((rows, tile), lambda i: (0, i))]
        + whole
        + [pl.BlockSpec((tile, v.shape[1]), lambda i: (i, 0)) for v in adds],
        out_specs=pl.BlockSpec((tile, width), lambda i: (i, 0)),
        out_shape=jax.ShapeDtypeStruct((m, width), bf16),
        compiler_params=params(1),
        cost_estimate=BRIEF,
        name="product_tn",
    )(left, *rights, *adds)


def nt_kernel(count, steps, *refs):
    ds, ws, out = refs[:count], refs[count:-1], refs[-1]

    def part(w):
        total, col = None, 0
        for d in ds:
            width = d.shape[1]
            term = dot_nt(d[...], w[:, col : col + width])
            total = term if total is None else total + term
            col += width
        out[...] = total.astype(bf16)

    if len(ws) == 1:
        part(ws[0])
    else:
        pl.when(pl.program_id(0) < steps)(lambda: part(ws[0]))
        pl.when(pl.program_id(0) >= steps)(lambda: part(ws[1]))


def product_nt(ds, ws):
    rows = ds[0].shape[0]
    m, width = ws[0].shape
    tile = tile_of(m)
    steps = m // tile
    maps = [lambda i: (jnp.minimum(i, steps - 1), 0), lambda i: (jnp.maximum(i - steps, 0), 0)]
    return pl.pallas_call(
        lambda *refs: nt_kernel(len(ds), steps, *refs),
        grid=(steps * len(ws),),
        in_specs=[pl.BlockSpec(v.shape, lambda i: (0, 0)) for v in ds]
        + [pl.BlockSpec((tile, width), maps[j]) for j in range(len(ws))],
        out_specs=pl.BlockSpec((rows, tile), lambda i: (0, i)),
        out_shape=jax.ShapeDtypeStruct((rows, m * len(ws)), bf16),
        compiler_params=params(1),
        cost_estimate=BRIEF,
        name="product_nt",
    )(*ds, *ws)


def gate_bwd_kernel(dy, w, gate, up, d_gate, d_up):
    d_hid = dot_nt(dy[...], w[...])
    g = gate[...].astype(f32)
    sig = sigmoid(g)
    d_gate[...] = (d_hid * up[...].astype(f32) * (sig * (1.0 + g * (1.0 - sig)))).astype(bf16)
    d_up[...] = (d_hid * (g * sig)).astype(bf16)


def gate_backward(dy, w, gate, up):
    rows, units = gate.shape
    tile = tile_of(units)
    column = pl.BlockSpec((rows, tile), lambda i: (0, i))
    return pl.pallas_call(
        gate_bwd_kernel,
        grid=(units // tile,),
        in_specs=[
            pl.BlockSpec(dy.shape, lambda i: (0, 0)),
            pl.BlockSpec((tile, w.shape[1]), lambda i: (i, 0)),
            column,
            column,
        ],
        out_specs=[column, column],
        out_shape=[jax.ShapeDtypeStruct((rows, units), bf16)] * 2,
        compiler_params=params(1),
        cost_estimate=BRIEF,
        name="gate_backward",
    )(dy, w, gate, up)


def spread_kernel(nz, count, *refs):
    terms, out = refs[:-1], refs[-1]
    total = sum(v[...].astype(f32) for v in terms)
    cols = total.shape[1] // count
    u = cols // (2 * nz)
    for i in range(count):
        blocks = []
        for z in range(nz):
            for y in range(2):
                at = i * cols + (y * nz + z) * u
                blocks.append(total[:, at : at + u])
        if count == 1:
            out[...] = jnp.concatenate(blocks, axis=1)
        elif u % 128 != 0:
            out[:, i, :] = jnp.concatenate(blocks, axis=1)
        else:
            for j, block in enumerate(blocks):
                out[:, i, j * u : (j + 1) * u] = block


def spread(terms, nz, shape):
    rows, cols = terms[0].shape
    count = shape[1] if len(shape) == 3 else 1
    tile = rows // 2 if rows % 32 == 0 else rows
    block = (tile, cols) if count == 1 else (tile, count, cols // count)
    return pl.pallas_call(
        lambda *refs: spread_kernel(nz, count, *refs),
        grid=(rows // tile,),
        in_specs=[pl.BlockSpec((tile, cols), lambda i: (i, 0))] * len(terms),
        out_specs=pl.BlockSpec(block, lambda i: (i,) + (0,) * (len(block) - 1)),
        out_shape=jax.ShapeDtypeStruct(shape, f32),
        compiler_params=params(1),
        cost_estimate=BRIEF,
        name="spread",
    )(*terms)


def gate_fwd_kernel(n, own_g, own_u, other_g, other_u, gate, up, hid):
    half = n.shape[1] // 2
    g = dot(n[:, :half], own_g[...]) + dot(n[:, half:], other_g[...])
    u = dot(n[:, :half], own_u[...]) + dot(n[:, half:], other_u[...])
    gate[...] = g.astype(bf16)
    up[...] = u.astype(bf16)
    hid[...] = (g * sigmoid(g) * u).astype(bf16)


def gate_forward(n, own, other):
    rows, features = n.shape
    units = own.shape[1] // 2
    tile = tile_of(units)
    steps = units // tile
    column = pl.BlockSpec((rows, tile), lambda i: (0, i))
    w_gate = pl.BlockSpec((own.shape[0], tile), lambda i: (0, i))
    w_up = pl.BlockSpec((own.shape[0], tile), lambda i: (0, i + steps))
    return pl.pallas_call(
        gate_fwd_kernel,
        grid=(steps,),
        in_specs=[pl.BlockSpec((rows, features), lambda i: (0, 0)), w_gate, w_up, w_gate, w_up],
        out_specs=[column] * 3,
        out_shape=[jax.ShapeDtypeStruct((rows, units), bf16)] * 3,
        compiler_params=params(1),
        cost_estimate=BRIEF,
        name="gate_forward",
    )(n, own, own, other, other)


class Links:
    def __init__(self, mesh):
        self.dp = mesh.shape["dp"]
        self.nz = self.dp // 2
        self.y = lax.axis_index("dp") % 2
        self.z = lax.axis_index("dp") // 2
        self.t = lax.axis_index("tensor")
        self.groups = [[2 * z + y for z in range(self.nz)] for y in range(2)]

    def swap_y(self, v):
        return lax.ppermute(v, "dp", [(i, i ^ 1) for i in range(self.dp)])

    def shift_z(self, v, k):
        n = self.nz
        return lax.ppermute(
            v, "dp", [(2 * z + y, 2 * ((z + k) % n) + y) for z in range(n) for y in range(2)]
        )

    def swap_core(self, v):
        return lax.ppermute(v, "tensor", [(i, i ^ 1) for i in range(PIECES)])

    def swap_x(self, v):
        return lax.ppermute(v, "tensor", [(i, i ^ 2) for i in range(PIECES)])

    def gather_z(self, v):
        return lax.all_gather(v, "dp", axis=0, tiled=True, axis_index_groups=self.groups)

    def scatter_z(self, v):
        return lax.psum_scatter(
            v, "dp", scatter_dimension=0, tiled=True, axis_index_groups=self.groups
        )

    def gather_small(self, v):
        if self.dp > 8:
            both = self.by_y(v[None], self.swap_y(v)[None])
            return jnp.swapaxes(self.gather_z(both[None]), 0, 1)
        n = self.dp
        came = [v] + [
            lax.ppermute(v, "dp", [(i, (i + k) % n) for i in range(n)]) for k in range(1, n)
        ]
        ring = jnp.stack(came[:0:-1] + came[:1] + came[:0:-1])
        window = lax.dynamic_slice_in_dim(ring, n - 1 - lax.axis_index("dp"), n, 0)
        return jnp.swapaxes(window.reshape(self.nz, 2, -1), 0, 1)

    def scatter_small(self, v, order=()):
        low = v.astype(bf16)
        own = lax.dynamic_index_in_dim(v, self.y, 0, False)
        other = self.swap_y(lax.dynamic_index_in_dim(low, 1 - self.y, 0, False))
        part = after(own + other.astype(f32), *order)
        if self.nz > 4:
            return self.scatter_z(part.astype(bf16))[0].astype(f32)
        total = lax.dynamic_index_in_dim(part, self.z, 0, False)
        part_low = part.astype(bf16)
        for k in range(1, self.nz):
            piece = lax.dynamic_index_in_dim(part_low, (self.z + k) % self.nz, 0, False)
            total = total + self.shift_z(piece, k).astype(f32)
        return total

    def by_y(self, own, other, axis=0):
        return jnp.where(
            self.y == 0,
            jnp.concatenate([own, other], axis),
            jnp.concatenate([other, own], axis),
        )

    def own_first(self, v):
        half = v.shape[1] // 2
        return jnp.where(
            self.y == 0, v, jnp.concatenate([v[:, half:], v[:, :half]], axis=1)
        )

    def gather_rows(self, v):
        x = self.swap_x(v)
        core = self.swap_core(v)
        return jnp.concatenate([v, x, core, self.swap_core(x)], axis=0)

    def scatter_rows(self, part, *order):
        quarter = part.shape[0] // PIECES
        came = self.swap_core(part[2 * quarter :].astype(bf16)).astype(f32)
        x = (part[quarter : 2 * quarter].astype(f32) + came[quarter:]).astype(bf16)
        x = self.swap_x(after(x, *order))
        return part[:quarter].astype(f32) + came[:quarter] + x.astype(f32)

    def sum_rows(self, v):
        low = v.astype(bf16)
        q = low.shape[0] // PIECES
        turned = jnp.concatenate([low[2 * q :], low[: 2 * q]], axis=0)
        low = (low.astype(f32) + self.swap_core(turned).astype(f32)).astype(bf16)
        turned = jnp.concatenate([low[q : 2 * q], low[:q], low[3 * q :], low[2 * q : 3 * q]], axis=0)
        return (low.astype(f32) + self.swap_x(turned).astype(f32)).astype(bf16)

    def gather_z_direct(self, shard):
        if self.nz > 4:
            return self.gather_z(shard)
        came = [shard] + [self.shift_z(shard, k) for k in range(1, self.nz)]
        ring = jnp.concatenate(came[:0:-1] + came[:1] + came[:0:-1], axis=0)
        rows = shard.shape[0]
        return lax.dynamic_slice_in_dim(
            ring, (self.nz - 1 - self.z) * rows, self.nz * rows, 0
        )

    def scatter_z_direct(self, v):
        if self.nz > 4:
            return [self.scatter_z(v)]
        rows = v.shape[0] // self.nz
        terms = [lax.dynamic_slice_in_dim(v, self.z * rows, rows, 0)]
        for k in range(1, self.nz):
            piece = lax.dynamic_slice_in_dim(v, ((self.z + k) % self.nz) * rows, rows, 0)
            terms.append(self.shift_z(piece, k))
        return terms


class Sent:
    def __init__(self, links, left_own, left_other, rights, *order):
        self.links, self.left, self.rights = links, left_own, rights
        self.product = product_tn(left_other, rights)
        self.came = links.swap_y(after(self.product, *order))

    def finish(self, *order, direct=False, last=()):
        self.total = product_tn(self.left, self.rights, [after(self.came, *order)])
        if direct:
            self.terms = self.links.scatter_z_direct(after(self.total, *last))
        else:
            self.terms = [self.links.scatter_z(self.total)]
        return self.total

    def land(self, *order):
        return [after(v, *order) for v in self.terms]


def after(v, *order):
    if not order:
        return v
    return lax.optimization_barrier((v,) + order)[0]


def regroup(v, nz, axis):
    shape = v.shape
    u = shape[axis] // (2 * nz)
    v = v.reshape(shape[:axis] + (nz, 2, u) + shape[axis + 1 :])
    return jnp.swapaxes(v, axis, axis + 1).reshape(shape)


def ungroup(v, nz, axis):
    shape = v.shape
    u = shape[axis] // (2 * nz)
    v = v.reshape(shape[:axis] + (2, nz, u) + shape[axis + 1 :])
    return jnp.swapaxes(v, axis, axis + 1).reshape(shape)


def norm_forward(x, gain):
    r = lax.rsqrt(jnp.mean(x * x, axis=1, keepdims=True) + epsilon)
    return (x * r * gain).astype(bf16), r


def norm_backward(x, r, gain, d_n):
    u = x * r
    g = d_n * gain
    d_x = r * (g - u * jnp.mean(g * u, axis=1, keepdims=True))
    return d_x, jnp.sum(d_n * u, axis=0)


def times(x, own, other):
    half = x.shape[1] // 2
    return dot(x[:, :half], own) + dot(x[:, half:], other)


def back_times(d, own, other):
    return jnp.concatenate([dot_nt(d, own), dot_nt(d, other)], axis=1)


def ffn_forward(n, w_in):
    gate, up, hid = gate_forward(n, *w_in)
    return hid, (n, gate, up, hid)


def split_y(links, v):
    half = v.shape[1] // 2
    own = lax.dynamic_slice_in_dim(v, links.y * half, half, 1)
    other = lax.dynamic_slice_in_dim(v, (1 - links.y) * half, half, 1)
    return own, other


def ffn_backward(links, dy, kept, w_out, *order, finish=None):
    n, gate, up, hid = kept
    hid_own, hid_other = split_y(links, hid)
    sent_out = Sent(links, hid_own, hid_other, [dy], *order)
    dy = after(dy, sent_out.product)
    if finish is not None:
        dy = after(dy, finish.finish(sent_out.product))
    d_pair = gate_backward(dy, w_out, gate, up)
    half = n.shape[1] // 2
    sent_in = Sent(links, n[:, :half], n[:, half:], d_pair, sent_out.came)
    return sent_in, sent_out, [after(d_pair[0], sent_in.product), d_pair[1]]


def per_device(
    mesh,
    hidden_in, out_grad, segment_ids, norm_gains, w_mixer_in, w_xproj, w_dtproj, mixer_params,
    w_mixer_out, w_ffn_a_in, w_ffn_a_out, w_qkv, w_attn_out, w_ffn_b_in, w_ffn_b_out,
):
    links = Links(mesh)
    nz, dp, t = links.nz, links.dp, links.t
    micro, rows, features = hidden_in.shape
    local = micro * rows
    length = PIECES * rows

    small = [norm_gains, w_xproj, w_dtproj, mixer_params]
    gathered = links.gather_small(jnp.concatenate([v.reshape(-1) for v in small]))
    offset = 0
    parts = []
    for v in small:
        parts.append(gathered[:, :, offset : offset + v.size].reshape((2, nz) + v.shape))
        offset += v.size
    gains = jnp.moveaxis(parts[0], 2, 0).reshape(norm_gains.shape[0], features).astype(f32)
    wx = parts[1].reshape(-1, w_xproj.shape[1])
    wdt = jnp.moveaxis(parts[2], 2, 0).reshape(w_dtproj.shape[0], -1)
    table = jnp.moveaxis(parts[3], 2, 0).reshape(mixer_params.shape[0], -1).astype(f32)
    width = table.shape[1]
    par = jnp.concatenate([table[: CONV + 3], jnp.zeros((1, width), f32)], axis=0)
    rate = -jnp.exp(table[CONV + 3 :])

    def in_shard(w, group):
        if group:
            w = regroup(w, nz, 2)
        return w.reshape(w.shape[0], -1)

    shards = [
        in_shard(w_mixer_in, True),
        jnp.concatenate([regroup(w_mixer_out, nz, 1), regroup(w_attn_out, nz, 1)], axis=0),
        in_shard(w_ffn_a_in, True),
        regroup(w_ffn_a_out, nz, 1),
        in_shard(w_qkv, False),
        in_shard(w_ffn_b_in, True),
        regroup(w_ffn_b_out, nz, 1),
    ]
    shards[1:] = lax.optimization_barrier(shards[1:])
    own = [links.gather_z(v) for v in shards]
    other = []
    for v in own:
        other.append(links.swap_y(after(v, *other[-1:])))
    mixer_in, outs, ffn_a_in, ffn_a_out, qkv_in, ffn_b_in, ffn_b_out = zip(own, other)

    def rows_of(v, lo, hi):
        return v.reshape(nz, -1, features)[:, lo:hi].reshape(-1, features)

    cut, end = w_mixer_out.shape[0], w_mixer_out.shape[0] + w_attn_out.shape[0]
    mixer_out = links.by_y(*[rows_of(v, 0, cut) for v in outs])
    attn_out = ungroup(links.by_y(*[rows_of(v, cut, end) for v in outs]), nz, 0)
    ffn_a_out = links.by_y(*ffn_a_out)

    seg = segment_ids.reshape(micro, length)
    masks = []
    for k in range(CONV):
        earlier = jnp.pad(seg, ((0, 0), (k, 0)), constant_values=-1)[:, :length]
        masks.append((earlier == seg).astype(f32))
    masks = jnp.stack(masks, axis=-1).reshape(micro, PIECES, rows, CONV)
    keep = masks[..., 1:2]
    slots = jnp.stack([sum(i * (ORDER[i] == (j ^ t)) for i in range(PIECES)) for j in range(PIECES)])
    slots = slots.astype(jnp.int32)
    seg_pieces = seg.reshape(micro, PIECES, rows)
    seg_rel = jnp.stack(
        [lax.dynamic_index_in_dim(seg_pieces, t ^ k, 1, False) for k in ORDER]
    )
    position = jnp.concatenate([(t ^ k) * rows + lax.iota(jnp.int32, rows) for k in ORDER])
    half = HEAD // 2
    frequency = jnp.exp(lax.iota(f32, half) * (-2.0 * math.log(10000.0) / HEAD))
    angles = position.astype(f32)[:, None] * frequency[None, :]
    cos, sin = jnp.cos(angles), jnp.sin(angles)
    tables = (
        jnp.concatenate([cos, cos], axis=1).reshape(PIECES, rows, HEAD),
        jnp.concatenate([-sin, sin], axis=1).reshape(PIECES, rows, HEAD),
        seg_rel[..., None],
        jnp.swapaxes(seg_rel, 0, 1).reshape(micro, 1, length),
        position[:, None],
        position[None, :],
    )

    def pieces(v):
        return v.reshape(PIECES, micro, rows, v.shape[-1])

    def flat(v):
        return v.reshape(PIECES * local, v.shape[-1])

    def enter(x, i):
        n, r = norm_forward(x, gains[i : i + 1])
        return links.gather_rows(links.own_first(n)), r

    x0 = regroup(after(hidden_in, *shards[1:]).reshape(local, features), nz, 1).astype(f32)
    n1, r1 = enter(x0, 0)
    pre = pieces(times(n1, *mixer_in))
    values, ext_part = conv_forward(slots, pre, masks, par, wx)
    ext = pieces(links.sum_rows(flat(ext_part)))
    gated, scanned, states = scan_forward(slots, ext, wdt, values, pre, par, rate, keep)
    x1 = x0 + links.scatter_rows(dot(flat(gated), mixer_out))

    n2, r2 = enter(x1, 1)
    g4_low = regroup(out_grad.reshape(local, features), nz, 1)
    dy4 = links.gather_rows(g4_low)
    hid_a, kept_a = ffn_forward(after(n2, dy4), ffn_a_in)
    hid_a = after(hid_a, own[4])
    x2 = x1 + links.scatter_rows(dot(hid_a, ffn_a_out), other[4])

    n3, r3 = enter(x2, 2)
    mix, low = attention_forward(pieces(times(n3, *qkv_in)), tables)
    mix = after(flat(mix), other[5])
    mix_own, mix_other = split_y(links, regroup(mix, nz, 1))
    x3 = x2 + links.scatter_rows(dot(mix, attn_out), own[6])

    n4, r4 = enter(x3, 3)
    n4 = after(n4, mix_own, mix_other)
    hid_b, kept_b = ffn_forward(n4, ffn_b_in)
    hid_b = after(hid_b, other[6])
    kept_b = kept_b[:3] + (hid_b,)

    def leave(g, x, r, i, d_normed, *order, late=()):
        d_n = links.own_first(after(links.scatter_rows(d_normed, *order), *late))
        d_x, d_gain = norm_backward(x, r, gains[i : i + 1], d_n)
        return g + d_x, d_gain

    g4 = g4_low.astype(f32)
    fh = features // 2
    ffn_b_out = links.by_y(own[6], after(other[6], hid_b))
    b_in, b_out, d_pair = ffn_backward(links, dy4, kept_b, ffn_b_out)
    x4 = x3 + links.scatter_rows(dot(after(hid_b, b_in.product), ffn_b_out))
    block_out = ungroup(x4, nz, 1).astype(bf16).reshape(hidden_in.shape)
    d_n4 = product_nt(d_pair, ffn_b_in)
    g3, gain_d = leave(g4, x3, r4, 3, d_n4, b_out.came)

    dy3 = links.gather_rows(g3.astype(bf16))
    dy3 = after(dy3, b_out.finish(g3))
    a_out = Sent(links, mix_own, mix_other, [dy3], b_in.came)
    d_mix = product_nt([after(dy3, a_out.product)], [attn_out])
    d_qkv = flat(attention_backward(low, pieces(d_mix), tables))
    q_in = Sent(links, n3[:, :fh], n3[:, fh:], [d_qkv], a_out.came)
    done = b_in.finish(b_out.terms[0], q_in.product, block_out)
    d_n3 = product_nt([after(d_qkv, done, a_out.came)], qkv_in)
    g2, gain_c = leave(g3, x2, r3, 2, d_n3, a_out.finish(d_n3))

    dy2 = links.gather_rows(g2.astype(bf16))
    dy2 = after(dy2, q_in.came)
    f_in, f_out, d_pair = ffn_backward(
        links, dy2, kept_a, ffn_a_out, q_in.came, finish=q_in
    )
    d_n2 = product_nt(d_pair, ffn_a_in)
    g1, gain_b = leave(g2, x1, r2, 1, d_n2, f_out.came)

    dy1 = links.gather_rows(g1.astype(bf16))
    dy1 = after(dy1, f_out.finish(b_in.terms[0], g1))
    gated = flat(gated)
    m_out = Sent(links, *split_y(links, gated), [dy1], f_in.came)
    d_gated = pieces(product_nt([after(dy1, m_out.product)], [mixer_out]))
    d_dt, d_val, d_z, d_bc, d_rate, sums = scan_backward(
        slots, ext, wdt, values, pre, par, rate, keep, d_gated, scanned, states
    )
    d_dt, d_z = flat(d_dt), flat(d_z)
    d_dt = after(d_dt, f_in.finish(d_z, a_out.terms[0], q_in.terms[0], f_out.terms[0]))
    d_bc = d_bc[:, :, :, 0, :].reshape(PIECES, micro, 2, rows, STATE)
    d_bc = jnp.swapaxes(d_bc, 2, 3).reshape(PIECES * local, 2 * STATE)
    d_ext = links.sum_rows(jnp.concatenate([dot_nt(d_dt, wdt), d_bc], axis=1))
    d_x, conv_sums = conv_backward(slots, pieces(d_ext), d_val, pre, masks, par, wx)
    d_x = flat(d_x)
    m_in = Sent(links, n1[:, :fh], n1[:, fh:], [d_x, d_z], m_out.came)
    done = m_out.finish(m_in.product)
    d_n1 = product_nt([after(d_x, m_in.product, done), d_z], mixer_in)

    done = m_in.finish(d_n1, *f_in.terms, direct=True, last=m_out.terms)
    g0, gain_a = leave(g1, x0, r1, 0, d_n1, late=(done,))
    input_grad = ungroup(g0, nz, 1).astype(bf16).reshape(hidden_in.shape)

    grad_dt = dot_tn(d_dt, flat(ext)[:, :RANK])
    grad_x = dot_tn(flat(values), d_ext)
    grad_table = jnp.concatenate([conv_sums[: CONV + 1], sums[:2], d_rate * rate], axis=0)
    packed = jnp.concatenate([grad_x, grad_dt, grad_table.T], axis=1)
    grad_gains = jnp.stack([gain_a, gain_b, gain_c, gain_d])
    grad_gains = jnp.moveaxis(grad_gains.reshape(4, 2, nz, -1), 0, 2)
    packed = jnp.concatenate(
        [after(packed, d_n1).reshape(2, nz, -1, packed.shape[1]), grad_gains.reshape(2, nz, width // dp, -1)],
        axis=3,
    )
    summed = links.scatter_small(packed)
    states = w_xproj.shape[1]
    tail = states + RANK + mixer_params.shape[0]
    grads = [
        summed[:, :states],
        summed[:, states : states + RANK].T,
        summed[:, states + RANK : tail].T,
    ]
    gain_total = summed[:, tail:].reshape(norm_gains.shape)
    gain_total = gain_total + links.swap_core(gain_total)
    gain_total = gain_total + links.swap_x(gain_total)

    def grad_of(sent, like):
        return spread(sent.land(done), nz, like.shape)

    outs = [
        grad_of(m_out, w_mixer_out),
        grad_of(f_in, w_ffn_a_in),
        grad_of(f_out, w_ffn_a_out),
        q_in.land(done)[0].astype(f32).reshape(w_qkv.shape),
        grad_of(a_out, w_attn_out),
        grad_of(b_in, w_ffn_b_in),
        grad_of(b_out, w_ffn_b_out),
    ]
    grad_in = grad_of(m_in, w_mixer_in)
    return (block_out, input_grad, gain_total, grad_in, *grads, *outs)


def solution(mesh):
    def body(*args):
        return per_device(mesh, *args)

    rows = P(None, ("dp", "tensor"), None)
    weight_in = P("dp", None, "tensor")
    weight_out = P(("tensor", "dp"), None)
    columns = P(None, ("tensor", "dp"))
    gains = P(None, "dp")
    weights = (
        gains, weight_in, weight_out, columns, columns, weight_out, weight_in, weight_out,
        weight_in, weight_out, weight_in, weight_out,
    )
    return jax.shard_map(
        body,
        mesh=mesh,
        in_specs=(rows, rows, P(None, "dp")) + weights,
        out_specs=(rows, rows) + weights,
        check_vma=False,
    )
```

```python
import math

import jax
import jax.numpy as jnp
from jax import lax
from jax.experimental import pallas as pl
from jax.experimental.pallas import tpu as pltpu
from jax.sharding import PartitionSpec as P

STATE = 16
CONV = 4
RANK = 96
HEAD = 128
MICRO = 2
PIECES = 4
ORDER = (0, 2, 1, 3)

f32 = jnp.float32
bf16 = jnp.bfloat16
epsilon = 1e-05
floor_score = -1e30


def dot(a, b, dims=((1,), (0,)), out=f32):
    return lax.dot_general(a, b, (dims, ((), ())), preferred_element_type=out)


def dot_tn(a, b, out=f32):
    return dot(a, b, ((0,), (0,)), out)


def dot_nt(a, b, out=f32):
    return dot(a, b, ((1,), (1,)), out)


def sigmoid(v):
    return 1.0 / (1.0 + jnp.exp(-v))


def dsilu(v):
    s = jax.nn.sigmoid(v)
    return s * (1.0 + v * (1.0 - s))


def soft_plus(v):
    return jnp.maximum(v, 0.0) + jnp.log1p(jnp.exp(-jnp.abs(v)))


def conv_fwd_kernel(slot, x_ref, mask_ref, par_ref, wx_ref, val_ref, ext_ref, prev):
    @pl.when((pl.program_id(0) == 0) & (pl.program_id(1) == 0))
    def _():
        prev[...] = jnp.zeros_like(prev)

    x = x_ref[0, 0]
    rows = x.shape[0]
    xe = jnp.concatenate([prev[...], x], axis=0)
    mask = mask_ref[0, 0]
    conv = jnp.broadcast_to(par_ref[4:5, :], x.shape)
    for k in range(CONV):
        conv = conv + par_ref[k : k + 1, :] * xe[8 - k : 8 - k + rows] * mask[:, k : k + 1]
    prev[...] = x[rows - 8 :]
    val = (conv * sigmoid(conv)).astype(bf16)
    val_ref[0, 0] = val
    ext_ref[0, 0] = dot(val, wx_ref[...]).astype(bf16)


def conv_bwd_kernel(
    slot, dext_ref, dval_ref, x_ref, xp_ref, mask_ref, par_ref, wx_ref, dx_ref, sum_ref, after
):
    @pl.when((pl.program_id(0) == 0) & (pl.program_id(1) == 0))
    def _():
        after[...] = jnp.zeros_like(after)
        sum_ref[...] = jnp.zeros_like(sum_ref)

    x = x_ref[0, 0]
    rows = x.shape[0]
    xe = jnp.concatenate([xp_ref[0, 0], x], axis=0)
    mask = mask_ref[0, 0]
    conv = jnp.broadcast_to(par_ref[4:5, :], x.shape)
    for k in range(CONV):
        conv = conv + par_ref[k : k + 1, :] * xe[8 - k : 8 - k + rows] * mask[:, k : k + 1]
    sig = sigmoid(conv)
    d_conv = (dval_ref[0, 0] + dot_nt(dext_ref[0, 0], wx_ref[...])) * (
        sig * (1.0 + conv * (1.0 - sig))
    )
    d_x = jnp.zeros_like(x)
    sums = []
    for k in range(CONV):
        held = d_conv * mask[:, k : k + 1]
        sums.append(jnp.sum(held * xe[8 - k : 8 - k + rows], axis=0, keepdims=True))
        if k == 0:
            d_x = d_x + par_ref[0:1, :] * held
        else:
            he = jnp.concatenate([held, after[k - 1]], axis=0)
            d_x = d_x + par_ref[k : k + 1, :] * he[k : k + rows]
            after[k - 1] = held[:8]
    sums.append(jnp.sum(d_conv, axis=0, keepdims=True))
    for k in range(CONV + 1):
        sum_ref[k : k + 1, :] += sums[k]
    dx_ref[0, 0] = d_x.astype(bf16)


def coefficient_rows(ext):
    both = jnp.concatenate([ext, ext], axis=0)
    return both.T[RANK:]


def scan_fwd_kernel(
    slot, ext_ref, wdt_ref, val_ref, z_ref, par_ref, rate_ref, keep_ref,
    gated_ref, scan_ref, h_ref, state, se, sv, sc,
):
    @pl.when((pl.program_id(0) == 0) & (pl.program_id(1) == 0))
    def _():
        state[...] = jnp.zeros_like(state)

    ext_low = ext_ref[0, 0]
    step = soft_plus(dot(ext_low[:, :RANK], wdt_ref[...]) + par_ref[5:6, :])
    val = val_ref[0, 0].astype(f32)
    se[...] = jnp.where(keep_ref[0, 0] > 0.0, step, 1e30)
    sv[...] = step * val
    rate = rate_ref[...]
    coef = coefficient_rows(ext_low.astype(f32))
    shape = rate.shape

    def body(g, h):
        base = pl.multiple_of(8 * g, 8)
        turned = pltpu.roll(coef, (128 - base) % 128, 1)
        se_t = se[pl.ds(base, 8), :]
        sv_t = sv[pl.ds(base, 8), :]
        for j in range(8):
            a = jnp.exp(jnp.broadcast_to(se_t[j : j + 1], shape) * rate)
            h = a * h + jnp.broadcast_to(sv_t[j : j + 1], shape) * turned[:STATE, j : j + 1]
            h_ref[0, base + j] = h.astype(bf16)
            sc[pl.ds(base + j, 1), :] = jnp.sum(
                h * turned[STATE:, j : j + 1], axis=0, keepdims=True
            )
        return h

    state[...] = lax.fori_loop(0, se.shape[0] // 8, body, state[...])
    scanned = sc[...]
    z = z_ref[0, 0]
    scan_ref[0, 0] = scanned
    gated_ref[0, 0] = ((scanned + par_ref[6:7, :] * val) * (z * sigmoid(z))).astype(bf16)


def scan_bwd_kernel(
    slot, ext_ref, wdt_ref, val_ref, z_ref, par_ref, rate_ref, keep_ref, dg_ref, scan_ref,
    h_ref, hp_ref, ddt_ref, dval_ref, dz_ref, dbc_ref, drate_ref, sum_ref,
    carry, se, st, sv, ds, r1, r2, pb, pc,
):
    @pl.when((pl.program_id(0) == 0) & (pl.program_id(1) == 0))
    def _():
        carry[...] = jnp.zeros_like(carry)
        drate_ref[...] = jnp.zeros_like(drate_ref)
        sum_ref[...] = jnp.zeros_like(sum_ref)

    ext_low = ext_ref[0, 0]
    pre = dot(ext_low[:, :RANK], wdt_ref[...]) + par_ref[5:6, :]
    step = soft_plus(pre)
    val = val_ref[0, 0].astype(f32)
    z = z_ref[0, 0]
    sig_z = sigmoid(z)
    d_gated = dg_ref[0, 0].astype(f32)
    skip = par_ref[6:7, :]
    d_scan = d_gated * (z * sig_z)
    dz_ref[0, 0] = (
        d_gated * (scan_ref[0, 0] + skip * val) * (sig_z * (1.0 + z * (1.0 - sig_z)))
    ).astype(bf16)
    se[...] = jnp.where(keep_ref[0, 0] > 0.0, step, 1e30)
    st[...] = step
    sv[...] = step * val
    ds[...] = d_scan
    rate = rate_ref[...]
    shape = rate.shape
    coef = coefficient_rows(ext_low.astype(f32))
    count = se.shape[0] // 8
    lanes = shape[1] // 128

    def fold(v):
        total = v[:, :128]
        for i in range(1, lanes):
            total = total + v[:, 128 * i : 128 * (i + 1)]
        return total

    def body(i, held):
        back, d_rate = held
        base = pl.multiple_of(8 * (count - 1 - i), 8)
        turned = pltpu.roll(coef, (128 - base) % 128, 1)
        se_t = se[pl.ds(base, 8), :]
        st_t = st[pl.ds(base, 8), :]
        sv_t = sv[pl.ds(base, 8), :]
        ds_t = ds[pl.ds(base, 8), :]
        for j in range(7, -1, -1):
            row = base + j
            h_now = h_ref[0, row].astype(f32)
            if j > 0:
                h_before = h_ref[0, row - 1].astype(f32)
            else:
                h_before = jnp.where(
                    base == 0,
                    hp_ref[0, 0].astype(f32),
                    h_ref[0, jnp.maximum(row - 1, 0)].astype(f32),
                )
            a = jnp.exp(jnp.broadcast_to(se_t[j : j + 1], shape) * rate)
            d_row = jnp.broadcast_to(ds_t[j : j + 1], shape)
            lam = d_row * turned[STATE:, j : j + 1] + back
            back = a * lam
            w = back * h_before
            d_rate = d_rate + w * jnp.broadcast_to(st_t[j : j + 1], shape)
            r1[pl.ds(row, 1), :] = jnp.sum(w * rate, axis=0, keepdims=True)
            r2[pl.ds(row, 1), :] = jnp.sum(lam * turned[:STATE, j : j + 1], axis=0, keepdims=True)
            at = pl.ds(pl.multiple_of(row * STATE, STATE), STATE)
            pb[at, :] = fold(lam * jnp.broadcast_to(sv_t[j : j + 1], shape)).astype(bf16)
            pc[at, :] = fold(d_row * h_now).astype(bf16)
        return back, d_rate

    back, d_rate = lax.fori_loop(0, count, body, (carry[...], jnp.zeros(shape, f32)))
    carry[...] = back
    drate_ref[...] += d_rate
    ones = jnp.ones((8, 128), bf16)
    dbc_ref[0, 0, 0] = dot_nt(ones, pb[...])
    dbc_ref[0, 0, 1] = dot_nt(ones, pc[...])
    d_step = r1[...] + val * r2[...]
    d_dt = d_step * sigmoid(pre)
    dval_ref[0, 0] = step * r2[...] + skip * d_scan
    ddt_ref[0, 0] = d_dt.astype(bf16)
    sum_ref[0:1, :] += jnp.sum(d_dt, axis=0, keepdims=True)
    sum_ref[1:2, :] += jnp.sum(d_scan * val, axis=0, keepdims=True)


def turn(v, cos, sin):
    return v * cos + pltpu.roll(v, HEAD // 2, 1) * sin


def attention_parts(seg_c, seg_r, pos_c, pos_r):
    return (seg_c == seg_r) & (pos_r <= pos_c)


def attn_fwd_kernel(qkv_ref, cos_ref, sin_ref, segc, segr, posc, posr, mix_ref, low_ref):
    heads = qkv_ref.shape[3] // (3 * HEAD)
    length = PIECES * qkv_ref.shape[2]
    cos = cos_ref[...].reshape(length, HEAD)
    sin = sin_ref[...].reshape(length, HEAD)
    allowed = attention_parts(segc[...].reshape(length, 1), segr[0], posc[...], posr[...])

    def take(i):
        return qkv_ref[:, 0, :, i * HEAD : (i + 1) * HEAD].reshape(length, HEAD)

    def put(ref, i, v):
        ref[:, 0, :, i * HEAD : (i + 1) * HEAD] = v.reshape(PIECES, -1, HEAD)

    for h in range(heads):
        q = turn(take(h), cos, sin).astype(bf16)
        k = turn(take(heads + h), cos, sin).astype(bf16)
        v = take(2 * heads + h).astype(bf16)
        scores = jnp.where(allowed, dot_nt(q, k) * HEAD ** (-0.5), floor_score)
        e = jnp.exp(scores - jnp.max(scores, axis=1, keepdims=True))
        probs = (e / jnp.sum(e, axis=1, keepdims=True)).astype(bf16)
        put(mix_ref, h, dot(probs, v).astype(bf16))
        put(low_ref, h, q)
        put(low_ref, heads + h, k)
        put(low_ref, 2 * heads + h, v)


def attn_bwd_kernel(low_ref, dmix_ref, cos_ref, sin_ref, segc, segr, posc, posr, dqkv_ref):
    heads = low_ref.shape[3] // (3 * HEAD)
    length = PIECES * low_ref.shape[2]
    cos = cos_ref[...].reshape(length, HEAD)
    sin = -sin_ref[...].reshape(length, HEAD)
    allowed = attention_parts(segc[...].reshape(length, 1), segr[0], posc[...], posr[...])
    scale = HEAD ** (-0.5)

    def take(ref, i):
        return ref[:, 0, :, i * HEAD : (i + 1) * HEAD].reshape(length, HEAD)

    def put(i, v):
        dqkv_ref[:, 0, :, i * HEAD : (i + 1) * HEAD] = v.astype(bf16).reshape(PIECES, -1, HEAD)

    for h in range(heads):
        q, k, v = take(low_ref, h), take(low_ref, heads + h), take(low_ref, 2 * heads + h)
        d_mix = take(dmix_ref, h)
        scores = jnp.where(allowed, dot_nt(q, k) * scale, floor_score)
        e = jnp.exp(scores - jnp.max(scores, axis=1, keepdims=True))
        probs = e / jnp.sum(e, axis=1, keepdims=True)
        d_probs = dot_nt(d_mix, v)
        d_scores = (
            probs * (d_probs - jnp.sum(probs * d_probs, axis=1, keepdims=True))
        ).astype(bf16)
        put(h, turn(dot(d_scores, k) * scale, cos, sin))
        put(heads + h, turn(dot_tn(d_scores, q) * scale, cos, sin))
        put(2 * heads + h, dot_tn(probs.astype(bf16), d_mix))


BIG = 48 * 1024 * 1024
BRIEF = pl.CostEstimate(flops=1, bytes_accessed=1, transcendentals=0)


def params(dims):
    return pltpu.CompilerParams(
        dimension_semantics=("arbitrary",) * dims, vmem_limit_bytes=BIG
    )


def rel(rows, cols, col=0):
    return pl.BlockSpec((1, 1, rows, cols), lambda m, j, s: (s[j], m, 0, col))


def rel_back(rows, cols, col=0):
    return pl.BlockSpec((1, 1, rows, cols), lambda m, j, s: (s[PIECES - 1 - j], m, 0, col))


def ordered(rows, cols):
    return pl.BlockSpec((1, 1, rows, cols), lambda m, j, s: (m, j, 0, 0))


def ordered_back(rows, cols):
    return pl.BlockSpec((1, 1, rows, cols), lambda m, j, s: (m, PIECES - 1 - j, 0, 0))


def fixed(*shape):
    return pl.BlockSpec(shape, lambda m, j, s: (0,) * len(shape))


def conv_forward(slots, pre, masks, par, wx):
    rows, width = pre.shape[2], pre.shape[3] // 2
    grid = pltpu.PrefetchScalarGridSpec(
        num_scalar_prefetch=1,
        grid=(MICRO, PIECES),
        in_specs=[rel(rows, width), ordered(rows, CONV), fixed(8, width), fixed(*wx.shape)],
        out_specs=[rel(rows, width), rel(rows, wx.shape[1])],
        scratch_shapes=[pltpu.VMEM((8, width), f32)],
    )
    return pl.pallas_call(
        conv_fwd_kernel,
        grid_spec=grid,
        out_shape=[
            jax.ShapeDtypeStruct((PIECES, MICRO, rows, width), bf16),
            jax.ShapeDtypeStruct((PIECES, MICRO, rows, wx.shape[1]), bf16),
        ],
        compiler_params=params(2),
        cost_estimate=BRIEF,
        name="conv_forward",
    )(slots, pre, masks, par, wx)


def conv_backward(slots, d_ext, d_val, pre, masks, par, wx):
    rows, width = pre.shape[2], pre.shape[3] // 2
    last = rows // 8 - 1
    grid = pltpu.PrefetchScalarGridSpec(
        num_scalar_prefetch=1,
        grid=(MICRO, PIECES),
        in_specs=[
            rel_back(rows, wx.shape[1]),
            rel_back(rows, width),
            rel_back(rows, width),
            pl.BlockSpec(
                (1, 1, 8, width),
                lambda m, j, s: (s[jnp.maximum(PIECES - 2 - j, 0)], m, last, 0),
            ),
            ordered_back(rows, CONV),
            fixed(8, width),
            fixed(*wx.shape),
        ],
        out_specs=[rel_back(rows, width), fixed(8, width)],
        scratch_shapes=[pltpu.VMEM((CONV - 1, 8, width), f32)],
    )
    return pl.pallas_call(
        conv_bwd_kernel,
        grid_spec=grid,
        out_shape=[
            jax.ShapeDtypeStruct((PIECES, MICRO, rows, width), bf16),
            jax.ShapeDtypeStruct((8, width), f32),
        ],
        compiler_params=params(2),
        cost_estimate=BRIEF,
        name="conv_backward",
    )(slots, d_ext, d_val, pre, pre, masks, par, wx)


def scan_forward(slots, ext, wdt, val, pre, par, rate, keep):
    rows, width = val.shape[2], val.shape[3]
    grid = pltpu.PrefetchScalarGridSpec(
        num_scalar_prefetch=1,
        grid=(MICRO, PIECES),
        in_specs=[
            rel(rows, ext.shape[3]), fixed(*wdt.shape), rel(rows, width), rel(rows, width, 1),
            fixed(8, width), fixed(STATE, width), ordered(rows, 1),
        ],
        out_specs=[
            rel(rows, width), rel(rows, width),
            pl.BlockSpec((1, rows, STATE, width), lambda m, j, s: (m * PIECES + j, 0, 0, 0)),
        ],
        scratch_shapes=[pltpu.VMEM((STATE, width), f32)] + [pltpu.VMEM((rows, width), f32)] * 3,
    )
    return pl.pallas_call(
        scan_fwd_kernel,
        grid_spec=grid,
        out_shape=[
            jax.ShapeDtypeStruct((PIECES, MICRO, rows, width), bf16),
            jax.ShapeDtypeStruct((PIECES, MICRO, rows, width), f32),
            jax.ShapeDtypeStruct((MICRO * PIECES, rows, STATE, width), bf16),
        ],
        compiler_params=params(2),
        cost_estimate=BRIEF,
        name="scan_forward",
    )(slots, ext, wdt, val, pre, par, rate, keep)


def scan_backward(slots, ext, wdt, val, pre, par, rate, keep, d_gated, scanned, states):
    rows, width = val.shape[2], val.shape[3]
    grid = pltpu.PrefetchScalarGridSpec(
        num_scalar_prefetch=1,
        grid=(MICRO, PIECES),
        in_specs=[
            rel_back(rows, ext.shape[3]), fixed(*wdt.shape), rel_back(rows, width),
            rel_back(rows, width, 1), fixed(8, width), fixed(STATE, width), ordered_back(rows, 1),
            rel_back(rows, width), rel_back(rows, width),
            pl.BlockSpec(
                (1, rows, STATE, width),
                lambda m, j, s: (m * PIECES + PIECES - 1 - j, 0, 0, 0),
            ),
            pl.BlockSpec(
                (1, 1, STATE, width),
                lambda m, j, s: (
                    jnp.maximum(m * PIECES + PIECES - 2 - j, 0), rows - 1, 0, 0,
                ),
            ),
        ],
        out_specs=[
            rel_back(rows, width), rel_back(rows, width), rel_back(rows, width),
            pl.BlockSpec(
                (1, 1, 2, 8, rows * STATE),
                lambda m, j, s: (s[PIECES - 1 - j], m, 0, 0, 0),
            ),
            fixed(STATE, width), fixed(8, width),
        ],
        scratch_shapes=[pltpu.VMEM((STATE, width), f32)]
        + [pltpu.VMEM((rows, width), f32)] * 6
        + [pltpu.VMEM((rows * STATE, 128), bf16)] * 2,
    )
    return pl.pallas_call(
        scan_bwd_kernel,
        grid_spec=grid,
        out_shape=[
            jax.ShapeDtypeStruct((PIECES, MICRO, rows, width), bf16),
            jax.ShapeDtypeStruct((PIECES, MICRO, rows, width), f32),
            jax.ShapeDtypeStruct((PIECES, MICRO, rows, width), bf16),
            jax.ShapeDtypeStruct((PIECES, MICRO, 2, 8, rows * STATE), f32),
            jax.ShapeDtypeStruct((STATE, width), f32),
            jax.ShapeDtypeStruct((8, width), f32),
        ],
        compiler_params=params(2),
        cost_estimate=BRIEF,
        name="scan_backward",
    )(slots, ext, wdt, val, pre, par, rate, keep, d_gated, scanned, states, states)


def attention_specs(rows, length):
    return [
        pl.BlockSpec((PIECES, rows, HEAD), lambda m: (0, 0, 0)),
        pl.BlockSpec((PIECES, rows, HEAD), lambda m: (0, 0, 0)),
        pl.BlockSpec((PIECES, 1, rows, 1), lambda m: (0, m, 0, 0)),
        pl.BlockSpec((1, 1, length), lambda m: (m, 0, 0)),
        pl.BlockSpec((length, 1), lambda m: (0, 0)),
        pl.BlockSpec((1, length), lambda m: (0, 0)),
    ]


def attention_forward(qkv, tables):
    rows, width = qkv.shape[2], qkv.shape[3]

    def whole(cols):
        return pl.BlockSpec((PIECES, 1, rows, cols), lambda m: (0, m, 0, 0))

    return pl.pallas_call(
        attn_fwd_kernel,
        grid=(MICRO,),
        in_specs=[whole(width)] + attention_specs(rows, PIECES * rows),
        out_specs=[whole(width // 3), whole(width)],
        out_shape=[
            jax.ShapeDtypeStruct((PIECES, MICRO, rows, width // 3), bf16),
            jax.ShapeDtypeStruct((PIECES, MICRO, rows, width), bf16),
        ],
        compiler_params=params(1),
        cost_estimate=BRIEF,
        name="attention_forward",
    )(qkv, *tables)


def attention_backward(low, d_mix, tables):
    rows, width = low.shape[2], low.shape[3]

    def whole(cols):
        return pl.BlockSpec((PIECES, 1, rows, cols), lambda m: (0, m, 0, 0))

    return pl.pallas_call(
        attn_bwd_kernel,
        grid=(MICRO,),
        in_specs=[whole(width), whole(width // 3)] + attention_specs(rows, PIECES * rows),
        out_specs=whole(width),
        out_shape=jax.ShapeDtypeStruct((PIECES, MICRO, rows, width), bf16),
        compiler_params=params(1),
        cost_estimate=BRIEF,
        name="attention_backward",
    )(low, d_mix, *tables)


def tile_of(n):
    return 256 if n % 256 == 0 else n


def tn_kernel(count, added, *refs):
    left, rights, adds, out = refs[0], refs[1 : 1 + count], refs[1 + count : -1], refs[-1]
    col = 0
    for i in range(count):
        width = rights[i].shape[1]
        part = dot_tn(left[...], rights[i][...])
        if added:
            part = part + adds[0][:, col : col + width].astype(f32)
        out[:, col : col + width] = part.astype(bf16)
        col += width


def product_tn(left, rights, adds=()):
    rows, m = left.shape
    tile = tile_of(m)
    width = sum(v.shape[1] for v in rights)
    whole = [pl.BlockSpec(v.shape, lambda i: (0, 0)) for v in rights]
    return pl.pallas_call(
        lambda *refs: tn_kernel(len(rights), bool(adds), *refs),
        grid=(m // tile,),
        in_specs=[pl.BlockSpec((rows, tile), lambda i: (0, i))]
        + whole
        + [pl.BlockSpec((tile, v.shape[1]), lambda i: (i, 0)) for v in adds],
        out_specs=pl.BlockSpec((tile, width), lambda i: (i, 0)),
        out_shape=jax.ShapeDtypeStruct((m, width), bf16),
        compiler_params=params(1),
        cost_estimate=BRIEF,
        name="product_tn",
    )(left, *rights, *adds)


def nt_kernel(count, steps, *refs):
    ds, ws, out = refs[:count], refs[count:-1], refs[-1]

    def part(w):
        total, col = None, 0
        for d in ds:
            width = d.shape[1]
            term = dot_nt(d[...], w[:, col : col + width])
            total = term if total is None else total + term
            col += width
        out[...] = total.astype(bf16)

    if len(ws) == 1:
        part(ws[0])
    else:
        pl.when(pl.program_id(0) < steps)(lambda: part(ws[0]))
        pl.when(pl.program_id(0) >= steps)(lambda: part(ws[1]))


def product_nt(ds, ws):
    rows = ds[0].shape[0]
    m, width = ws[0].shape
    tile = tile_of(m)
    steps = m // tile
    maps = [lambda i: (jnp.minimum(i, steps - 1), 0), lambda i: (jnp.maximum(i - steps, 0), 0)]
    return pl.pallas_call(
        lambda *refs: nt_kernel(len(ds), steps, *refs),
        grid=(steps * len(ws),),
        in_specs=[pl.BlockSpec(v.shape, lambda i: (0, 0)) for v in ds]
        + [pl.BlockSpec((tile, width), maps[j]) for j in range(len(ws))],
        out_specs=pl.BlockSpec((rows, tile), lambda i: (0, i)),
        out_shape=jax.ShapeDtypeStruct((rows, m * len(ws)), bf16),
        compiler_params=params(1),
        cost_estimate=BRIEF,
        name="product_nt",
    )(*ds, *ws)


def gate_bwd_kernel(dy, w, gate, up, d_gate, d_up):
    d_hid = dot_nt(dy[...], w[...])
    g = gate[...].astype(f32)
    sig = sigmoid(g)
    d_gate[...] = (d_hid * up[...].astype(f32) * (sig * (1.0 + g * (1.0 - sig)))).astype(bf16)
    d_up[...] = (d_hid * (g * sig)).astype(bf16)


def gate_backward(dy, w, gate, up):
    rows, units = gate.shape
    tile = tile_of(units)
    column = pl.BlockSpec((rows, tile), lambda i: (0, i))
    return pl.pallas_call(
        gate_bwd_kernel,
        grid=(units // tile,),
        in_specs=[
            pl.BlockSpec(dy.shape, lambda i: (0, 0)),
            pl.BlockSpec((tile, w.shape[1]), lambda i: (i, 0)),
            column,
            column,
        ],
        out_specs=[column, column],
        out_shape=[jax.ShapeDtypeStruct((rows, units), bf16)] * 2,
        compiler_params=params(1),
        cost_estimate=BRIEF,
        name="gate_backward",
    )(dy, w, gate, up)


def spread_kernel(nz, count, *refs):
    terms, out = refs[:-1], refs[-1]
    total = sum(v[...].astype(f32) for v in terms)
    cols = total.shape[1] // count
    u = cols // (2 * nz)
    for i in range(count):
        blocks = []
        for z in range(nz):
            for y in range(2):
                at = i * cols + (y * nz + z) * u
                blocks.append(total[:, at : at + u])
        if count == 1:
            out[...] = jnp.concatenate(blocks, axis=1)
        elif u % 128 != 0:
            out[:, i, :] = jnp.concatenate(blocks, axis=1)
        else:
            for j, block in enumerate(blocks):
                out[:, i, j * u : (j + 1) * u] = block


def spread(terms, nz, shape):
    rows, cols = terms[0].shape
    count = shape[1] if len(shape) == 3 else 1
    tile = rows // 2 if rows % 32 == 0 else rows
    block = (tile, cols) if count == 1 else (tile, count, cols // count)
    return pl.pallas_call(
        lambda *refs: spread_kernel(nz, count, *refs),
        grid=(rows // tile,),
        in_specs=[pl.BlockSpec((tile, cols), lambda i: (i, 0))] * len(terms),
        out_specs=pl.BlockSpec(block, lambda i: (i,) + (0,) * (len(block) - 1)),
        out_shape=jax.ShapeDtypeStruct(shape, f32),
        compiler_params=params(1),
        cost_estimate=BRIEF,
        name="spread",
    )(*terms)


def gate_fwd_kernel(n, own_g, own_u, other_g, other_u, gate, up, hid):
    half = n.shape[1] // 2
    g = dot(n[:, :half], own_g[...]) + dot(n[:, half:], other_g[...])
    u = dot(n[:, :half], own_u[...]) + dot(n[:, half:], other_u[...])
    gate[...] = g.astype(bf16)
    up[...] = u.astype(bf16)
    hid[...] = (g * sigmoid(g) * u).astype(bf16)


def gate_forward(n, own, other):
    rows, features = n.shape
    units = own.shape[1] // 2
    tile = tile_of(units)
    steps = units // tile
    column = pl.BlockSpec((rows, tile), lambda i: (0, i))
    w_gate = pl.BlockSpec((own.shape[0], tile), lambda i: (0, i))
    w_up = pl.BlockSpec((own.shape[0], tile), lambda i: (0, i + steps))
    return pl.pallas_call(
        gate_fwd_kernel,
        grid=(steps,),
        in_specs=[pl.BlockSpec((rows, features), lambda i: (0, 0)), w_gate, w_up, w_gate, w_up],
        out_specs=[column] * 3,
        out_shape=[jax.ShapeDtypeStruct((rows, units), bf16)] * 3,
        compiler_params=params(1),
        cost_estimate=BRIEF,
        name="gate_forward",
    )(n, own, own, other, other)


class Links:
    def __init__(self, mesh):
        self.dp = mesh.shape["dp"]
        self.nz = self.dp // 2
        self.y = lax.axis_index("dp") % 2
        self.z = lax.axis_index("dp") // 2
        self.t = lax.axis_index("tensor")
        self.groups = [[2 * z + y for z in range(self.nz)] for y in range(2)]

    def swap_y(self, v):
        return lax.ppermute(v, "dp", [(i, i ^ 1) for i in range(self.dp)])

    def shift_z(self, v, k):
        n = self.nz
        return lax.ppermute(
            v, "dp", [(2 * z + y, 2 * ((z + k) % n) + y) for z in range(n) for y in range(2)]
        )

    def swap_core(self, v):
        return lax.ppermute(v, "tensor", [(i, i ^ 1) for i in range(PIECES)])

    def swap_x(self, v):
        return lax.ppermute(v, "tensor", [(i, i ^ 2) for i in range(PIECES)])

    def gather_z(self, v):
        return lax.all_gather(v, "dp", axis=0, tiled=True, axis_index_groups=self.groups)

    def scatter_z(self, v):
        return lax.psum_scatter(
            v, "dp", scatter_dimension=0, tiled=True, axis_index_groups=self.groups
        )

    def gather_small(self, v):
        if self.dp > 8:
            both = self.by_y(v[None], self.swap_y(v)[None])
            return jnp.swapaxes(self.gather_z(both[None]), 0, 1)
        n = self.dp
        came = [v] + [
            lax.ppermute(v, "dp", [(i, (i + k) % n) for i in range(n)]) for k in range(1, n)
        ]
        ring = jnp.stack(came[:0:-1] + came[:1] + came[:0:-1])
        window = lax.dynamic_slice_in_dim(ring, n - 1 - lax.axis_index("dp"), n, 0)
        return jnp.swapaxes(window.reshape(self.nz, 2, -1), 0, 1)

    def scatter_small(self, v):
        low = v.astype(bf16)
        if self.nz > 4:
            total = self.scatter_z(jnp.swapaxes(low, 0, 1))[0].astype(f32)
        else:
            total = lax.dynamic_index_in_dim(v, self.z, 1, False)
            for k in range(1, self.nz):
                piece = lax.dynamic_index_in_dim(low, (self.z + k) % self.nz, 1, False)
                total = total + self.shift_z(piece, k).astype(f32)
        other = lax.dynamic_index_in_dim(total.astype(bf16), 1 - self.y, 0, False)
        own = lax.dynamic_index_in_dim(total, self.y, 0, False)
        return own + self.swap_y(other).astype(f32)

    def by_y(self, own, other, axis=0):
        return jnp.where(
            self.y == 0,
            jnp.concatenate([own, other], axis),
            jnp.concatenate([other, own], axis),
        )

    def own_first(self, v):
        half = v.shape[1] // 2
        return jnp.where(
            self.y == 0, v, jnp.concatenate([v[:, half:], v[:, :half]], axis=1)
        )

    def gather_rows(self, v):
        x = self.swap_x(v)
        core = self.swap_core(v)
        return jnp.concatenate([v, x, core, self.swap_core(x)], axis=0)

    def scatter_rows(self, part, *order):
        quarter = part.shape[0] // PIECES
        came = self.swap_core(part[2 * quarter :].astype(bf16)).astype(f32)
        x = (part[quarter : 2 * quarter].astype(f32) + came[quarter:]).astype(bf16)
        x = self.swap_x(after(x, *order))
        return part[:quarter].astype(f32) + came[:quarter] + x.astype(f32)

    def sum_rows(self, v):
        low = v.astype(bf16)
        q = low.shape[0] // PIECES
        turned = jnp.concatenate([low[2 * q :], low[: 2 * q]], axis=0)
        low = (low.astype(f32) + self.swap_core(turned).astype(f32)).astype(bf16)
        turned = jnp.concatenate([low[q : 2 * q], low[:q], low[3 * q :], low[2 * q : 3 * q]], axis=0)
        return (low.astype(f32) + self.swap_x(turned).astype(f32)).astype(bf16)

    def gather_z_direct(self, shard):
        if self.nz > 4:
            return self.gather_z(shard)
        came = [shard] + [self.shift_z(shard, k) for k in range(1, self.nz)]
        ring = jnp.concatenate(came[:0:-1] + came[:1] + came[:0:-1], axis=0)
        rows = shard.shape[0]
        return lax.dynamic_slice_in_dim(
            ring, (self.nz - 1 - self.z) * rows, self.nz * rows, 0
        )

    def scatter_z_direct(self, v):
        if self.nz > 4:
            return [self.scatter_z(v)]
        rows = v.shape[0] // self.nz
        terms = [lax.dynamic_slice_in_dim(v, self.z * rows, rows, 0)]
        for k in range(1, self.nz):
            piece = lax.dynamic_slice_in_dim(v, ((self.z + k) % self.nz) * rows, rows, 0)
            terms.append(self.shift_z(piece, k))
        return terms


class Sent:
    def __init__(self, links, left_own, left_other, rights, *order):
        self.links, self.left, self.rights = links, left_own, rights
        self.product = product_tn(left_other, rights)
        self.came = links.swap_y(after(self.product, *order))

    def finish(self, *order, direct=False, last=()):
        self.total = product_tn(self.left, self.rights, [after(self.came, *order)])
        if direct:
            self.terms = self.links.scatter_z_direct(after(self.total, *last))
        else:
            self.terms = [self.links.scatter_z(self.total)]
        return self.total

    def land(self, *order):
        return [after(v, *order) for v in self.terms]


def after(v, *order):
    if not order:
        return v
    return lax.optimization_barrier((v,) + order)[0]


def regroup(v, nz, axis):
    shape = v.shape
    u = shape[axis] // (2 * nz)
    v = v.reshape(shape[:axis] + (nz, 2, u) + shape[axis + 1 :])
    return jnp.swapaxes(v, axis, axis + 1).reshape(shape)


def ungroup(v, nz, axis):
    shape = v.shape
    u = shape[axis] // (2 * nz)
    v = v.reshape(shape[:axis] + (2, nz, u) + shape[axis + 1 :])
    return jnp.swapaxes(v, axis, axis + 1).reshape(shape)


def norm_forward(x, gain):
    r = lax.rsqrt(jnp.mean(x * x, axis=1, keepdims=True) + epsilon)
    return (x * r * gain).astype(bf16), r


def norm_backward(x, r, gain, d_n):
    u = x * r
    g = d_n * gain
    d_x = r * (g - u * jnp.mean(g * u, axis=1, keepdims=True))
    return d_x, jnp.sum(d_n * u, axis=0)


def times(x, own, other):
    half = x.shape[1] // 2
    return dot(x[:, :half], own) + dot(x[:, half:], other)


def back_times(d, own, other):
    return jnp.concatenate([dot_nt(d, own), dot_nt(d, other)], axis=1)


def ffn_forward(n, w_in):
    gate, up, hid = gate_forward(n, *w_in)
    return hid, (n, gate, up, hid)


def split_y(links, v):
    half = v.shape[1] // 2
    own = lax.dynamic_slice_in_dim(v, links.y * half, half, 1)
    other = lax.dynamic_slice_in_dim(v, (1 - links.y) * half, half, 1)
    return own, other


def ffn_backward(links, dy, kept, w_out, *order, finish=None):
    n, gate, up, hid = kept
    hid_own, hid_other = split_y(links, hid)
    sent_out = Sent(links, hid_own, hid_other, [dy], *order)
    dy = after(dy, sent_out.product)
    if finish is not None:
        dy = after(dy, finish.finish(sent_out.product))
    d_pair = gate_backward(dy, w_out, gate, up)
    half = n.shape[1] // 2
    sent_in = Sent(links, n[:, :half], n[:, half:], d_pair, sent_out.came)
    return sent_in, sent_out, [after(d_pair[0], sent_in.product), d_pair[1]]


def per_device(
    mesh,
    hidden_in, out_grad, segment_ids, norm_gains, w_mixer_in, w_xproj, w_dtproj, mixer_params,
    w_mixer_out, w_ffn_a_in, w_ffn_a_out, w_qkv, w_attn_out, w_ffn_b_in, w_ffn_b_out,
):
    links = Links(mesh)
    nz, dp, t = links.nz, links.dp, links.t
    micro, rows, features = hidden_in.shape
    local = micro * rows
    length = PIECES * rows

    small = [norm_gains, w_xproj, w_dtproj, mixer_params]
    gathered = links.gather_small(jnp.concatenate([v.reshape(-1) for v in small]))
    offset = 0
    parts = []
    for v in small:
        parts.append(gathered[:, :, offset : offset + v.size].reshape((2, nz) + v.shape))
        offset += v.size
    gains = jnp.moveaxis(parts[0], 2, 0).reshape(norm_gains.shape[0], features).astype(f32)
    wx = parts[1].reshape(-1, w_xproj.shape[1])
    wdt = jnp.moveaxis(parts[2], 2, 0).reshape(w_dtproj.shape[0], -1)
    table = jnp.moveaxis(parts[3], 2, 0).reshape(mixer_params.shape[0], -1).astype(f32)
    width = table.shape[1]
    par = jnp.concatenate([table[: CONV + 3], jnp.zeros((1, width), f32)], axis=0)
    rate = -jnp.exp(table[CONV + 3 :])

    def in_shard(w, group):
        if group:
            w = regroup(w, nz, 2)
        return w.reshape(w.shape[0], -1)

    shards = [
        in_shard(w_mixer_in, True),
        jnp.concatenate([regroup(w_mixer_out, nz, 1), regroup(w_attn_out, nz, 1)], axis=0),
        in_shard(w_ffn_a_in, True),
        regroup(w_ffn_a_out, nz, 1),
        in_shard(w_qkv, False),
        in_shard(w_ffn_b_in, True),
        regroup(w_ffn_b_out, nz, 1),
    ]
    shards[1:] = lax.optimization_barrier(shards[1:])
    own = [links.gather_z(v) for v in shards]
    other = []
    for v in own:
        other.append(links.swap_y(after(v, *other[-1:])))
    mixer_in, outs, ffn_a_in, ffn_a_out, qkv_in, ffn_b_in, ffn_b_out = zip(own, other)

    def rows_of(v, lo, hi):
        return v.reshape(nz, -1, features)[:, lo:hi].reshape(-1, features)

    cut, end = w_mixer_out.shape[0], w_mixer_out.shape[0] + w_attn_out.shape[0]
    mixer_out = links.by_y(*[rows_of(v, 0, cut) for v in outs])
    attn_out = ungroup(links.by_y(*[rows_of(v, cut, end) for v in outs]), nz, 0)
    ffn_a_out = links.by_y(*ffn_a_out)

    seg = segment_ids.reshape(micro, length)
    masks = []
    for k in range(CONV):
        earlier = jnp.pad(seg, ((0, 0), (k, 0)), constant_values=-1)[:, :length]
        masks.append((earlier == seg).astype(f32))
    masks = jnp.stack(masks, axis=-1).reshape(micro, PIECES, rows, CONV)
    keep = masks[..., 1:2]
    slots = jnp.stack([sum(i * (ORDER[i] == (j ^ t)) for i in range(PIECES)) for j in range(PIECES)])
    slots = slots.astype(jnp.int32)
    seg_pieces = seg.reshape(micro, PIECES, rows)
    seg_rel = jnp.stack(
        [lax.dynamic_index_in_dim(seg_pieces, t ^ k, 1, False) for k in ORDER]
    )
    position = jnp.concatenate([(t ^ k) * rows + lax.iota(jnp.int32, rows) for k in ORDER])
    half = HEAD // 2
    frequency = jnp.exp(lax.iota(f32, half) * (-2.0 * math.log(10000.0) / HEAD))
    angles = position.astype(f32)[:, None] * frequency[None, :]
    cos, sin = jnp.cos(angles), jnp.sin(angles)
    tables = (
        jnp.concatenate([cos, cos], axis=1).reshape(PIECES, rows, HEAD),
        jnp.concatenate([-sin, sin], axis=1).reshape(PIECES, rows, HEAD),
        seg_rel[..., None],
        jnp.swapaxes(seg_rel, 0, 1).reshape(micro, 1, length),
        position[:, None],
        position[None, :],
    )

    def pieces(v):
        return v.reshape(PIECES, micro, rows, v.shape[-1])

    def flat(v):
        return v.reshape(PIECES * local, v.shape[-1])

    def enter(x, i):
        n, r = norm_forward(x, gains[i : i + 1])
        return links.gather_rows(links.own_first(n)), r

    x0 = regroup(after(hidden_in, *shards[1:]).reshape(local, features), nz, 1).astype(f32)
    n1, r1 = enter(x0, 0)
    pre = pieces(times(n1, *mixer_in))
    values, ext_part = conv_forward(slots, pre, masks, par, wx)
    ext = pieces(links.sum_rows(flat(ext_part)))
    gated, scanned, states = scan_forward(slots, ext, wdt, values, pre, par, rate, keep)
    x1 = x0 + links.scatter_rows(dot(flat(gated), mixer_out))

    n2, r2 = enter(x1, 1)
    g4_low = regroup(out_grad.reshape(local, features), nz, 1)
    dy4 = links.gather_rows(g4_low)
    hid_a, kept_a = ffn_forward(after(n2, dy4), ffn_a_in)
    hid_a = after(hid_a, own[4])
    x2 = x1 + links.scatter_rows(dot(hid_a, ffn_a_out), other[4])

    n3, r3 = enter(x2, 2)
    mix, low = attention_forward(pieces(times(n3, *qkv_in)), tables)
    mix = after(flat(mix), other[5])
    mix_own, mix_other = split_y(links, regroup(mix, nz, 1))
    x3 = x2 + links.scatter_rows(dot(mix, attn_out), own[6])

    n4, r4 = enter(x3, 3)
    n4 = after(n4, mix_own, mix_other)
    hid_b, kept_b = ffn_forward(n4, ffn_b_in)
    hid_b = after(hid_b, other[6])
    kept_b = kept_b[:3] + (hid_b,)

    def leave(g, x, r, i, d_normed, *order, late=()):
        d_n = links.own_first(after(links.scatter_rows(d_normed, *order), *late))
        d_x, d_gain = norm_backward(x, r, gains[i : i + 1], d_n)
        return g + d_x, d_gain

    g4 = g4_low.astype(f32)
    fh = features // 2
    ffn_b_out = links.by_y(own[6], after(other[6], hid_b))
    b_in, b_out, d_pair = ffn_backward(links, dy4, kept_b, ffn_b_out)
    x4 = x3 + links.scatter_rows(dot(after(hid_b, b_in.product), ffn_b_out))
    block_out = ungroup(x4, nz, 1).astype(bf16).reshape(hidden_in.shape)
    d_n4 = product_nt(d_pair, ffn_b_in)
    g3, gain_d = leave(g4, x3, r4, 3, d_n4, b_out.came)

    dy3 = links.gather_rows(g3.astype(bf16))
    dy3 = after(dy3, b_out.finish(g3))
    a_out = Sent(links, mix_own, mix_other, [dy3], b_in.came)
    d_mix = product_nt([after(dy3, a_out.product)], [attn_out])
    d_qkv = flat(attention_backward(low, pieces(d_mix), tables))
    q_in = Sent(links, n3[:, :fh], n3[:, fh:], [d_qkv], a_out.came)
    seen = after(b_in.came, q_in.product)[:8, :128]
    d_n3 = product_nt([after(d_qkv, q_in.product, seen + seen)], qkv_in)
    done = b_in.finish(b_out.terms[0], d_n3, block_out)
    g2, gain_c = leave(g3, x2, r3, 2, d_n3, done, a_out.came)

    dy2 = links.gather_rows(g2.astype(bf16))
    dy2 = after(dy2, a_out.finish(g2), q_in.came)
    f_in, f_out, d_pair = ffn_backward(
        links, dy2, kept_a, ffn_a_out, q_in.came, finish=q_in
    )
    d_n2 = product_nt(d_pair, ffn_a_in)
    g1, gain_b = leave(g2, x1, r2, 1, d_n2, f_out.came)

    dy1 = links.gather_rows(g1.astype(bf16))
    dy1 = after(dy1, f_out.finish(b_in.terms[0], g1))
    gated = flat(gated)
    m_out = Sent(links, *split_y(links, gated), [dy1], f_in.came)
    d_gated = pieces(product_nt([after(dy1, m_out.product)], [mixer_out]))
    d_dt, d_val, d_z, d_bc, d_rate, sums = scan_backward(
        slots, ext, wdt, values, pre, par, rate, keep, d_gated, scanned, states
    )
    d_dt, d_z = flat(d_dt), flat(d_z)
    d_dt = after(d_dt, f_in.finish(d_z, a_out.terms[0], q_in.terms[0], f_out.terms[0]))
    d_bc = d_bc[:, :, :, 0, :].reshape(PIECES, micro, 2, rows, STATE)
    d_bc = jnp.swapaxes(d_bc, 2, 3).reshape(PIECES * local, 2 * STATE)
    d_ext = links.sum_rows(jnp.concatenate([dot_nt(d_dt, wdt), d_bc], axis=1))
    d_x, conv_sums = conv_backward(slots, pieces(d_ext), d_val, pre, masks, par, wx)
    d_x = flat(d_x)
    m_in = Sent(links, n1[:, :fh], n1[:, fh:], [d_x, d_z], m_out.came)
    done = m_out.finish(m_in.product)
    d_n1 = product_nt([after(d_x, m_in.product, done), d_z], mixer_in)

    g0, gain_a = leave(g1, x0, r1, 0, d_n1, late=(m_in.came,))

    grad_dt = dot_tn(d_dt, flat(ext)[:, :RANK])
    grad_x = dot_tn(flat(values), d_ext)
    grad_table = jnp.concatenate([conv_sums[: CONV + 1], sums[:2], d_rate * rate], axis=0)
    packed = jnp.concatenate([grad_x, grad_dt, grad_table.T], axis=1)
    grad_gains = jnp.stack([gain_a, gain_b, gain_c, gain_d])
    grad_gains = jnp.moveaxis(grad_gains.reshape(4, 2, nz, -1), 0, 2)
    packed = jnp.concatenate(
        [after(packed, d_n1).reshape(2, nz, -1, packed.shape[1]), grad_gains.reshape(2, nz, width // dp, -1)],
        axis=3,
    )
    summed = links.scatter_small(packed)
    states = w_xproj.shape[1]
    tail = states + RANK + mixer_params.shape[0]
    grads = [
        summed[:, :states],
        summed[:, states : states + RANK].T,
        summed[:, states + RANK : tail].T,
    ]
    done = m_in.finish(packed, *f_in.terms, direct=True, last=m_out.terms)
    input_grad = ungroup(after(g0, done), nz, 1).astype(bf16).reshape(hidden_in.shape)
    gain_total = summed[:, tail:].reshape(norm_gains.shape)
    gain_total = gain_total + links.swap_core(gain_total)
    gain_total = gain_total + links.swap_x(gain_total)

    def grad_of(sent, like):
        return spread(sent.land(done), nz, like.shape)

    outs = [
        grad_of(m_out, w_mixer_out),
        grad_of(f_in, w_ffn_a_in),
        grad_of(f_out, w_ffn_a_out),
        q_in.land(done)[0].astype(f32).reshape(w_qkv.shape),
        grad_of(a_out, w_attn_out),
        grad_of(b_in, w_ffn_b_in),
        grad_of(b_out, w_ffn_b_out),
    ]
    grad_in = grad_of(m_in, w_mixer_in)
    return (block_out, input_grad, gain_total, grad_in, *grads, *outs)


def solution(mesh):
    def body(*args):
        return per_device(mesh, *args)

    rows = P(None, ("dp", "tensor"), None)
    weight_in = P("dp", None, "tensor")
    weight_out = P(("tensor", "dp"), None)
    columns = P(None, ("tensor", "dp"))
    gains = P(None, "dp")
    weights = (
        gains, weight_in, weight_out, columns, columns, weight_out, weight_in, weight_out,
        weight_in, weight_out, weight_in, weight_out,
    )
    return jax.shard_map(
        body,
        mesh=mesh,
        in_specs=(rows, rows, P(None, "dp")) + weights,
        out_specs=(rows, rows) + weights,
        check_vma=False,
    )
```

```python
import math

import jax
import jax.numpy as jnp
from jax import lax
from jax.experimental import pallas as pl
from jax.experimental.pallas import tpu as pltpu
from jax.sharding import PartitionSpec as P

STATE = 16
CONV = 4
RANK = 96
HEAD = 128
MICRO = 2
PIECES = 4
ORDER = (0, 2, 1, 3)

f32 = jnp.float32
bf16 = jnp.bfloat16
epsilon = 1e-05
floor_score = -1e30


def dot(a, b, dims=((1,), (0,)), out=f32):
    return lax.dot_general(a, b, (dims, ((), ())), preferred_element_type=out)


def dot_tn(a, b, out=f32):
    return dot(a, b, ((0,), (0,)), out)


def dot_nt(a, b, out=f32):
    return dot(a, b, ((1,), (1,)), out)


def sigmoid(v):
    return 1.0 / (1.0 + jnp.exp(-v))


def dsilu(v):
    s = jax.nn.sigmoid(v)
    return s * (1.0 + v * (1.0 - s))


def soft_plus(v):
    return jnp.maximum(v, 0.0) + jnp.log1p(jnp.exp(-jnp.abs(v)))


def conv_fwd_kernel(slot, x_ref, mask_ref, par_ref, wx_ref, val_ref, ext_ref, prev):
    @pl.when((pl.program_id(0) == 0) & (pl.program_id(1) == 0))
    def _():
        prev[...] = jnp.zeros_like(prev)

    x = x_ref[0, 0]
    rows = x.shape[0]
    xe = jnp.concatenate([prev[...], x], axis=0)
    mask = mask_ref[0, 0]
    conv = jnp.broadcast_to(par_ref[4:5, :], x.shape)
    for k in range(CONV):
        conv = conv + par_ref[k : k + 1, :] * xe[8 - k : 8 - k + rows] * mask[:, k : k + 1]
    prev[...] = x[rows - 8 :]
    val = (conv * sigmoid(conv)).astype(bf16)
    val_ref[0, 0] = val
    ext_ref[0, 0] = dot(val, wx_ref[...]).astype(bf16)


def conv_bwd_kernel(
    slot, dext_ref, dval_ref, x_ref, xp_ref, mask_ref, par_ref, wx_ref, dx_ref, sum_ref, after
):
    @pl.when((pl.program_id(0) == 0) & (pl.program_id(1) == 0))
    def _():
        after[...] = jnp.zeros_like(after)
        sum_ref[...] = jnp.zeros_like(sum_ref)

    x = x_ref[0, 0]
    rows = x.shape[0]
    xe = jnp.concatenate([xp_ref[0, 0], x], axis=0)
    mask = mask_ref[0, 0]
    conv = jnp.broadcast_to(par_ref[4:5, :], x.shape)
    for k in range(CONV):
        conv = conv + par_ref[k : k + 1, :] * xe[8 - k : 8 - k + rows] * mask[:, k : k + 1]
    sig = sigmoid(conv)
    d_conv = (dval_ref[0, 0] + dot_nt(dext_ref[0, 0], wx_ref[...])) * (
        sig * (1.0 + conv * (1.0 - sig))
    )
    d_x = jnp.zeros_like(x)
    sums = []
    for k in range(CONV):
        held = d_conv * mask[:, k : k + 1]
        sums.append(jnp.sum(held * xe[8 - k : 8 - k + rows], axis=0, keepdims=True))
        if k == 0:
            d_x = d_x + par_ref[0:1, :] * held
        else:
            he = jnp.concatenate([held, after[k - 1]], axis=0)
            d_x = d_x + par_ref[k : k + 1, :] * he[k : k + rows]
            after[k - 1] = held[:8]
    sums.append(jnp.sum(d_conv, axis=0, keepdims=True))
    for k in range(CONV + 1):
        sum_ref[k : k + 1, :] += sums[k]
    dx_ref[0, 0] = d_x.astype(bf16)


def coefficient_rows(ext):
    both = jnp.concatenate([ext, ext], axis=0)
    return both.T[RANK:]


def scan_fwd_kernel(
    slot, ext_ref, wdt_ref, val_ref, z_ref, par_ref, rate_ref, keep_ref,
    gated_ref, scan_ref, h_ref, state, se, sv, sc,
):
    @pl.when((pl.program_id(0) == 0) & (pl.program_id(1) == 0))
    def _():
        state[...] = jnp.zeros_like(state)

    ext_low = ext_ref[0, 0]
    step = soft_plus(dot(ext_low[:, :RANK], wdt_ref[...]) + par_ref[5:6, :])
    val = val_ref[0, 0].astype(f32)
    se[...] = jnp.where(keep_ref[0, 0] > 0.0, step, 1e30)
    sv[...] = step * val
    rate = rate_ref[...]
    coef = coefficient_rows(ext_low.astype(f32))
    shape = rate.shape

    def body(g, h):
        base = pl.multiple_of(8 * g, 8)
        turned = pltpu.roll(coef, (128 - base) % 128, 1)
        se_t = se[pl.ds(base, 8), :]
        sv_t = sv[pl.ds(base, 8), :]
        for j in range(8):
            a = jnp.exp(jnp.broadcast_to(se_t[j : j + 1], shape) * rate)
            h = a * h + jnp.broadcast_to(sv_t[j : j + 1], shape) * turned[:STATE, j : j + 1]
            h_ref[0, base + j] = h.astype(bf16)
            sc[pl.ds(base + j, 1), :] = jnp.sum(
                h * turned[STATE:, j : j + 1], axis=0, keepdims=True
            )
        return h

    state[...] = lax.fori_loop(0, se.shape[0] // 8, body, state[...])
    scanned = sc[...]
    z = z_ref[0, 0]
    scan_ref[0, 0] = scanned
    gated_ref[0, 0] = ((scanned + par_ref[6:7, :] * val) * (z * sigmoid(z))).astype(bf16)


def scan_bwd_kernel(
    slot, ext_ref, wdt_ref, val_ref, z_ref, par_ref, rate_ref, keep_ref, dg_ref, scan_ref,
    h_ref, hp_ref, ddt_ref, dval_ref, dz_ref, dbc_ref, drate_ref, sum_ref,
    carry, se, st, sv, ds, r1, r2, pb, pc,
):
    @pl.when((pl.program_id(0) == 0) & (pl.program_id(1) == 0))
    def _():
        carry[...] = jnp.zeros_like(carry)
        drate_ref[...] = jnp.zeros_like(drate_ref)
        sum_ref[...] = jnp.zeros_like(sum_ref)

    ext_low = ext_ref[0, 0]
    pre = dot(ext_low[:, :RANK], wdt_ref[...]) + par_ref[5:6, :]
    step = soft_plus(pre)
    val = val_ref[0, 0].astype(f32)
    z = z_ref[0, 0]
    sig_z = sigmoid(z)
    d_gated = dg_ref[0, 0].astype(f32)
    skip = par_ref[6:7, :]
    d_scan = d_gated * (z * sig_z)
    dz_ref[0, 0] = (
        d_gated * (scan_ref[0, 0] + skip * val) * (sig_z * (1.0 + z * (1.0 - sig_z)))
    ).astype(bf16)
    se[...] = jnp.where(keep_ref[0, 0] > 0.0, step, 1e30)
    st[...] = step
    sv[...] = step * val
    ds[...] = d_scan
    rate = rate_ref[...]
    shape = rate.shape
    coef = coefficient_rows(ext_low.astype(f32))
    count = se.shape[0] // 8
    lanes = shape[1] // 128

    def fold(v):
        total = v[:, :128]
        for i in range(1, lanes):
            total = total + v[:, 128 * i : 128 * (i + 1)]
        return total

    def body(i, held):
        back, d_rate = held
        base = pl.multiple_of(8 * (count - 1 - i), 8)
        turned = pltpu.roll(coef, (128 - base) % 128, 1)
        se_t = se[pl.ds(base, 8), :]
        st_t = st[pl.ds(base, 8), :]
        sv_t = sv[pl.ds(base, 8), :]
        ds_t = ds[pl.ds(base, 8), :]
        for j in range(7, -1, -1):
            row = base + j
            h_now = h_ref[0, row].astype(f32)
            if j > 0:
                h_before = h_ref[0, row - 1].astype(f32)
            else:
                h_before = jnp.where(
                    base == 0,
                    hp_ref[0, 0].astype(f32),
                    h_ref[0, jnp.maximum(row - 1, 0)].astype(f32),
                )
            a = jnp.exp(jnp.broadcast_to(se_t[j : j + 1], shape) * rate)
            d_row = jnp.broadcast_to(ds_t[j : j + 1], shape)
            lam = d_row * turned[STATE:, j : j + 1] + back
            back = a * lam
            w = back * h_before
            d_rate = d_rate + w * jnp.broadcast_to(st_t[j : j + 1], shape)
            r1[pl.ds(row, 1), :] = jnp.sum(w * rate, axis=0, keepdims=True)
            r2[pl.ds(row, 1), :] = jnp.sum(lam * turned[:STATE, j : j + 1], axis=0, keepdims=True)
            at = pl.ds(pl.multiple_of(row * STATE, STATE), STATE)
            pb[at, :] = fold(lam * jnp.broadcast_to(sv_t[j : j + 1], shape)).astype(bf16)
            pc[at, :] = fold(d_row * h_now).astype(bf16)
        return back, d_rate

    back, d_rate = lax.fori_loop(0, count, body, (carry[...], jnp.zeros(shape, f32)))
    carry[...] = back
    drate_ref[...] += d_rate
    ones = jnp.ones((8, 128), bf16)
    dbc_ref[0, 0, 0] = dot_nt(ones, pb[...])
    dbc_ref[0, 0, 1] = dot_nt(ones, pc[...])
    d_step = r1[...] + val * r2[...]
    d_dt = d_step * sigmoid(pre)
    dval_ref[0, 0] = step * r2[...] + skip * d_scan
    ddt_ref[0, 0] = d_dt.astype(bf16)
    sum_ref[0:1, :] += jnp.sum(d_dt, axis=0, keepdims=True)
    sum_ref[1:2, :] += jnp.sum(d_scan * val, axis=0, keepdims=True)


def turn(v, cos, sin):
    return v * cos + pltpu.roll(v, HEAD // 2, 1) * sin


def attention_parts(seg_c, seg_r, pos_c, pos_r):
    return (seg_c == seg_r) & (pos_r <= pos_c)


def attn_fwd_kernel(qkv_ref, cos_ref, sin_ref, segc, segr, posc, posr, mix_ref, low_ref):
    heads = qkv_ref.shape[3] // (3 * HEAD)
    length = PIECES * qkv_ref.shape[2]
    cos = cos_ref[...].reshape(length, HEAD)
    sin = sin_ref[...].reshape(length, HEAD)
    allowed = attention_parts(segc[...].reshape(length, 1), segr[0], posc[...], posr[...])

    def take(i):
        return qkv_ref[:, 0, :, i * HEAD : (i + 1) * HEAD].reshape(length, HEAD)

    def put(ref, i, v):
        ref[:, 0, :, i * HEAD : (i + 1) * HEAD] = v.reshape(PIECES, -1, HEAD)

    for h in range(heads):
        q = turn(take(h), cos, sin).astype(bf16)
        k = turn(take(heads + h), cos, sin).astype(bf16)
        v = take(2 * heads + h).astype(bf16)
        scores = jnp.where(allowed, dot_nt(q, k) * HEAD ** (-0.5), floor_score)
        e = jnp.exp(scores - jnp.max(scores, axis=1, keepdims=True))
        probs = (e / jnp.sum(e, axis=1, keepdims=True)).astype(bf16)
        put(mix_ref, h, dot(probs, v).astype(bf16))
        put(low_ref, h, q)
        put(low_ref, heads + h, k)
        put(low_ref, 2 * heads + h, v)


def attn_bwd_kernel(low_ref, dmix_ref, cos_ref, sin_ref, segc, segr, posc, posr, dqkv_ref):
    heads = low_ref.shape[3] // (3 * HEAD)
    length = PIECES * low_ref.shape[2]
    cos = cos_ref[...].reshape(length, HEAD)
    sin = -sin_ref[...].reshape(length, HEAD)
    allowed = attention_parts(segc[...].reshape(length, 1), segr[0], posc[...], posr[...])
    scale = HEAD ** (-0.5)

    def take(ref, i):
        return ref[:, 0, :, i * HEAD : (i + 1) * HEAD].reshape(length, HEAD)

    def put(i, v):
        dqkv_ref[:, 0, :, i * HEAD : (i + 1) * HEAD] = v.astype(bf16).reshape(PIECES, -1, HEAD)

    for h in range(heads):
        q, k, v = take(low_ref, h), take(low_ref, heads + h), take(low_ref, 2 * heads + h)
        d_mix = take(dmix_ref, h)
        scores = jnp.where(allowed, dot_nt(q, k) * scale, floor_score)
        e = jnp.exp(scores - jnp.max(scores, axis=1, keepdims=True))
        probs = e / jnp.sum(e, axis=1, keepdims=True)
        d_probs = dot_nt(d_mix, v)
        d_scores = (
            probs * (d_probs - jnp.sum(probs * d_probs, axis=1, keepdims=True))
        ).astype(bf16)
        put(h, turn(dot(d_scores, k) * scale, cos, sin))
        put(heads + h, turn(dot_tn(d_scores, q) * scale, cos, sin))
        put(2 * heads + h, dot_tn(probs.astype(bf16), d_mix))


BIG = 48 * 1024 * 1024
BRIEF = pl.CostEstimate(flops=1, bytes_accessed=1, transcendentals=0)


def params(dims):
    return pltpu.CompilerParams(
        dimension_semantics=("arbitrary",) * dims, vmem_limit_bytes=BIG
    )


def rel(rows, cols, col=0):
    return pl.BlockSpec((1, 1, rows, cols), lambda m, j, s: (s[j], m, 0, col))


def rel_back(rows, cols, col=0):
    return pl.BlockSpec((1, 1, rows, cols), lambda m, j, s: (s[PIECES - 1 - j], m, 0, col))


def ordered(rows, cols):
    return pl.BlockSpec((1, 1, rows, cols), lambda m, j, s: (m, j, 0, 0))


def ordered_back(rows, cols):
    return pl.BlockSpec((1, 1, rows, cols), lambda m, j, s: (m, PIECES - 1 - j, 0, 0))


def fixed(*shape):
    return pl.BlockSpec(shape, lambda m, j, s: (0,) * len(shape))


def conv_forward(slots, pre, masks, par, wx):
    rows, width = pre.shape[2], pre.shape[3] // 2
    grid = pltpu.PrefetchScalarGridSpec(
        num_scalar_prefetch=1,
        grid=(MICRO, PIECES),
        in_specs=[rel(rows, width), ordered(rows, CONV), fixed(8, width), fixed(*wx.shape)],
        out_specs=[rel(rows, width), rel(rows, wx.shape[1])],
        scratch_shapes=[pltpu.VMEM((8, width), f32)],
    )
    return pl.pallas_call(
        conv_fwd_kernel,
        grid_spec=grid,
        out_shape=[
            jax.ShapeDtypeStruct((PIECES, MICRO, rows, width), bf16),
            jax.ShapeDtypeStruct((PIECES, MICRO, rows, wx.shape[1]), bf16),
        ],
        compiler_params=params(2),
        cost_estimate=BRIEF,
        name="conv_forward",
    )(slots, pre, masks, par, wx)


def conv_backward(slots, d_ext, d_val, pre, masks, par, wx):
    rows, width = pre.shape[2], pre.shape[3] // 2
    last = rows // 8 - 1
    grid = pltpu.PrefetchScalarGridSpec(
        num_scalar_prefetch=1,
        grid=(MICRO, PIECES),
        in_specs=[
            rel_back(rows, wx.shape[1]),
            rel_back(rows, width),
            rel_back(rows, width),
            pl.BlockSpec(
                (1, 1, 8, width),
                lambda m, j, s: (s[jnp.maximum(PIECES - 2 - j, 0)], m, last, 0),
            ),
            ordered_back(rows, CONV),
            fixed(8, width),
            fixed(*wx.shape),
        ],
        out_specs=[rel_back(rows, width), fixed(8, width)],
        scratch_shapes=[pltpu.VMEM((CONV - 1, 8, width), f32)],
    )
    return pl.pallas_call(
        conv_bwd_kernel,
        grid_spec=grid,
        out_shape=[
            jax.ShapeDtypeStruct((PIECES, MICRO, rows, width), bf16),
            jax.ShapeDtypeStruct((8, width), f32),
        ],
        compiler_params=params(2),
        cost_estimate=BRIEF,
        name="conv_backward",
    )(slots, d_ext, d_val, pre, pre, masks, par, wx)


def scan_forward(slots, ext, wdt, val, pre, par, rate, keep):
    rows, width = val.shape[2], val.shape[3]
    grid = pltpu.PrefetchScalarGridSpec(
        num_scalar_prefetch=1,
        grid=(MICRO, PIECES),
        in_specs=[
            rel(rows, ext.shape[3]), fixed(*wdt.shape), rel(rows, width), rel(rows, width, 1),
            fixed(8, width), fixed(STATE, width), ordered(rows, 1),
        ],
        out_specs=[
            rel(rows, width), rel(rows, width),
            pl.BlockSpec((1, rows, STATE, width), lambda m, j, s: (m * PIECES + j, 0, 0, 0)),
        ],
        scratch_shapes=[pltpu.VMEM((STATE, width), f32)] + [pltpu.VMEM((rows, width), f32)] * 3,
    )
    return pl.pallas_call(
        scan_fwd_kernel,
        grid_spec=grid,
        out_shape=[
            jax.ShapeDtypeStruct((PIECES, MICRO, rows, width), bf16),
            jax.ShapeDtypeStruct((PIECES, MICRO, rows, width), f32),
            jax.ShapeDtypeStruct((MICRO * PIECES, rows, STATE, width), bf16),
        ],
        compiler_params=params(2),
        cost_estimate=BRIEF,
        name="scan_forward",
    )(slots, ext, wdt, val, pre, par, rate, keep)


def scan_backward(slots, ext, wdt, val, pre, par, rate, keep, d_gated, scanned, states):
    rows, width = val.shape[2], val.shape[3]
    grid = pltpu.PrefetchScalarGridSpec(
        num_scalar_prefetch=1,
        grid=(MICRO, PIECES),
        in_specs=[
            rel_back(rows, ext.shape[3]), fixed(*wdt.shape), rel_back(rows, width),
            rel_back(rows, width, 1), fixed(8, width), fixed(STATE, width), ordered_back(rows, 1),
            rel_back(rows, width), rel_back(rows, width),
            pl.BlockSpec(
                (1, rows, STATE, width),
                lambda m, j, s: (m * PIECES + PIECES - 1 - j, 0, 0, 0),
            ),
            pl.BlockSpec(
                (1, 1, STATE, width),
                lambda m, j, s: (
                    jnp.maximum(m * PIECES + PIECES - 2 - j, 0), rows - 1, 0, 0,
                ),
            ),
        ],
        out_specs=[
            rel_back(rows, width), rel_back(rows, width), rel_back(rows, width),
            pl.BlockSpec(
                (1, 1, 2, 8, rows * STATE),
                lambda m, j, s: (s[PIECES - 1 - j], m, 0, 0, 0),
            ),
            fixed(STATE, width), fixed(8, width),
        ],
        scratch_shapes=[pltpu.VMEM((STATE, width), f32)]
        + [pltpu.VMEM((rows, width), f32)] * 6
        + [pltpu.VMEM((rows * STATE, 128), bf16)] * 2,
    )
    return pl.pallas_call(
        scan_bwd_kernel,
        grid_spec=grid,
        out_shape=[
            jax.ShapeDtypeStruct((PIECES, MICRO, rows, width), bf16),
            jax.ShapeDtypeStruct((PIECES, MICRO, rows, width), f32),
            jax.ShapeDtypeStruct((PIECES, MICRO, rows, width), bf16),
            jax.ShapeDtypeStruct((PIECES, MICRO, 2, 8, rows * STATE), f32),
            jax.ShapeDtypeStruct((STATE, width), f32),
            jax.ShapeDtypeStruct((8, width), f32),
        ],
        compiler_params=params(2),
        cost_estimate=BRIEF,
        name="scan_backward",
    )(slots, ext, wdt, val, pre, par, rate, keep, d_gated, scanned, states, states)


def attention_specs(rows, length):
    return [
        pl.BlockSpec((PIECES, rows, HEAD), lambda m: (0, 0, 0)),
        pl.BlockSpec((PIECES, rows, HEAD), lambda m: (0, 0, 0)),
        pl.BlockSpec((PIECES, 1, rows, 1), lambda m: (0, m, 0, 0)),
        pl.BlockSpec((1, 1, length), lambda m: (m, 0, 0)),
        pl.BlockSpec((length, 1), lambda m: (0, 0)),
        pl.BlockSpec((1, length), lambda m: (0, 0)),
    ]


def attention_forward(qkv, tables):
    rows, width = qkv.shape[2], qkv.shape[3]

    def whole(cols):
        return pl.BlockSpec((PIECES, 1, rows, cols), lambda m: (0, m, 0, 0))

    return pl.pallas_call(
        attn_fwd_kernel,
        grid=(MICRO,),
        in_specs=[whole(width)] + attention_specs(rows, PIECES * rows),
        out_specs=[whole(width // 3), whole(width)],
        out_shape=[
            jax.ShapeDtypeStruct((PIECES, MICRO, rows, width // 3), bf16),
            jax.ShapeDtypeStruct((PIECES, MICRO, rows, width), bf16),
        ],
        compiler_params=params(1),
        cost_estimate=BRIEF,
        name="attention_forward",
    )(qkv, *tables)


def attention_backward(low, d_mix, tables):
    rows, width = low.shape[2], low.shape[3]

    def whole(cols):
        return pl.BlockSpec((PIECES, 1, rows, cols), lambda m: (0, m, 0, 0))

    return pl.pallas_call(
        attn_bwd_kernel,
        grid=(MICRO,),
        in_specs=[whole(width), whole(width // 3)] + attention_specs(rows, PIECES * rows),
        out_specs=whole(width),
        out_shape=jax.ShapeDtypeStruct((PIECES, MICRO, rows, width), bf16),
        compiler_params=params(1),
        cost_estimate=BRIEF,
        name="attention_backward",
    )(low, d_mix, *tables)


def tile_of(n):
    return 256 if n % 256 == 0 else n


def tn_kernel(count, added, *refs):
    left, rights, adds, out = refs[0], refs[1 : 1 + count], refs[1 + count : -1], refs[-1]
    col = 0
    for i in range(count):
        width = rights[i].shape[1]
        part = dot_tn(left[...], rights[i][...])
        if added:
            part = part + adds[0][:, col : col + width].astype(f32)
        out[:, col : col + width] = part.astype(bf16)
        col += width


def product_tn(left, rights, adds=()):
    rows, m = left.shape
    tile = tile_of(m)
    width = sum(v.shape[1] for v in rights)
    whole = [pl.BlockSpec(v.shape, lambda i: (0, 0)) for v in rights]
    return pl.pallas_call(
        lambda *refs: tn_kernel(len(rights), bool(adds), *refs),
        grid=(m // tile,),
        in_specs=[pl.BlockSpec((rows, tile), lambda i: (0, i))]
        + whole
        + [pl.BlockSpec((tile, v.shape[1]), lambda i: (i, 0)) for v in adds],
        out_specs=pl.BlockSpec((tile, width), lambda i: (i, 0)),
        out_shape=jax.ShapeDtypeStruct((m, width), bf16),
        compiler_params=params(1),
        cost_estimate=BRIEF,
        name="product_tn",
    )(left, *rights, *adds)


def nt_kernel(count, steps, *refs):
    ds, ws, out = refs[:count], refs[count:-1], refs[-1]

    def part(w):
        total, col = None, 0
        for d in ds:
            width = d.shape[1]
            term = dot_nt(d[...], w[:, col : col + width])
            total = term if total is None else total + term
            col += width
        out[...] = total.astype(bf16)

    if len(ws) == 1:
        part(ws[0])
    else:
        pl.when(pl.program_id(0) < steps)(lambda: part(ws[0]))
        pl.when(pl.program_id(0) >= steps)(lambda: part(ws[1]))


def product_nt(ds, ws):
    rows = ds[0].shape[0]
    m, width = ws[0].shape
    tile = tile_of(m)
    steps = m // tile
    maps = [lambda i: (jnp.minimum(i, steps - 1), 0), lambda i: (jnp.maximum(i - steps, 0), 0)]
    return pl.pallas_call(
        lambda *refs: nt_kernel(len(ds), steps, *refs),
        grid=(steps * len(ws),),
        in_specs=[pl.BlockSpec(v.shape, lambda i: (0, 0)) for v in ds]
        + [pl.BlockSpec((tile, width), maps[j]) for j in range(len(ws))],
        out_specs=pl.BlockSpec((rows, tile), lambda i: (0, i)),
        out_shape=jax.ShapeDtypeStruct((rows, m * len(ws)), bf16),
        compiler_params=params(1),
        cost_estimate=BRIEF,
        name="product_nt",
    )(*ds, *ws)


def gate_bwd_kernel(dy, w, gate, up, d_gate, d_up):
    d_hid = dot_nt(dy[...], w[...])
    g = gate[...].astype(f32)
    sig = sigmoid(g)
    d_gate[...] = (d_hid * up[...].astype(f32) * (sig * (1.0 + g * (1.0 - sig)))).astype(bf16)
    d_up[...] = (d_hid * (g * sig)).astype(bf16)


def gate_backward(dy, w, gate, up):
    rows, units = gate.shape
    tile = tile_of(units)
    column = pl.BlockSpec((rows, tile), lambda i: (0, i))
    return pl.pallas_call(
        gate_bwd_kernel,
        grid=(units // tile,),
        in_specs=[
            pl.BlockSpec(dy.shape, lambda i: (0, 0)),
            pl.BlockSpec((tile, w.shape[1]), lambda i: (i, 0)),
            column,
            column,
        ],
        out_specs=[column, column],
        out_shape=[jax.ShapeDtypeStruct((rows, units), bf16)] * 2,
        compiler_params=params(1),
        cost_estimate=BRIEF,
        name="gate_backward",
    )(dy, w, gate, up)


def spread_kernel(nz, count, *refs):
    terms, out = refs[:-1], refs[-1]
    total = sum(v[...].astype(f32) for v in terms)
    cols = total.shape[1] // count
    u = cols // (2 * nz)
    for i in range(count):
        blocks = []
        for z in range(nz):
            for y in range(2):
                at = i * cols + (y * nz + z) * u
                blocks.append(total[:, at : at + u])
        if count == 1:
            out[...] = jnp.concatenate(blocks, axis=1)
        elif u % 128 != 0:
            out[:, i, :] = jnp.concatenate(blocks, axis=1)
        else:
            for j, block in enumerate(blocks):
                out[:, i, j * u : (j + 1) * u] = block


def spread(terms, nz, shape):
    rows, cols = terms[0].shape
    count = shape[1] if len(shape) == 3 else 1
    tile = rows // 2 if rows % 32 == 0 else rows
    block = (tile, cols) if count == 1 else (tile, count, cols // count)
    return pl.pallas_call(
        lambda *refs: spread_kernel(nz, count, *refs),
        grid=(rows // tile,),
        in_specs=[pl.BlockSpec((tile, cols), lambda i: (i, 0))] * len(terms),
        out_specs=pl.BlockSpec(block, lambda i: (i,) + (0,) * (len(block) - 1)),
        out_shape=jax.ShapeDtypeStruct(shape, f32),
        compiler_params=params(1),
        cost_estimate=BRIEF,
        name="spread",
    )(*terms)


def gate_fwd_kernel(n, own_g, own_u, other_g, other_u, gate, up, hid):
    half = n.shape[1] // 2
    g = dot(n[:, :half], own_g[...]) + dot(n[:, half:], other_g[...])
    u = dot(n[:, :half], own_u[...]) + dot(n[:, half:], other_u[...])
    gate[...] = g.astype(bf16)
    up[...] = u.astype(bf16)
    hid[...] = (g * sigmoid(g) * u).astype(bf16)


def gate_forward(n, own, other):
    rows, features = n.shape
    units = own.shape[1] // 2
    tile = tile_of(units)
    steps = units // tile
    column = pl.BlockSpec((rows, tile), lambda i: (0, i))
    w_gate = pl.BlockSpec((own.shape[0], tile), lambda i: (0, i))
    w_up = pl.BlockSpec((own.shape[0], tile), lambda i: (0, i + steps))
    return pl.pallas_call(
        gate_fwd_kernel,
        grid=(steps,),
        in_specs=[pl.BlockSpec((rows, features), lambda i: (0, 0)), w_gate, w_up, w_gate, w_up],
        out_specs=[column] * 3,
        out_shape=[jax.ShapeDtypeStruct((rows, units), bf16)] * 3,
        compiler_params=params(1),
        cost_estimate=BRIEF,
        name="gate_forward",
    )(n, own, own, other, other)


class Links:
    def __init__(self, mesh):
        self.dp = mesh.shape["dp"]
        self.nz = self.dp // 2
        self.y = lax.axis_index("dp") % 2
        self.z = lax.axis_index("dp") // 2
        self.t = lax.axis_index("tensor")
        self.groups = [[2 * z + y for z in range(self.nz)] for y in range(2)]

    def swap_y(self, v):
        return lax.ppermute(v, "dp", [(i, i ^ 1) for i in range(self.dp)])

    def shift_z(self, v, k):
        n = self.nz
        return lax.ppermute(
            v, "dp", [(2 * z + y, 2 * ((z + k) % n) + y) for z in range(n) for y in range(2)]
        )

    def swap_core(self, v):
        return lax.ppermute(v, "tensor", [(i, i ^ 1) for i in range(PIECES)])

    def swap_x(self, v):
        return lax.ppermute(v, "tensor", [(i, i ^ 2) for i in range(PIECES)])

    def gather_z(self, v):
        return lax.all_gather(v, "dp", axis=0, tiled=True, axis_index_groups=self.groups)

    def scatter_z(self, v):
        return lax.psum_scatter(
            v, "dp", scatter_dimension=0, tiled=True, axis_index_groups=self.groups
        )

    def gather_small(self, v):
        if self.dp > 8:
            both = self.by_y(v[None], self.swap_y(v)[None])
            return jnp.swapaxes(self.gather_z(both[None]), 0, 1)
        n = self.dp
        came = [v] + [
            lax.ppermute(v, "dp", [(i, (i + k) % n) for i in range(n)]) for k in range(1, n)
        ]
        ring = jnp.stack(came[:0:-1] + came[:1] + came[:0:-1])
        window = lax.dynamic_slice_in_dim(ring, n - 1 - lax.axis_index("dp"), n, 0)
        return jnp.swapaxes(window.reshape(self.nz, 2, -1), 0, 1)

    def scatter_small(self, v):
        low = v.astype(bf16)
        if self.nz > 4:
            total = self.scatter_z(jnp.swapaxes(low, 0, 1))[0].astype(f32)
        else:
            total = lax.dynamic_index_in_dim(v, self.z, 1, False)
            for k in range(1, self.nz):
                piece = lax.dynamic_index_in_dim(low, (self.z + k) % self.nz, 1, False)
                total = total + self.shift_z(piece, k).astype(f32)
        other = lax.dynamic_index_in_dim(total.astype(bf16), 1 - self.y, 0, False)
        own = lax.dynamic_index_in_dim(total, self.y, 0, False)
        return own + self.swap_y(other).astype(f32)

    def by_y(self, own, other, axis=0):
        return jnp.where(
            self.y == 0,
            jnp.concatenate([own, other], axis),
            jnp.concatenate([other, own], axis),
        )

    def own_first(self, v):
        half = v.shape[1] // 2
        return jnp.where(
            self.y == 0, v, jnp.concatenate([v[:, half:], v[:, :half]], axis=1)
        )

    def gather_rows(self, v):
        x = self.swap_x(v)
        core = self.swap_core(v)
        return jnp.concatenate([v, x, core, self.swap_core(x)], axis=0)

    def scatter_rows(self, part, *order):
        quarter = part.shape[0] // PIECES
        came = self.swap_core(part[2 * quarter :].astype(bf16)).astype(f32)
        x = (part[quarter : 2 * quarter].astype(f32) + came[quarter:]).astype(bf16)
        x = self.swap_x(after(x, *order))
        return part[:quarter].astype(f32) + came[:quarter] + x.astype(f32)

    def sum_rows(self, v):
        low = v.astype(bf16)
        q = low.shape[0] // PIECES
        turned = jnp.concatenate([low[2 * q :], low[: 2 * q]], axis=0)
        low = (low.astype(f32) + self.swap_core(turned).astype(f32)).astype(bf16)
        turned = jnp.concatenate([low[q : 2 * q], low[:q], low[3 * q :], low[2 * q : 3 * q]], axis=0)
        return (low.astype(f32) + self.swap_x(turned).astype(f32)).astype(bf16)

    def gather_z_direct(self, shard):
        if self.nz > 4:
            return self.gather_z(shard)
        came = [shard] + [self.shift_z(shard, k) for k in range(1, self.nz)]
        ring = jnp.concatenate(came[:0:-1] + came[:1] + came[:0:-1], axis=0)
        rows = shard.shape[0]
        return lax.dynamic_slice_in_dim(
            ring, (self.nz - 1 - self.z) * rows, self.nz * rows, 0
        )

    def scatter_z_direct(self, v):
        if self.nz > 4:
            return [self.scatter_z(v)]
        rows = v.shape[0] // self.nz
        terms = [lax.dynamic_slice_in_dim(v, self.z * rows, rows, 0)]
        for k in range(1, self.nz):
            piece = lax.dynamic_slice_in_dim(v, ((self.z + k) % self.nz) * rows, rows, 0)
            terms.append(self.shift_z(piece, k))
        return terms


class Sent:
    def __init__(self, links, left_own, left_other, rights, *order):
        self.links, self.left, self.rights = links, left_own, rights
        self.product = product_tn(left_other, rights)
        self.came = links.swap_y(after(self.product, *order))

    def finish(self, *order, direct=False, last=()):
        self.total = product_tn(self.left, self.rights, [after(self.came, *order)])
        if direct:
            self.terms = self.links.scatter_z_direct(after(self.total, *last))
        else:
            self.terms = [self.links.scatter_z(self.total)]
        return self.total

    def land(self, *order):
        return [after(v, *order) for v in self.terms]


def after(v, *order):
    if not order:
        return v
    return lax.optimization_barrier((v,) + order)[0]


def regroup(v, nz, axis):
    shape = v.shape
    u = shape[axis] // (2 * nz)
    v = v.reshape(shape[:axis] + (nz, 2, u) + shape[axis + 1 :])
    return jnp.swapaxes(v, axis, axis + 1).reshape(shape)


def ungroup(v, nz, axis):
    shape = v.shape
    u = shape[axis] // (2 * nz)
    v = v.reshape(shape[:axis] + (2, nz, u) + shape[axis + 1 :])
    return jnp.swapaxes(v, axis, axis + 1).reshape(shape)


def norm_forward(x, gain):
    r = lax.rsqrt(jnp.mean(x * x, axis=1, keepdims=True) + epsilon)
    return (x * r * gain).astype(bf16), r


def norm_backward(x, r, gain, d_n):
    u = x * r
    g = d_n * gain
    d_x = r * (g - u * jnp.mean(g * u, axis=1, keepdims=True))
    return d_x, jnp.sum(d_n * u, axis=0)


def times(x, own, other):
    half = x.shape[1] // 2
    return dot(x[:, :half], own) + dot(x[:, half:], other)


def back_times(d, own, other):
    return jnp.concatenate([dot_nt(d, own), dot_nt(d, other)], axis=1)


def ffn_forward(n, w_in):
    gate, up, hid = gate_forward(n, *w_in)
    return hid, (n, gate, up, hid)


def split_y(links, v):
    half = v.shape[1] // 2
    own = lax.dynamic_slice_in_dim(v, links.y * half, half, 1)
    other = lax.dynamic_slice_in_dim(v, (1 - links.y) * half, half, 1)
    return own, other


def ffn_backward(links, dy, kept, w_out, *order, finish=None):
    n, gate, up, hid = kept
    hid_own, hid_other = split_y(links, hid)
    sent_out = Sent(links, hid_own, hid_other, [dy], *order)
    dy = after(dy, sent_out.product)
    if finish is not None:
        dy = after(dy, finish.finish(sent_out.product))
    d_pair = gate_backward(dy, w_out, gate, up)
    half = n.shape[1] // 2
    sent_in = Sent(links, n[:, :half], n[:, half:], d_pair, sent_out.came)
    return sent_in, sent_out, [after(d_pair[0], sent_in.product), d_pair[1]]


def per_device(
    mesh,
    hidden_in, out_grad, segment_ids, norm_gains, w_mixer_in, w_xproj, w_dtproj, mixer_params,
    w_mixer_out, w_ffn_a_in, w_ffn_a_out, w_qkv, w_attn_out, w_ffn_b_in, w_ffn_b_out,
):
    links = Links(mesh)
    nz, dp, t = links.nz, links.dp, links.t
    micro, rows, features = hidden_in.shape
    local = micro * rows
    length = PIECES * rows

    small = [norm_gains, w_xproj, w_dtproj, mixer_params]
    gathered = links.gather_small(jnp.concatenate([v.reshape(-1) for v in small]))
    offset = 0
    parts = []
    for v in small:
        parts.append(gathered[:, :, offset : offset + v.size].reshape((2, nz) + v.shape))
        offset += v.size
    gains = jnp.moveaxis(parts[0], 2, 0).reshape(norm_gains.shape[0], features).astype(f32)
    wx = parts[1].reshape(-1, w_xproj.shape[1])
    wdt = jnp.moveaxis(parts[2], 2, 0).reshape(w_dtproj.shape[0], -1)
    table = jnp.moveaxis(parts[3], 2, 0).reshape(mixer_params.shape[0], -1).astype(f32)
    width = table.shape[1]
    par = jnp.concatenate([table[: CONV + 3], jnp.zeros((1, width), f32)], axis=0)
    rate = -jnp.exp(table[CONV + 3 :])

    def in_shard(w, group):
        if group:
            w = regroup(w, nz, 2)
        return w.reshape(w.shape[0], -1)

    shards = [
        in_shard(w_mixer_in, True),
        jnp.concatenate([regroup(w_mixer_out, nz, 1), regroup(w_attn_out, nz, 1)], axis=0),
        in_shard(w_ffn_a_in, True),
        regroup(w_ffn_a_out, nz, 1),
        in_shard(w_qkv, False),
        in_shard(w_ffn_b_in, True),
        regroup(w_ffn_b_out, nz, 1),
    ]
    shards[1:] = lax.optimization_barrier(shards[1:])
    own = [links.gather_z(v) for v in shards]
    other = []
    for v in own:
        other.append(links.swap_y(after(v, *other[-1:])))
    mixer_in, outs, ffn_a_in, ffn_a_out, qkv_in, ffn_b_in, ffn_b_out = zip(own, other)

    def rows_of(v, lo, hi):
        return v.reshape(nz, -1, features)[:, lo:hi].reshape(-1, features)

    cut, end = w_mixer_out.shape[0], w_mixer_out.shape[0] + w_attn_out.shape[0]
    mixer_out = links.by_y(*[rows_of(v, 0, cut) for v in outs])
    attn_out = ungroup(links.by_y(*[rows_of(v, cut, end) for v in outs]), nz, 0)
    ffn_a_out = links.by_y(*ffn_a_out)

    seg = segment_ids.reshape(micro, length)
    masks = []
    for k in range(CONV):
        earlier = jnp.pad(seg, ((0, 0), (k, 0)), constant_values=-1)[:, :length]
        masks.append((earlier == seg).astype(f32))
    masks = jnp.stack(masks, axis=-1).reshape(micro, PIECES, rows, CONV)
    keep = masks[..., 1:2]
    slots = jnp.stack([sum(i * (ORDER[i] == (j ^ t)) for i in range(PIECES)) for j in range(PIECES)])
    slots = slots.astype(jnp.int32)
    seg_pieces = seg.reshape(micro, PIECES, rows)
    seg_rel = jnp.stack(
        [lax.dynamic_index_in_dim(seg_pieces, t ^ k, 1, False) for k in ORDER]
    )
    position = jnp.concatenate([(t ^ k) * rows + lax.iota(jnp.int32, rows) for k in ORDER])
    half = HEAD // 2
    frequency = jnp.exp(lax.iota(f32, half) * (-2.0 * math.log(10000.0) / HEAD))
    angles = position.astype(f32)[:, None] * frequency[None, :]
    cos, sin = jnp.cos(angles), jnp.sin(angles)
    tables = (
        jnp.concatenate([cos, cos], axis=1).reshape(PIECES, rows, HEAD),
        jnp.concatenate([-sin, sin], axis=1).reshape(PIECES, rows, HEAD),
        seg_rel[..., None],
        jnp.swapaxes(seg_rel, 0, 1).reshape(micro, 1, length),
        position[:, None],
        position[None, :],
    )

    def pieces(v):
        return v.reshape(PIECES, micro, rows, v.shape[-1])

    def flat(v):
        return v.reshape(PIECES * local, v.shape[-1])

    def enter(x, i):
        n, r = norm_forward(x, gains[i : i + 1])
        return links.gather_rows(links.own_first(n)), r

    x0 = regroup(after(hidden_in, *shards[1:]).reshape(local, features), nz, 1).astype(f32)
    n1, r1 = enter(x0, 0)
    pre = pieces(times(n1, *mixer_in))
    values, ext_part = conv_forward(slots, pre, masks, par, wx)
    ext = pieces(links.sum_rows(flat(ext_part)))
    gated, scanned, states = scan_forward(slots, ext, wdt, values, pre, par, rate, keep)
    x1 = x0 + links.scatter_rows(dot(flat(gated), mixer_out))

    n2, r2 = enter(x1, 1)
    g4_low = regroup(out_grad.reshape(local, features), nz, 1)
    dy4 = links.gather_rows(g4_low)
    hid_a, kept_a = ffn_forward(after(n2, dy4), ffn_a_in)
    hid_a = after(hid_a, own[4])
    x2 = x1 + links.scatter_rows(dot(hid_a, ffn_a_out), other[4])

    n3, r3 = enter(x2, 2)
    mix, low = attention_forward(pieces(times(n3, *qkv_in)), tables)
    mix = after(flat(mix), other[5])
    mix_own, mix_other = split_y(links, regroup(mix, nz, 1))
    x3 = x2 + links.scatter_rows(dot(mix, attn_out), own[6])

    n4, r4 = enter(x3, 3)
    n4 = after(n4, mix_own, mix_other)
    hid_b, kept_b = ffn_forward(n4, ffn_b_in)
    hid_b = after(hid_b, other[6])
    kept_b = kept_b[:3] + (hid_b,)

    def leave(g, x, r, i, d_normed, *order, late=()):
        d_n = links.own_first(after(links.scatter_rows(d_normed, *order), *late))
        d_x, d_gain = norm_backward(x, r, gains[i : i + 1], d_n)
        return g + d_x, d_gain

    g4 = g4_low.astype(f32)
    fh = features // 2
    ffn_b_out = links.by_y(own[6], after(other[6], hid_b))
    b_in, b_out, d_pair = ffn_backward(links, dy4, kept_b, ffn_b_out)
    x4 = x3 + links.scatter_rows(dot(after(hid_b, b_in.product), ffn_b_out))
    block_out = ungroup(x4, nz, 1).astype(bf16).reshape(hidden_in.shape)
    d_n4 = product_nt(d_pair, ffn_b_in)
    g3, gain_d = leave(g4, x3, r4, 3, d_n4, b_out.came)

    dy3 = links.gather_rows(g3.astype(bf16))
    dy3 = after(dy3, b_out.finish(g3))
    a_out = Sent(links, mix_own, mix_other, [dy3], b_in.came)
    d_mix = product_nt([after(dy3, a_out.product)], [attn_out])
    d_qkv = flat(attention_backward(low, pieces(d_mix), tables))
    q_in = Sent(links, n3[:, :fh], n3[:, fh:], [d_qkv], a_out.came)
    seen = after(b_in.came, q_in.product)[:8, :128]
    d_n3 = product_nt([after(d_qkv, q_in.product, seen + seen)], qkv_in)
    done = b_in.finish(b_out.terms[0], d_n3, block_out)
    g2, gain_c = leave(g3, x2, r3, 2, d_n3, done, a_out.came)

    dy2 = links.gather_rows(g2.astype(bf16))
    dy2 = after(dy2, a_out.finish(g2), q_in.came)
    f_in, f_out, d_pair = ffn_backward(
        links, dy2, kept_a, ffn_a_out, q_in.came, finish=q_in
    )
    d_n2 = product_nt(d_pair, ffn_a_in)
    g1, gain_b = leave(g2, x1, r2, 1, d_n2, f_out.came)

    dy1 = links.gather_rows(g1.astype(bf16))
    dy1 = after(dy1, f_out.finish(b_in.terms[0], g1))
    gated = flat(gated)
    m_out = Sent(links, *split_y(links, gated), [dy1], f_in.came)
    d_gated = pieces(product_nt([after(dy1, m_out.product)], [mixer_out]))
    d_dt, d_val, d_z, d_bc, d_rate, sums = scan_backward(
        slots, ext, wdt, values, pre, par, rate, keep, d_gated, scanned, states
    )
    d_dt, d_z = flat(d_dt), flat(d_z)
    d_dt = after(d_dt, f_in.finish(d_z, a_out.terms[0], q_in.terms[0], f_out.terms[0]))
    d_bc = d_bc[:, :, :, 0, :].reshape(PIECES, micro, 2, rows, STATE)
    d_bc = jnp.swapaxes(d_bc, 2, 3).reshape(PIECES * local, 2 * STATE)
    d_ext = links.sum_rows(jnp.concatenate([dot_nt(d_dt, wdt), d_bc], axis=1))
    d_x, conv_sums = conv_backward(slots, pieces(d_ext), d_val, pre, masks, par, wx)
    d_x = flat(d_x)
    m_in = Sent(links, n1[:, :fh], n1[:, fh:], [d_x, d_z], m_out.came)
    done = m_out.finish(m_in.product)
    d_n1 = product_nt([after(d_x, m_in.product, done), d_z], mixer_in)

    g0, gain_a = leave(g1, x0, r1, 0, d_n1, late=(m_in.came,))

    grad_dt = dot_tn(d_dt, flat(ext)[:, :RANK])
    grad_x = dot_tn(flat(values), d_ext)
    grad_table = jnp.concatenate([conv_sums[: CONV + 1], sums[:2], d_rate * rate], axis=0)
    packed = jnp.concatenate([grad_x, grad_dt, grad_table.T], axis=1)
    grad_gains = jnp.stack([gain_a, gain_b, gain_c, gain_d])
    grad_gains = jnp.moveaxis(grad_gains.reshape(4, 2, nz, -1), 0, 2)
    packed = jnp.concatenate(
        [after(packed, d_n1).reshape(2, nz, -1, packed.shape[1]), grad_gains.reshape(2, nz, width // dp, -1)],
        axis=3,
    )
    done = m_in.finish(g0, *f_in.terms)
    summed = links.scatter_small(after(packed, done))
    states = w_xproj.shape[1]
    tail = states + RANK + mixer_params.shape[0]
    grads = [
        summed[:, :states],
        summed[:, states : states + RANK].T,
        summed[:, states + RANK : tail].T,
    ]
    input_grad = ungroup(after(g0, done), nz, 1).astype(bf16).reshape(hidden_in.shape)
    gain_total = summed[:, tail:].reshape(norm_gains.shape)
    gain_total = gain_total + links.swap_core(gain_total)
    gain_total = gain_total + links.swap_x(gain_total)

    def grad_of(sent, like):
        return spread(sent.land(done), nz, like.shape)

    outs = [
        grad_of(m_out, w_mixer_out),
        grad_of(f_in, w_ffn_a_in),
        grad_of(f_out, w_ffn_a_out),
        q_in.land(done)[0].astype(f32).reshape(w_qkv.shape),
        grad_of(a_out, w_attn_out),
        grad_of(b_in, w_ffn_b_in),
        grad_of(b_out, w_ffn_b_out),
    ]
    grad_in = grad_of(m_in, w_mixer_in)
    return (block_out, input_grad, gain_total, grad_in, *grads, *outs)


def solution(mesh):
    def body(*args):
        return per_device(mesh, *args)

    rows = P(None, ("dp", "tensor"), None)
    weight_in = P("dp", None, "tensor")
    weight_out = P(("tensor", "dp"), None)
    columns = P(None, ("tensor", "dp"))
    gains = P(None, "dp")
    weights = (
        gains, weight_in, weight_out, columns, columns, weight_out, weight_in, weight_out,
        weight_in, weight_out, weight_in, weight_out,
    )
    return jax.shard_map(
        body,
        mesh=mesh,
        in_specs=(rows, rows, P(None, "dp")) + weights,
        out_specs=(rows, rows) + weights,
        check_vma=False,
    )
```

```python
import math

import jax
import jax.numpy as jnp
from jax import lax
from jax.experimental import pallas as pl
from jax.experimental.pallas import tpu as pltpu
from jax.sharding import PartitionSpec as P

STATE = 16
CONV = 4
RANK = 96
HEAD = 128
MICRO = 2
PIECES = 4
ORDER = (0, 2, 1, 3)

f32 = jnp.float32
bf16 = jnp.bfloat16
epsilon = 1e-05
floor_score = -1e30


def dot(a, b, dims=((1,), (0,)), out=f32):
    return lax.dot_general(a, b, (dims, ((), ())), preferred_element_type=out)


def dot_tn(a, b, out=f32):
    return dot(a, b, ((0,), (0,)), out)


def dot_nt(a, b, out=f32):
    return dot(a, b, ((1,), (1,)), out)


def sigmoid(v):
    return 1.0 / (1.0 + jnp.exp(-v))


def dsilu(v):
    s = jax.nn.sigmoid(v)
    return s * (1.0 + v * (1.0 - s))


def soft_plus(v):
    return jnp.maximum(v, 0.0) + jnp.log1p(jnp.exp(-jnp.abs(v)))


def conv_fwd_kernel(slot, x_ref, mask_ref, par_ref, wx_ref, val_ref, ext_ref, prev):
    @pl.when((pl.program_id(0) == 0) & (pl.program_id(1) == 0))
    def _():
        prev[...] = jnp.zeros_like(prev)

    x = x_ref[0, 0]
    rows = x.shape[0]
    xe = jnp.concatenate([prev[...], x], axis=0)
    mask = mask_ref[0, 0]
    conv = jnp.broadcast_to(par_ref[4:5, :], x.shape)
    for k in range(CONV):
        conv = conv + par_ref[k : k + 1, :] * xe[8 - k : 8 - k + rows] * mask[:, k : k + 1]
    prev[...] = x[rows - 8 :]
    val = (conv * sigmoid(conv)).astype(bf16)
    val_ref[0, 0] = val
    ext_ref[0, 0] = dot(val, wx_ref[...]).astype(bf16)


def conv_bwd_kernel(
    slot, dext_ref, dval_ref, x_ref, xp_ref, mask_ref, par_ref, wx_ref, dx_ref, sum_ref, after
):
    @pl.when((pl.program_id(0) == 0) & (pl.program_id(1) == 0))
    def _():
        after[...] = jnp.zeros_like(after)
        sum_ref[...] = jnp.zeros_like(sum_ref)

    x = x_ref[0, 0]
    rows = x.shape[0]
    xe = jnp.concatenate([xp_ref[0, 0], x], axis=0)
    mask = mask_ref[0, 0]
    conv = jnp.broadcast_to(par_ref[4:5, :], x.shape)
    for k in range(CONV):
        conv = conv + par_ref[k : k + 1, :] * xe[8 - k : 8 - k + rows] * mask[:, k : k + 1]
    sig = sigmoid(conv)
    d_conv = (dval_ref[0, 0] + dot_nt(dext_ref[0, 0], wx_ref[...])) * (
        sig * (1.0 + conv * (1.0 - sig))
    )
    d_x = jnp.zeros_like(x)
    sums = []
    for k in range(CONV):
        held = d_conv * mask[:, k : k + 1]
        sums.append(jnp.sum(held * xe[8 - k : 8 - k + rows], axis=0, keepdims=True))
        if k == 0:
            d_x = d_x + par_ref[0:1, :] * held
        else:
            he = jnp.concatenate([held, after[k - 1]], axis=0)
            d_x = d_x + par_ref[k : k + 1, :] * he[k : k + rows]
            after[k - 1] = held[:8]
    sums.append(jnp.sum(d_conv, axis=0, keepdims=True))
    for k in range(CONV + 1):
        sum_ref[k : k + 1, :] += sums[k]
    dx_ref[0, 0] = d_x.astype(bf16)


def coefficient_rows(ext):
    both = jnp.concatenate([ext, ext], axis=0)
    return both.T[RANK:]


def scan_fwd_kernel(
    slot, ext_ref, wdt_ref, val_ref, z_ref, par_ref, rate_ref, keep_ref,
    gated_ref, scan_ref, h_ref, state, se, sv, sc,
):
    @pl.when((pl.program_id(0) == 0) & (pl.program_id(1) == 0))
    def _():
        state[...] = jnp.zeros_like(state)

    ext_low = ext_ref[0, 0]
    step = soft_plus(dot(ext_low[:, :RANK], wdt_ref[...]) + par_ref[5:6, :])
    val = val_ref[0, 0].astype(f32)
    se[...] = jnp.where(keep_ref[0, 0] > 0.0, step, 1e30)
    sv[...] = step * val
    rate = rate_ref[...]
    coef = coefficient_rows(ext_low.astype(f32))
    shape = rate.shape

    def body(g, h):
        base = pl.multiple_of(8 * g, 8)
        turned = pltpu.roll(coef, (128 - base) % 128, 1)
        se_t = se[pl.ds(base, 8), :]
        sv_t = sv[pl.ds(base, 8), :]
        for j in range(8):
            a = jnp.exp(jnp.broadcast_to(se_t[j : j + 1], shape) * rate)
            h = a * h + jnp.broadcast_to(sv_t[j : j + 1], shape) * turned[:STATE, j : j + 1]
            h_ref[0, base + j] = h.astype(bf16)
            sc[pl.ds(base + j, 1), :] = jnp.sum(
                h * turned[STATE:, j : j + 1], axis=0, keepdims=True
            )
        return h

    state[...] = lax.fori_loop(0, se.shape[0] // 8, body, state[...])
    scanned = sc[...]
    z = z_ref[0, 0]
    scan_ref[0, 0] = scanned
    gated_ref[0, 0] = ((scanned + par_ref[6:7, :] * val) * (z * sigmoid(z))).astype(bf16)


def scan_bwd_kernel(
    slot, ext_ref, wdt_ref, val_ref, z_ref, par_ref, rate_ref, keep_ref, dg_ref, scan_ref,
    h_ref, hp_ref, ddt_ref, dval_ref, dz_ref, dbc_ref, drate_ref, sum_ref,
    carry, se, st, sv, ds, r1, r2, pb, pc,
):
    @pl.when((pl.program_id(0) == 0) & (pl.program_id(1) == 0))
    def _():
        carry[...] = jnp.zeros_like(carry)
        drate_ref[...] = jnp.zeros_like(drate_ref)
        sum_ref[...] = jnp.zeros_like(sum_ref)

    ext_low = ext_ref[0, 0]
    pre = dot(ext_low[:, :RANK], wdt_ref[...]) + par_ref[5:6, :]
    step = soft_plus(pre)
    val = val_ref[0, 0].astype(f32)
    z = z_ref[0, 0]
    sig_z = sigmoid(z)
    d_gated = dg_ref[0, 0].astype(f32)
    skip = par_ref[6:7, :]
    d_scan = d_gated * (z * sig_z)
    dz_ref[0, 0] = (
        d_gated * (scan_ref[0, 0] + skip * val) * (sig_z * (1.0 + z * (1.0 - sig_z)))
    ).astype(bf16)
    se[...] = jnp.where(keep_ref[0, 0] > 0.0, step, 1e30)
    st[...] = step
    sv[...] = step * val
    ds[...] = d_scan
    rate = rate_ref[...]
    shape = rate.shape
    coef = coefficient_rows(ext_low.astype(f32))
    count = se.shape[0] // 8
    lanes = shape[1] // 128

    def fold(v):
        total = v[:, :128]
        for i in range(1, lanes):
            total = total + v[:, 128 * i : 128 * (i + 1)]
        return total

    def body(i, held):
        back, d_rate = held
        base = pl.multiple_of(8 * (count - 1 - i), 8)
        turned = pltpu.roll(coef, (128 - base) % 128, 1)
        se_t = se[pl.ds(base, 8), :]
        st_t = st[pl.ds(base, 8), :]
        sv_t = sv[pl.ds(base, 8), :]
        ds_t = ds[pl.ds(base, 8), :]
        for j in range(7, -1, -1):
            row = base + j
            h_now = h_ref[0, row].astype(f32)
            if j > 0:
                h_before = h_ref[0, row - 1].astype(f32)
            else:
                h_before = jnp.where(
                    base == 0,
                    hp_ref[0, 0].astype(f32),
                    h_ref[0, jnp.maximum(row - 1, 0)].astype(f32),
                )
            a = jnp.exp(jnp.broadcast_to(se_t[j : j + 1], shape) * rate)
            d_row = jnp.broadcast_to(ds_t[j : j + 1], shape)
            lam = d_row * turned[STATE:, j : j + 1] + back
            back = a * lam
            w = back * h_before
            d_rate = d_rate + w * jnp.broadcast_to(st_t[j : j + 1], shape)
            r1[pl.ds(row, 1), :] = jnp.sum(w * rate, axis=0, keepdims=True)
            r2[pl.ds(row, 1), :] = jnp.sum(lam * turned[:STATE, j : j + 1], axis=0, keepdims=True)
            at = pl.ds(pl.multiple_of(row * STATE, STATE), STATE)
            pb[at, :] = fold(lam * jnp.broadcast_to(sv_t[j : j + 1], shape)).astype(bf16)
            pc[at, :] = fold(d_row * h_now).astype(bf16)
        return back, d_rate

    back, d_rate = lax.fori_loop(0, count, body, (carry[...], jnp.zeros(shape, f32)))
    carry[...] = back
    drate_ref[...] += d_rate
    ones = jnp.ones((8, 128), bf16)
    dbc_ref[0, 0, 0] = dot_nt(ones, pb[...])
    dbc_ref[0, 0, 1] = dot_nt(ones, pc[...])
    d_step = r1[...] + val * r2[...]
    d_dt = d_step * sigmoid(pre)
    dval_ref[0, 0] = step * r2[...] + skip * d_scan
    ddt_ref[0, 0] = d_dt.astype(bf16)
    sum_ref[0:1, :] += jnp.sum(d_dt, axis=0, keepdims=True)
    sum_ref[1:2, :] += jnp.sum(d_scan * val, axis=0, keepdims=True)


def turn(v, cos, sin):
    return v * cos + pltpu.roll(v, HEAD // 2, 1) * sin


def attention_parts(seg_c, seg_r, pos_c, pos_r):
    return (seg_c == seg_r) & (pos_r <= pos_c)


def attn_fwd_kernel(qkv_ref, cos_ref, sin_ref, segc, segr, posc, posr, mix_ref, low_ref):
    heads = qkv_ref.shape[3] // (3 * HEAD)
    length = PIECES * qkv_ref.shape[2]
    cos = cos_ref[...].reshape(length, HEAD)
    sin = sin_ref[...].reshape(length, HEAD)
    allowed = attention_parts(segc[...].reshape(length, 1), segr[0], posc[...], posr[...])

    def take(i):
        return qkv_ref[:, 0, :, i * HEAD : (i + 1) * HEAD].reshape(length, HEAD)

    def put(ref, i, v):
        ref[:, 0, :, i * HEAD : (i + 1) * HEAD] = v.reshape(PIECES, -1, HEAD)

    for h in range(heads):
        q = turn(take(h), cos, sin).astype(bf16)
        k = turn(take(heads + h), cos, sin).astype(bf16)
        v = take(2 * heads + h).astype(bf16)
        scores = jnp.where(allowed, dot_nt(q, k) * HEAD ** (-0.5), floor_score)
        e = jnp.exp(scores - jnp.max(scores, axis=1, keepdims=True))
        probs = (e / jnp.sum(e, axis=1, keepdims=True)).astype(bf16)
        put(mix_ref, h, dot(probs, v).astype(bf16))
        put(low_ref, h, q)
        put(low_ref, heads + h, k)
        put(low_ref, 2 * heads + h, v)


def attn_bwd_kernel(low_ref, dmix_ref, cos_ref, sin_ref, segc, segr, posc, posr, dqkv_ref):
    heads = low_ref.shape[3] // (3 * HEAD)
    length = PIECES * low_ref.shape[2]
    cos = cos_ref[...].reshape(length, HEAD)
    sin = -sin_ref[...].reshape(length, HEAD)
    allowed = attention_parts(segc[...].reshape(length, 1), segr[0], posc[...], posr[...])
    scale = HEAD ** (-0.5)

    def take(ref, i):
        return ref[:, 0, :, i * HEAD : (i + 1) * HEAD].reshape(length, HEAD)

    def put(i, v):
        dqkv_ref[:, 0, :, i * HEAD : (i + 1) * HEAD] = v.astype(bf16).reshape(PIECES, -1, HEAD)

    for h in range(heads):
        q, k, v = take(low_ref, h), take(low_ref, heads + h), take(low_ref, 2 * heads + h)
        d_mix = take(dmix_ref, h)
        scores = jnp.where(allowed, dot_nt(q, k) * scale, floor_score)
        e = jnp.exp(scores - jnp.max(scores, axis=1, keepdims=True))
        probs = e / jnp.sum(e, axis=1, keepdims=True)
        d_probs = dot_nt(d_mix, v)
        d_scores = (
            probs * (d_probs - jnp.sum(probs * d_probs, axis=1, keepdims=True))
        ).astype(bf16)
        put(h, turn(dot(d_scores, k) * scale, cos, sin))
        put(heads + h, turn(dot_tn(d_scores, q) * scale, cos, sin))
        put(2 * heads + h, dot_tn(probs.astype(bf16), d_mix))


BIG = 48 * 1024 * 1024
BRIEF = pl.CostEstimate(flops=1, bytes_accessed=1, transcendentals=0)


def params(dims):
    return pltpu.CompilerParams(
        dimension_semantics=("arbitrary",) * dims, vmem_limit_bytes=BIG
    )


def rel(rows, cols, col=0):
    return pl.BlockSpec((1, 1, rows, cols), lambda m, j, s: (s[j], m, 0, col))


def rel_back(rows, cols, col=0):
    return pl.BlockSpec((1, 1, rows, cols), lambda m, j, s: (s[PIECES - 1 - j], m, 0, col))


def ordered(rows, cols):
    return pl.BlockSpec((1, 1, rows, cols), lambda m, j, s: (m, j, 0, 0))


def ordered_back(rows, cols):
    return pl.BlockSpec((1, 1, rows, cols), lambda m, j, s: (m, PIECES - 1 - j, 0, 0))


def fixed(*shape):
    return pl.BlockSpec(shape, lambda m, j, s: (0,) * len(shape))


def conv_forward(slots, pre, masks, par, wx):
    rows, width = pre.shape[2], pre.shape[3] // 2
    grid = pltpu.PrefetchScalarGridSpec(
        num_scalar_prefetch=1,
        grid=(MICRO, PIECES),
        in_specs=[rel(rows, width), ordered(rows, CONV), fixed(8, width), fixed(*wx.shape)],
        out_specs=[rel(rows, width), rel(rows, wx.shape[1])],
        scratch_shapes=[pltpu.VMEM((8, width), f32)],
    )
    return pl.pallas_call(
        conv_fwd_kernel,
        grid_spec=grid,
        out_shape=[
            jax.ShapeDtypeStruct((PIECES, MICRO, rows, width), bf16),
            jax.ShapeDtypeStruct((PIECES, MICRO, rows, wx.shape[1]), bf16),
        ],
        compiler_params=params(2),
        cost_estimate=BRIEF,
        name="conv_forward",
    )(slots, pre, masks, par, wx)


def conv_backward(slots, d_ext, d_val, pre, masks, par, wx):
    rows, width = pre.shape[2], pre.shape[3] // 2
    last = rows // 8 - 1
    grid = pltpu.PrefetchScalarGridSpec(
        num_scalar_prefetch=1,
        grid=(MICRO, PIECES),
        in_specs=[
            rel_back(rows, wx.shape[1]),
            rel_back(rows, width),
            rel_back(rows, width),
            pl.BlockSpec(
                (1, 1, 8, width),
                lambda m, j, s: (s[jnp.maximum(PIECES - 2 - j, 0)], m, last, 0),
            ),
            ordered_back(rows, CONV),
            fixed(8, width),
            fixed(*wx.shape),
        ],
        out_specs=[rel_back(rows, width), fixed(8, width)],
        scratch_shapes=[pltpu.VMEM((CONV - 1, 8, width), f32)],
    )
    return pl.pallas_call(
        conv_bwd_kernel,
        grid_spec=grid,
        out_shape=[
            jax.ShapeDtypeStruct((PIECES, MICRO, rows, width), bf16),
            jax.ShapeDtypeStruct((8, width), f32),
        ],
        compiler_params=params(2),
        cost_estimate=BRIEF,
        name="conv_backward",
    )(slots, d_ext, d_val, pre, pre, masks, par, wx)


def scan_forward(slots, ext, wdt, val, pre, par, rate, keep):
    rows, width = val.shape[2], val.shape[3]
    grid = pltpu.PrefetchScalarGridSpec(
        num_scalar_prefetch=1,
        grid=(MICRO, PIECES),
        in_specs=[
            rel(rows, ext.shape[3]), fixed(*wdt.shape), rel(rows, width), rel(rows, width, 1),
            fixed(8, width), fixed(STATE, width), ordered(rows, 1),
        ],
        out_specs=[
            rel(rows, width), rel(rows, width),
            pl.BlockSpec((1, rows, STATE, width), lambda m, j, s: (m * PIECES + j, 0, 0, 0)),
        ],
        scratch_shapes=[pltpu.VMEM((STATE, width), f32)] + [pltpu.VMEM((rows, width), f32)] * 3,
    )
    return pl.pallas_call(
        scan_fwd_kernel,
        grid_spec=grid,
        out_shape=[
            jax.ShapeDtypeStruct((PIECES, MICRO, rows, width), bf16),
            jax.ShapeDtypeStruct((PIECES, MICRO, rows, width), f32),
            jax.ShapeDtypeStruct((MICRO * PIECES, rows, STATE, width), bf16),
        ],
        compiler_params=params(2),
        cost_estimate=BRIEF,
        name="scan_forward",
    )(slots, ext, wdt, val, pre, par, rate, keep)


def scan_backward(slots, ext, wdt, val, pre, par, rate, keep, d_gated, scanned, states):
    rows, width = val.shape[2], val.shape[3]
    grid = pltpu.PrefetchScalarGridSpec(
        num_scalar_prefetch=1,
        grid=(MICRO, PIECES),
        in_specs=[
            rel_back(rows, ext.shape[3]), fixed(*wdt.shape), rel_back(rows, width),
            rel_back(rows, width, 1), fixed(8, width), fixed(STATE, width), ordered_back(rows, 1),
            rel_back(rows, width), rel_back(rows, width),
            pl.BlockSpec(
                (1, rows, STATE, width),
                lambda m, j, s: (m * PIECES + PIECES - 1 - j, 0, 0, 0),
            ),
            pl.BlockSpec(
                (1, 1, STATE, width),
                lambda m, j, s: (
                    jnp.maximum(m * PIECES + PIECES - 2 - j, 0), rows - 1, 0, 0,
                ),
            ),
        ],
        out_specs=[
            rel_back(rows, width), rel_back(rows, width), rel_back(rows, width),
            pl.BlockSpec(
                (1, 1, 2, 8, rows * STATE),
                lambda m, j, s: (s[PIECES - 1 - j], m, 0, 0, 0),
            ),
            fixed(STATE, width), fixed(8, width),
        ],
        scratch_shapes=[pltpu.VMEM((STATE, width), f32)]
        + [pltpu.VMEM((rows, width), f32)] * 6
        + [pltpu.VMEM((rows * STATE, 128), bf16)] * 2,
    )
    return pl.pallas_call(
        scan_bwd_kernel,
        grid_spec=grid,
        out_shape=[
            jax.ShapeDtypeStruct((PIECES, MICRO, rows, width), bf16),
            jax.ShapeDtypeStruct((PIECES, MICRO, rows, width), f32),
            jax.ShapeDtypeStruct((PIECES, MICRO, rows, width), bf16),
            jax.ShapeDtypeStruct((PIECES, MICRO, 2, 8, rows * STATE), f32),
            jax.ShapeDtypeStruct((STATE, width), f32),
            jax.ShapeDtypeStruct((8, width), f32),
        ],
        compiler_params=params(2),
        cost_estimate=BRIEF,
        name="scan_backward",
    )(slots, ext, wdt, val, pre, par, rate, keep, d_gated, scanned, states, states)


def attention_specs(rows, length):
    return [
        pl.BlockSpec((PIECES, rows, HEAD), lambda m: (0, 0, 0)),
        pl.BlockSpec((PIECES, rows, HEAD), lambda m: (0, 0, 0)),
        pl.BlockSpec((PIECES, 1, rows, 1), lambda m: (0, m, 0, 0)),
        pl.BlockSpec((1, 1, length), lambda m: (m, 0, 0)),
        pl.BlockSpec((length, 1), lambda m: (0, 0)),
        pl.BlockSpec((1, length), lambda m: (0, 0)),
    ]


def attention_forward(qkv, tables):
    rows, width = qkv.shape[2], qkv.shape[3]

    def whole(cols):
        return pl.BlockSpec((PIECES, 1, rows, cols), lambda m: (0, m, 0, 0))

    return pl.pallas_call(
        attn_fwd_kernel,
        grid=(MICRO,),
        in_specs=[whole(width)] + attention_specs(rows, PIECES * rows),
        out_specs=[whole(width // 3), whole(width)],
        out_shape=[
            jax.ShapeDtypeStruct((PIECES, MICRO, rows, width // 3), bf16),
            jax.ShapeDtypeStruct((PIECES, MICRO, rows, width), bf16),
        ],
        compiler_params=params(1),
        cost_estimate=BRIEF,
        name="attention_forward",
    )(qkv, *tables)


def attention_backward(low, d_mix, tables):
    rows, width = low.shape[2], low.shape[3]

    def whole(cols):
        return pl.BlockSpec((PIECES, 1, rows, cols), lambda m: (0, m, 0, 0))

    return pl.pallas_call(
        attn_bwd_kernel,
        grid=(MICRO,),
        in_specs=[whole(width), whole(width // 3)] + attention_specs(rows, PIECES * rows),
        out_specs=whole(width),
        out_shape=jax.ShapeDtypeStruct((PIECES, MICRO, rows, width), bf16),
        compiler_params=params(1),
        cost_estimate=BRIEF,
        name="attention_backward",
    )(low, d_mix, *tables)


def tile_of(n):
    return 256 if n % 256 == 0 else n


def tn_kernel(count, added, *refs):
    left, rights, adds, out = refs[0], refs[1 : 1 + count], refs[1 + count : -1], refs[-1]
    col = 0
    for i in range(count):
        width = rights[i].shape[1]
        part = dot_tn(left[...], rights[i][...])
        if added:
            part = part + adds[0][:, col : col + width].astype(f32)
        out[:, col : col + width] = part.astype(bf16)
        col += width


def product_tn(left, rights, adds=()):
    rows, m = left.shape
    tile = tile_of(m)
    width = sum(v.shape[1] for v in rights)
    whole = [pl.BlockSpec(v.shape, lambda i: (0, 0)) for v in rights]
    return pl.pallas_call(
        lambda *refs: tn_kernel(len(rights), bool(adds), *refs),
        grid=(m // tile,),
        in_specs=[pl.BlockSpec((rows, tile), lambda i: (0, i))]
        + whole
        + [pl.BlockSpec((tile, v.shape[1]), lambda i: (i, 0)) for v in adds],
        out_specs=pl.BlockSpec((tile, width), lambda i: (i, 0)),
        out_shape=jax.ShapeDtypeStruct((m, width), bf16),
        compiler_params=params(1),
        cost_estimate=BRIEF,
        name="product_tn",
    )(left, *rights, *adds)


def nt_kernel(count, steps, *refs):
    ds, ws, out = refs[:count], refs[count:-1], refs[-1]

    def part(w):
        total, col = None, 0
        for d in ds:
            width = d.shape[1]
            term = dot_nt(d[...], w[:, col : col + width])
            total = term if total is None else total + term
            col += width
        out[...] = total.astype(bf16)

    if len(ws) == 1:
        part(ws[0])
    else:
        pl.when(pl.program_id(0) < steps)(lambda: part(ws[0]))
        pl.when(pl.program_id(0) >= steps)(lambda: part(ws[1]))


def product_nt(ds, ws):
    rows = ds[0].shape[0]
    m, width = ws[0].shape
    tile = tile_of(m)
    steps = m // tile
    maps = [lambda i: (jnp.minimum(i, steps - 1), 0), lambda i: (jnp.maximum(i - steps, 0), 0)]
    return pl.pallas_call(
        lambda *refs: nt_kernel(len(ds), steps, *refs),
        grid=(steps * len(ws),),
        in_specs=[pl.BlockSpec(v.shape, lambda i: (0, 0)) for v in ds]
        + [pl.BlockSpec((tile, width), maps[j]) for j in range(len(ws))],
        out_specs=pl.BlockSpec((rows, tile), lambda i: (0, i)),
        out_shape=jax.ShapeDtypeStruct((rows, m * len(ws)), bf16),
        compiler_params=params(1),
        cost_estimate=BRIEF,
        name="product_nt",
    )(*ds, *ws)


def gate_bwd_kernel(dy, w, gate, up, d_gate, d_up):
    d_hid = dot_nt(dy[...], w[...])
    g = gate[...].astype(f32)
    sig = sigmoid(g)
    d_gate[...] = (d_hid * up[...].astype(f32) * (sig * (1.0 + g * (1.0 - sig)))).astype(bf16)
    d_up[...] = (d_hid * (g * sig)).astype(bf16)


def gate_backward(dy, w, gate, up):
    rows, units = gate.shape
    tile = tile_of(units)
    column = pl.BlockSpec((rows, tile), lambda i: (0, i))
    return pl.pallas_call(
        gate_bwd_kernel,
        grid=(units // tile,),
        in_specs=[
            pl.BlockSpec(dy.shape, lambda i: (0, 0)),
            pl.BlockSpec((tile, w.shape[1]), lambda i: (i, 0)),
            column,
            column,
        ],
        out_specs=[column, column],
        out_shape=[jax.ShapeDtypeStruct((rows, units), bf16)] * 2,
        compiler_params=params(1),
        cost_estimate=BRIEF,
        name="gate_backward",
    )(dy, w, gate, up)


def spread_kernel(nz, count, *refs):
    terms, out = refs[:-1], refs[-1]
    total = sum(v[...].astype(f32) for v in terms)
    cols = total.shape[1] // count
    u = cols // (2 * nz)
    for i in range(count):
        blocks = []
        for z in range(nz):
            for y in range(2):
                at = i * cols + (y * nz + z) * u
                blocks.append(total[:, at : at + u])
        if count == 1:
            out[...] = jnp.concatenate(blocks, axis=1)
        elif u % 128 != 0:
            out[:, i, :] = jnp.concatenate(blocks, axis=1)
        else:
            for j, block in enumerate(blocks):
                out[:, i, j * u : (j + 1) * u] = block


def spread(terms, nz, shape):
    rows, cols = terms[0].shape
    count = shape[1] if len(shape) == 3 else 1
    tile = rows // 2 if rows % 32 == 0 else rows
    block = (tile, cols) if count == 1 else (tile, count, cols // count)
    return pl.pallas_call(
        lambda *refs: spread_kernel(nz, count, *refs),
        grid=(rows // tile,),
        in_specs=[pl.BlockSpec((tile, cols), lambda i: (i, 0))] * len(terms),
        out_specs=pl.BlockSpec(block, lambda i: (i,) + (0,) * (len(block) - 1)),
        out_shape=jax.ShapeDtypeStruct(shape, f32),
        compiler_params=params(1),
        cost_estimate=BRIEF,
        name="spread",
    )(*terms)


def gate_fwd_kernel(n, own_g, own_u, other_g, other_u, gate, up, hid):
    half = n.shape[1] // 2
    g = dot(n[:, :half], own_g[...]) + dot(n[:, half:], other_g[...])
    u = dot(n[:, :half], own_u[...]) + dot(n[:, half:], other_u[...])
    gate[...] = g.astype(bf16)
    up[...] = u.astype(bf16)
    hid[...] = (g * sigmoid(g) * u).astype(bf16)


def gate_forward(n, own, other):
    rows, features = n.shape
    units = own.shape[1] // 2
    tile = tile_of(units)
    steps = units // tile
    column = pl.BlockSpec((rows, tile), lambda i: (0, i))
    w_gate = pl.BlockSpec((own.shape[0], tile), lambda i: (0, i))
    w_up = pl.BlockSpec((own.shape[0], tile), lambda i: (0, i + steps))
    return pl.pallas_call(
        gate_fwd_kernel,
        grid=(steps,),
        in_specs=[pl.BlockSpec((rows, features), lambda i: (0, 0)), w_gate, w_up, w_gate, w_up],
        out_specs=[column] * 3,
        out_shape=[jax.ShapeDtypeStruct((rows, units), bf16)] * 3,
        compiler_params=params(1),
        cost_estimate=BRIEF,
        name="gate_forward",
    )(n, own, own, other, other)


class Links:
    def __init__(self, mesh):
        self.dp = mesh.shape["dp"]
        self.nz = self.dp // 2
        self.y = lax.axis_index("dp") % 2
        self.z = lax.axis_index("dp") // 2
        self.t = lax.axis_index("tensor")
        self.groups = [[2 * z + y for z in range(self.nz)] for y in range(2)]

    def swap_y(self, v):
        return lax.ppermute(v, "dp", [(i, i ^ 1) for i in range(self.dp)])

    def shift_z(self, v, k):
        n = self.nz
        return lax.ppermute(
            v, "dp", [(2 * z + y, 2 * ((z + k) % n) + y) for z in range(n) for y in range(2)]
        )

    def swap_core(self, v):
        return lax.ppermute(v, "tensor", [(i, i ^ 1) for i in range(PIECES)])

    def swap_x(self, v):
        return lax.ppermute(v, "tensor", [(i, i ^ 2) for i in range(PIECES)])

    def gather_z(self, v):
        return lax.all_gather(v, "dp", axis=0, tiled=True, axis_index_groups=self.groups)

    def scatter_z(self, v):
        return lax.psum_scatter(
            v, "dp", scatter_dimension=0, tiled=True, axis_index_groups=self.groups
        )

    def gather_small(self, v):
        if self.dp > 8:
            both = self.by_y(v[None], self.swap_y(v)[None])
            return jnp.swapaxes(self.gather_z(both[None]), 0, 1)
        n = self.dp
        came = [v] + [
            lax.ppermute(v, "dp", [(i, (i + k) % n) for i in range(n)]) for k in range(1, n)
        ]
        ring = jnp.stack(came[:0:-1] + came[:1] + came[:0:-1])
        window = lax.dynamic_slice_in_dim(ring, n - 1 - lax.axis_index("dp"), n, 0)
        return jnp.swapaxes(window.reshape(self.nz, 2, -1), 0, 1)

    def scatter_small(self, v):
        low = v.astype(bf16)
        if self.nz > 4:
            total = self.scatter_z(jnp.swapaxes(low, 0, 1))[0].astype(f32)
        else:
            total = lax.dynamic_index_in_dim(v, self.z, 1, False)
            for k in range(1, self.nz):
                piece = lax.dynamic_index_in_dim(low, (self.z + k) % self.nz, 1, False)
                total = total + self.shift_z(piece, k).astype(f32)
        other = lax.dynamic_index_in_dim(total.astype(bf16), 1 - self.y, 0, False)
        own = lax.dynamic_index_in_dim(total, self.y, 0, False)
        return own + self.swap_y(other).astype(f32)

    def by_y(self, own, other, axis=0):
        return jnp.where(
            self.y == 0,
            jnp.concatenate([own, other], axis),
            jnp.concatenate([other, own], axis),
        )

    def own_first(self, v):
        half = v.shape[1] // 2
        return jnp.where(
            self.y == 0, v, jnp.concatenate([v[:, half:], v[:, :half]], axis=1)
        )

    def gather_rows(self, v, *order):
        x = self.swap_x(v)
        core = self.swap_core(after(v, *order))
        return jnp.concatenate([v, x, core, self.swap_core(x)], axis=0)

    def scatter_rows(self, part, *order):
        quarter = part.shape[0] // PIECES
        came = self.swap_core(part[2 * quarter :].astype(bf16)).astype(f32)
        x = (part[quarter : 2 * quarter].astype(f32) + came[quarter:]).astype(bf16)
        x = self.swap_x(after(x, *order))
        return part[:quarter].astype(f32) + came[:quarter] + x.astype(f32)

    def sum_rows(self, v):
        low = v.astype(bf16)
        q = low.shape[0] // PIECES
        turned = jnp.concatenate([low[2 * q :], low[: 2 * q]], axis=0)
        low = (low.astype(f32) + self.swap_core(turned).astype(f32)).astype(bf16)
        turned = jnp.concatenate([low[q : 2 * q], low[:q], low[3 * q :], low[2 * q : 3 * q]], axis=0)
        return (low.astype(f32) + self.swap_x(turned).astype(f32)).astype(bf16)

    def gather_z_direct(self, shard):
        if self.nz > 4:
            return self.gather_z(shard)
        came = [shard] + [self.shift_z(shard, k) for k in range(1, self.nz)]
        ring = jnp.concatenate(came[:0:-1] + came[:1] + came[:0:-1], axis=0)
        rows = shard.shape[0]
        return lax.dynamic_slice_in_dim(
            ring, (self.nz - 1 - self.z) * rows, self.nz * rows, 0
        )

    def scatter_z_direct(self, v):
        if self.nz > 4:
            return [self.scatter_z(v)]
        rows = v.shape[0] // self.nz
        terms = [lax.dynamic_slice_in_dim(v, self.z * rows, rows, 0)]
        for k in range(1, self.nz):
            piece = lax.dynamic_slice_in_dim(v, ((self.z + k) % self.nz) * rows, rows, 0)
            terms.append(self.shift_z(piece, k))
        return terms


class Sent:
    def __init__(self, links, left_own, left_other, rights, *order):
        self.links, self.left, self.rights = links, left_own, rights
        self.product = product_tn(left_other, rights)
        self.came = links.swap_y(after(self.product, *order))

    def finish(self, *order, direct=False, last=()):
        self.total = product_tn(self.left, self.rights, [after(self.came, *order)])
        if direct:
            self.terms = self.links.scatter_z_direct(after(self.total, *last))
        else:
            self.terms = [self.links.scatter_z(self.total)]
        return self.total

    def land(self, *order):
        return [after(v, *order) for v in self.terms]


def after(v, *order):
    if not order:
        return v
    return lax.optimization_barrier((v,) + order)[0]


def regroup(v, nz, axis):
    shape = v.shape
    u = shape[axis] // (2 * nz)
    v = v.reshape(shape[:axis] + (nz, 2, u) + shape[axis + 1 :])
    return jnp.swapaxes(v, axis, axis + 1).reshape(shape)


def ungroup(v, nz, axis):
    shape = v.shape
    u = shape[axis] // (2 * nz)
    v = v.reshape(shape[:axis] + (2, nz, u) + shape[axis + 1 :])
    return jnp.swapaxes(v, axis, axis + 1).reshape(shape)


def norm_forward(x, gain):
    r = lax.rsqrt(jnp.mean(x * x, axis=1, keepdims=True) + epsilon)
    return (x * r * gain).astype(bf16), r


def norm_backward(x, r, gain, d_n):
    u = x * r
    g = d_n * gain
    d_x = r * (g - u * jnp.mean(g * u, axis=1, keepdims=True))
    return d_x, jnp.sum(d_n * u, axis=0)


def times(x, own, other):
    half = x.shape[1] // 2
    return dot(x[:, :half], own) + dot(x[:, half:], other)


def back_times(d, own, other):
    return jnp.concatenate([dot_nt(d, own), dot_nt(d, other)], axis=1)


def ffn_forward(n, w_in):
    gate, up, hid = gate_forward(n, *w_in)
    return hid, (n, gate, up, hid)


def split_y(links, v):
    half = v.shape[1] // 2
    own = lax.dynamic_slice_in_dim(v, links.y * half, half, 1)
    other = lax.dynamic_slice_in_dim(v, (1 - links.y) * half, half, 1)
    return own, other


def ffn_backward(links, dy, kept, w_out, *order, finish=None):
    n, gate, up, hid = kept
    hid_own, hid_other = split_y(links, hid)
    sent_out = Sent(links, hid_own, hid_other, [dy], *order)
    dy = after(dy, sent_out.product)
    if finish is not None:
        dy = after(dy, finish.finish(sent_out.product))
    d_pair = gate_backward(dy, w_out, gate, up)
    half = n.shape[1] // 2
    sent_in = Sent(links, n[:, :half], n[:, half:], d_pair, sent_out.came)
    return sent_in, sent_out, [after(d_pair[0], sent_in.product), d_pair[1]]


def per_device(
    mesh,
    hidden_in, out_grad, segment_ids, norm_gains, w_mixer_in, w_xproj, w_dtproj, mixer_params,
    w_mixer_out, w_ffn_a_in, w_ffn_a_out, w_qkv, w_attn_out, w_ffn_b_in, w_ffn_b_out,
):
    links = Links(mesh)
    nz, dp, t = links.nz, links.dp, links.t
    micro, rows, features = hidden_in.shape
    local = micro * rows
    length = PIECES * rows

    small = [norm_gains, w_xproj, w_dtproj, mixer_params]
    gathered = links.gather_small(jnp.concatenate([v.reshape(-1) for v in small]))
    offset = 0
    parts = []
    for v in small:
        parts.append(gathered[:, :, offset : offset + v.size].reshape((2, nz) + v.shape))
        offset += v.size
    gains = jnp.moveaxis(parts[0], 2, 0).reshape(norm_gains.shape[0], features).astype(f32)
    wx = parts[1].reshape(-1, w_xproj.shape[1])
    wdt = jnp.moveaxis(parts[2], 2, 0).reshape(w_dtproj.shape[0], -1)
    table = jnp.moveaxis(parts[3], 2, 0).reshape(mixer_params.shape[0], -1).astype(f32)
    width = table.shape[1]
    par = jnp.concatenate([table[: CONV + 3], jnp.zeros((1, width), f32)], axis=0)
    rate = -jnp.exp(table[CONV + 3 :])

    def in_shard(w, group):
        if group:
            w = regroup(w, nz, 2)
        return w.reshape(w.shape[0], -1)

    shards = [
        in_shard(w_mixer_in, True),
        jnp.concatenate([regroup(w_mixer_out, nz, 1), regroup(w_attn_out, nz, 1)], axis=0),
        in_shard(w_ffn_a_in, True),
        regroup(w_ffn_a_out, nz, 1),
        in_shard(w_qkv, False),
        in_shard(w_ffn_b_in, True),
        regroup(w_ffn_b_out, nz, 1),
    ]
    shards[1:] = lax.optimization_barrier(shards[1:])
    own = [links.gather_z(v) for v in shards]
    other = []
    for v in own:
        other.append(links.swap_y(after(v, *other[-1:])))
    mixer_in, outs, ffn_a_in, ffn_a_out, qkv_in, ffn_b_in, ffn_b_out = zip(own, other)

    def rows_of(v, lo, hi):
        return v.reshape(nz, -1, features)[:, lo:hi].reshape(-1, features)

    cut, end = w_mixer_out.shape[0], w_mixer_out.shape[0] + w_attn_out.shape[0]
    mixer_out = links.by_y(*[rows_of(v, 0, cut) for v in outs])
    attn_out = ungroup(links.by_y(*[rows_of(v, cut, end) for v in outs]), nz, 0)
    ffn_a_out = links.by_y(*ffn_a_out)

    seg = segment_ids.reshape(micro, length)
    masks = []
    for k in range(CONV):
        earlier = jnp.pad(seg, ((0, 0), (k, 0)), constant_values=-1)[:, :length]
        masks.append((earlier == seg).astype(f32))
    masks = jnp.stack(masks, axis=-1).reshape(micro, PIECES, rows, CONV)
    keep = masks[..., 1:2]
    slots = jnp.stack([sum(i * (ORDER[i] == (j ^ t)) for i in range(PIECES)) for j in range(PIECES)])
    slots = slots.astype(jnp.int32)
    seg_pieces = seg.reshape(micro, PIECES, rows)
    seg_rel = jnp.stack(
        [lax.dynamic_index_in_dim(seg_pieces, t ^ k, 1, False) for k in ORDER]
    )
    position = jnp.concatenate([(t ^ k) * rows + lax.iota(jnp.int32, rows) for k in ORDER])
    half = HEAD // 2
    frequency = jnp.exp(lax.iota(f32, half) * (-2.0 * math.log(10000.0) / HEAD))
    angles = position.astype(f32)[:, None] * frequency[None, :]
    cos, sin = jnp.cos(angles), jnp.sin(angles)
    tables = (
        jnp.concatenate([cos, cos], axis=1).reshape(PIECES, rows, HEAD),
        jnp.concatenate([-sin, sin], axis=1).reshape(PIECES, rows, HEAD),
        seg_rel[..., None],
        jnp.swapaxes(seg_rel, 0, 1).reshape(micro, 1, length),
        position[:, None],
        position[None, :],
    )

    def pieces(v):
        return v.reshape(PIECES, micro, rows, v.shape[-1])

    def flat(v):
        return v.reshape(PIECES * local, v.shape[-1])

    def enter(x, i):
        n, r = norm_forward(x, gains[i : i + 1])
        return links.gather_rows(links.own_first(n)), r

    x0 = regroup(after(hidden_in, *shards[1:]).reshape(local, features), nz, 1).astype(f32)
    n1, r1 = enter(x0, 0)
    pre = pieces(times(n1, *mixer_in))
    values, ext_part = conv_forward(slots, pre, masks, par, wx)
    ext = pieces(links.sum_rows(flat(ext_part)))
    gated, scanned, states = scan_forward(slots, ext, wdt, values, pre, par, rate, keep)
    x1 = x0 + links.scatter_rows(dot(flat(gated), mixer_out))

    n2, r2 = enter(x1, 1)
    g4_low = regroup(out_grad.reshape(local, features), nz, 1)
    dy4 = links.gather_rows(g4_low)
    hid_a, kept_a = ffn_forward(after(n2, dy4), ffn_a_in)
    hid_a = after(hid_a, own[4])
    x2 = x1 + links.scatter_rows(dot(hid_a, ffn_a_out), other[4])

    n3, r3 = enter(x2, 2)
    mix, low = attention_forward(pieces(times(n3, *qkv_in)), tables)
    mix = after(flat(mix), other[5])
    mix_own, mix_other = split_y(links, regroup(mix, nz, 1))
    x3 = x2 + links.scatter_rows(dot(mix, attn_out), own[6])

    n4, r4 = enter(x3, 3)
    n4 = after(n4, mix_own, mix_other)
    hid_b, kept_b = ffn_forward(n4, ffn_b_in)
    hid_b = after(hid_b, other[6])
    kept_b = kept_b[:3] + (hid_b,)

    def leave(g, x, r, i, d_normed, *order, late=()):
        d_n = links.own_first(after(links.scatter_rows(d_normed, *order), *late))
        d_x, d_gain = norm_backward(x, r, gains[i : i + 1], d_n)
        return g + d_x, d_gain

    g4 = g4_low.astype(f32)
    fh = features // 2
    ffn_b_out = links.by_y(own[6], after(other[6], hid_b))
    b_in, b_out, d_pair = ffn_backward(links, dy4, kept_b, ffn_b_out)
    x4 = x3 + links.scatter_rows(dot(after(hid_b, b_in.product), ffn_b_out))
    block_out = ungroup(x4, nz, 1).astype(bf16).reshape(hidden_in.shape)
    d_n4 = product_nt(d_pair, ffn_b_in)
    g3, gain_d = leave(g4, x3, r4, 3, d_n4, b_out.came)

    dy3 = links.gather_rows(g3.astype(bf16))
    dy3 = after(dy3, b_out.finish(g3))
    a_out = Sent(links, mix_own, mix_other, [dy3], b_in.came)
    d_mix = product_nt([after(dy3, a_out.product)], [attn_out])
    d_qkv = flat(attention_backward(low, pieces(d_mix), tables))
    q_in = Sent(links, n3[:, :fh], n3[:, fh:], [d_qkv], a_out.came)
    seen = after(b_in.came, q_in.product)[:8, :128]
    d_n3 = product_nt([after(d_qkv, q_in.product, seen + seen)], qkv_in)
    done = b_in.finish(b_out.terms[0], d_n3, block_out)
    g2, gain_c = leave(g3, x2, r3, 2, d_n3, done, a_out.came)

    dy2 = links.gather_rows(g2.astype(bf16), q_in.came)
    dy2 = after(dy2, a_out.finish(g2))
    f_in, f_out, d_pair = ffn_backward(
        links, dy2, kept_a, ffn_a_out, q_in.came, finish=q_in
    )
    d_n2 = product_nt(d_pair, ffn_a_in)
    g1, gain_b = leave(g2, x1, r2, 1, d_n2, f_out.came)

    dy1 = links.gather_rows(g1.astype(bf16))
    dy1 = after(dy1, f_out.finish(b_in.terms[0], g1))
    gated = flat(gated)
    m_out = Sent(links, *split_y(links, gated), [dy1], f_in.came)
    d_gated = pieces(product_nt([after(dy1, m_out.product)], [mixer_out]))
    d_dt, d_val, d_z, d_bc, d_rate, sums = scan_backward(
        slots, ext, wdt, values, pre, par, rate, keep, d_gated, scanned, states
    )
    d_dt, d_z = flat(d_dt), flat(d_z)
    d_dt = after(d_dt, f_in.finish(d_z, a_out.terms[0], q_in.terms[0], f_out.terms[0]))
    d_bc = d_bc[:, :, :, 0, :].reshape(PIECES, micro, 2, rows, STATE)
    d_bc = jnp.swapaxes(d_bc, 2, 3).reshape(PIECES * local, 2 * STATE)
    d_ext = links.sum_rows(jnp.concatenate([dot_nt(d_dt, wdt), d_bc], axis=1))
    d_x, conv_sums = conv_backward(slots, pieces(d_ext), d_val, pre, masks, par, wx)
    d_x = flat(d_x)
    m_in = Sent(links, n1[:, :fh], n1[:, fh:], [d_x, d_z], m_out.came)
    done = m_out.finish(m_in.product)
    d_n1 = product_nt([after(d_x, m_in.product, done), d_z], mixer_in)

    g0, gain_a = leave(g1, x0, r1, 0, d_n1, late=(m_in.came,))

    grad_dt = dot_tn(d_dt, flat(ext)[:, :RANK])
    grad_x = dot_tn(flat(values), d_ext)
    grad_table = jnp.concatenate([conv_sums[: CONV + 1], sums[:2], d_rate * rate], axis=0)
    packed = jnp.concatenate([grad_x, grad_dt, grad_table.T], axis=1)
    grad_gains = jnp.stack([gain_a, gain_b, gain_c, gain_d])
    grad_gains = jnp.moveaxis(grad_gains.reshape(4, 2, nz, -1), 0, 2)
    packed = jnp.concatenate(
        [after(packed, d_n1).reshape(2, nz, -1, packed.shape[1]), grad_gains.reshape(2, nz, width // dp, -1)],
        axis=3,
    )
    done = m_in.finish(g0, *f_in.terms)
    summed = links.scatter_small(after(packed, done))
    states = w_xproj.shape[1]
    tail = states + RANK + mixer_params.shape[0]
    grads = [
        summed[:, :states],
        summed[:, states : states + RANK].T,
        summed[:, states + RANK : tail].T,
    ]
    input_grad = ungroup(after(g0, done), nz, 1).astype(bf16).reshape(hidden_in.shape)
    gain_total = summed[:, tail:].reshape(norm_gains.shape)
    gain_total = gain_total + links.swap_core(gain_total)
    gain_total = gain_total + links.swap_x(gain_total)

    def grad_of(sent, like):
        return spread(sent.land(done), nz, like.shape)

    outs = [
        grad_of(m_out, w_mixer_out),
        grad_of(f_in, w_ffn_a_in),
        grad_of(f_out, w_ffn_a_out),
        q_in.land(done)[0].astype(f32).reshape(w_qkv.shape),
        grad_of(a_out, w_attn_out),
        grad_of(b_in, w_ffn_b_in),
        grad_of(b_out, w_ffn_b_out),
    ]
    grad_in = grad_of(m_in, w_mixer_in)
    return (block_out, input_grad, gain_total, grad_in, *grads, *outs)


def solution(mesh):
    def body(*args):
        return per_device(mesh, *args)

    rows = P(None, ("dp", "tensor"), None)
    weight_in = P("dp", None, "tensor")
    weight_out = P(("tensor", "dp"), None)
    columns = P(None, ("tensor", "dp"))
    gains = P(None, "dp")
    weights = (
        gains, weight_in, weight_out, columns, columns, weight_out, weight_in, weight_out,
        weight_in, weight_out, weight_in, weight_out,
    )
    return jax.shard_map(
        body,
        mesh=mesh,
        in_specs=(rows, rows, P(None, "dp")) + weights,
        out_specs=(rows, rows) + weights,
        check_vma=False,
    )
```
